32 devices in a mesh: dp: 4 (over x, core), cent: 8 (over z, y).
Axes of the slice: x: 2, y: 2, z: 4, core: 2. Of those that a mesh axis runs over, the one named last changes fastest.
Arguments:
- points: bfloat16 [32768, 1024], P(('dp', 'cent')), may hold values from -16 to 16
- point_cluster: int32 [32768], P(('dp', 'cent')), may hold values from 0 to 8191, as said below
- cand_blocks: int32 [256, 8], P(('dp', 'cent')), may hold values from 0 to 15, as said below
- cent1_prev: float32 [8192, 1024], P(('dp', 'cent')), may hold values from -6 to 6
- parent: int32 [8192], P(('dp', 'cent')), may hold values from 0 to 2047, as said below
- cent2_prev: bfloat16 [2048, 1024], P('dp'), may hold values from -6 to 6
Outputs:
- cent1_new: float32 [8192, 1024], P(('dp', 'cent'))
- cent2_new: float32 [2048, 1024], P('dp')
- point_score: float32 [32768], P(('dp', 'cent'))
The draws below stay inside these ranges and needn't reach their ends.
Inputs may be any that keep to these rules, and one draw needn't show every extreme that they name: All points of an aligned block of 128 points share one level-one block (point_cluster // 128); on a device these block numbers never fall; the points of a device at index i of dp name only centroids from i * 8 * 256 to (i + 1) * 8 * 256 - 1; at most 2 point blocks of one device fall to one owner's 256 centroids, and in every draw one owner in each index of dp receives exactly 2 blocks from every device of that index. `parent`: the level-one centroids held at index i of dp name level-two centroids from i * 512 to (i + 1) * 512 - 1. `cand_blocks`: each row lists 8 different level-two blocks.
All inputs are finite; a program needn't handle non-finite values.
Results may differ from the reference program's by a relative error of at most 0.00094.
Values may be sent and summed in bfloat16 or wider, within the bound.
No kernel may reach another device: no remote copies, remote signals or barrier semaphores. Data moves between devices by JAX's collectives and lax.ppermute only.
A program may use at most 128 MiB of HBM per device.

```python
import jax
import jax.numpy as jnp
from jax import lax

D = 1024
BLOCK = 128
PT_DEV = 1024
CAP = 2
C1_DEV = 256
C2_DEV = 512
NCAND = 8
C1 = 8192
N_DP = 4
N_CENT = 8


def shared_table(key):
    level_two = C2_DEV * N_DP
    table_key = jax.random.fold_in(key, 11)
    values = jnp.clip(jax.random.normal(table_key, (level_two, D), jnp.float32), -6.0, 6.0)
    return values


def shared_cands(key):
    block_rows = PT_DEV * N_DP * N_CENT // BLOCK
    upper_blocks = C2_DEV * N_DP // BLOCK
    scores = jax.random.randint(jax.random.fold_in(key, 13), (block_rows, upper_blocks), 0, 4096)
    scores = scores * upper_blocks + jnp.arange(upper_blocks, dtype=jnp.int32)[None, :]
    _, picked = lax.top_k(scores, NCAND)
    return picked.astype(jnp.int32)


def draw_cand_blocks(key, part):
    return shared_cands(key)


def draw_cent2_prev(key, part):
    return shared_table(key).astype(jnp.bfloat16)


def draw_points(key, part):
    total = PT_DEV * N_DP * N_CENT
    table = shared_table(key)
    cands = shared_cands(key)
    key_slot, key_row, key_mix, key_noise = jax.random.split(jax.random.fold_in(key, 17), 4)
    slot = jax.random.randint(key_slot, (total,), 0, NCAND)
    block_of = jnp.arange(total, dtype=jnp.int32) // BLOCK
    chosen_block = cands[block_of, slot]
    row = chosen_block * BLOCK + jax.random.randint(key_row, (total,), 0, BLOCK)
    anchor = table[row]
    mix = jax.random.uniform(key_mix, (total, 1), jnp.float32, 0.0, 0.65)
    noise = jnp.clip(jax.random.normal(key_noise, (total, D), jnp.float32), -6.0, 6.0)
    values = mix * anchor + jnp.sqrt(1.0 - mix * mix) * noise
    return values.astype(jnp.bfloat16)


def draw_point_cluster(key, part):
    device_total = N_DP * N_CENT
    block_total = PT_DEV // BLOCK
    slot_total = N_CENT * CAP
    owned_blocks = C1_DEV // BLOCK
    key_base, key_heat, key_forced, key_local, key_offset = jax.random.split(jax.random.fold_in(key, 71), 5)
    initial_score = jax.random.randint(key_base, (device_total, slot_total), 0, 4096)
    heat_rows = jax.random.randint(key_heat, (N_DP, N_CENT), 0, 4) * 4096
    heat_devices = jnp.repeat(heat_rows, N_CENT, axis=0)
    hotness_positions = jnp.repeat(heat_devices, CAP, axis=1)
    forced_rows = jax.random.randint(key_forced, (N_DP, 1), 0, N_CENT)
    pinned_workers = jnp.repeat(forced_rows, N_CENT, axis=0)
    position_index = jnp.arange(slot_total, dtype=jnp.int32)
    position_holder = position_index // CAP
    extra_reward = jnp.where(position_holder[None, :] == pinned_workers, 1 << 29, 0)
    precedence_rank = (initial_score + hotness_positions) * 4096 + position_index[None, :] + extra_reward
    _, chosen = lax.top_k(precedence_rank, block_total)
    local_block = jax.random.randint(key_local, (device_total, slot_total), 0, owned_blocks)
    chosen_local = jnp.take_along_axis(local_block, chosen, axis=1)
    chosen_owner = chosen // CAP
    composite = (chosen_owner * owned_blocks + chosen_local) * slot_total + chosen
    composite = jnp.sort(composite, axis=1)
    block_number = composite // slot_total
    row_index = jnp.arange(device_total, dtype=jnp.int32) // N_CENT
    first_ids = (row_index[:, None] * N_CENT * owned_blocks + block_number) * BLOCK
    offsets = jax.random.randint(key_offset, (device_total, block_total, BLOCK), 0, BLOCK)
    return (first_ids[:, :, None] + offsets).reshape(-1).astype(jnp.int32)


def draw_parent(key, part):
    level_one = C1_DEV * N_DP * N_CENT
    row_index = jnp.arange(level_one, dtype=jnp.int32) // (N_CENT * C1_DEV)
    offsets = jax.random.randint(jax.random.fold_in(key, 93), (level_one,), 0, C2_DEV)
    return (offsets + row_index * C2_DEV).astype(jnp.int32)


def shard_levels(rng, extent, shards, smallest, high):
    def one(axis_at, shards_of):
        draws = jax.random.uniform(jax.random.fold_in(jax.random.fold_in(rng, 6), axis_at), (shards_of,), jnp.float32, smallest / len(shards), high / len(shards))
        return jnp.repeat(jnp.exp(draws), extent[axis_at] // shards_of).reshape((-1,) + (1,) * (len(extent) - axis_at - 1))

    loudness = one(*shards[0])
    for cut in shards[1:]:
        loudness = loudness * one(*cut)
    return loudness


def gaussian(own_key, shape, scale, bound, cuts=(), kind=jnp.bfloat16):
    result = jax.random.normal(own_key, shape, jnp.float32) * scale
    if len(cuts) > 0:
        result = shard_levels(own_key, shape, cuts, -0.22, 0.18) * result
    return jnp.clip(result, min=-bound, max=bound).astype(kind)


def setup_inputs(seed: int = 0) -> dict:
    arg_keys = jax.random.split(jax.random.key(seed), 7)
    points = draw_points(jax.random.fold_in(arg_keys[6], 71), 0)
    point_cluster = draw_point_cluster(jax.random.fold_in(arg_keys[6], 71), 0)
    cand_blocks = draw_cand_blocks(jax.random.fold_in(arg_keys[6], 71), 0)
    cent1_prev = gaussian(arg_keys[3], (C1, D), 1.0, 6.0, ((0, 32),), jnp.float32)
    parent = draw_parent(jax.random.fold_in(arg_keys[6], 71), 0)
    cent2_prev = draw_cent2_prev(jax.random.fold_in(arg_keys[6], 71), 0)
    return {"points": points, "point_cluster": point_cluster, "cand_blocks": cand_blocks, "cent1_prev": cent1_prev, "parent": parent, "cent2_prev": cent2_prev}


EPSILON = 1e-06
SHARPNESS = 20.0

def rms_norm(values):
    return values * lax.rsqrt(lax.optimization_barrier(jnp.mean(values * values, axis=-1, keepdims=True)) + EPSILON)

def reference(points, point_cluster, cand_blocks, cent1_prev, parent, cent2_prev):
    devices_all = N_DP * N_CENT
    level_one = C1_DEV * devices_all
    level_two = C2_DEV * N_DP
    width = points.shape[1]
    point_groups = points.reshape(devices_all, PT_DEV, width)
    cluster_groups = point_cluster.reshape(devices_all, PT_DEV)

    def accumulate(carry, item):
        level_sums, counts = carry
        group_points, group_ids = item
        level_sums = level_sums + jax.ops.segment_sum(group_points.astype(jnp.float32), group_ids, num_segments=level_one)
        counts = counts + jax.ops.segment_sum(jnp.ones((PT_DEV,), jnp.float32), group_ids, num_segments=level_one)
        return ((level_sums, counts), None)
    start_state = (jnp.zeros((level_one, width), jnp.float32), jnp.zeros((level_one,), jnp.float32))
    (level_sums, counts), _ = lax.scan(accumulate, start_state, (point_groups, cluster_groups))
    average = level_sums / jnp.maximum(counts, 1.0)[:, None]
    cent1_new = rms_norm(average + cent1_prev)
    upper_sums = jax.ops.segment_sum(cent1_new, parent, num_segments=level_two)
    cent2_new = rms_norm(upper_sums)
    table = rms_norm(cent2_prev.astype(jnp.float32)).astype(jnp.bfloat16)
    table_blocks = table.reshape(level_two // BLOCK, BLOCK, width)
    unit_points = rms_norm(points.astype(jnp.float32)).astype(jnp.bfloat16)
    blocks_per = PT_DEV // BLOCK
    unit_groups = unit_points.reshape(devices_all, blocks_per, BLOCK, width)
    cand_groups = cand_blocks.reshape(devices_all, blocks_per, NCAND)

    def score_group(item):
        group_units, group_cands = item
        chosen = table_blocks[group_cands]
        products = jnp.einsum('bpd,bkcd->bpkc', group_units.astype(jnp.float32), chosen.astype(jnp.float32))
        weights = jnp.exp(products * (SHARPNESS / width))
        return jnp.log(lax.optimization_barrier(jnp.sum(weights, axis=(2, 3)))).reshape(PT_DEV)
    point_score = lax.map(score_group, (unit_groups, cand_groups)).reshape(-1)
    return (cent1_new, cent2_new, point_score)
```

```python
import functools

import jax
import jax.numpy as jnp
from jax import lax
from jax.experimental import pallas as pl
from jax.experimental.pallas import tpu as pltpu
from jax.sharding import PartitionSpec as P

BLOCK = 128
EPSILON = 1e-06
SHARPNESS = 20.0
CODE = 32000.0
FLOOR = 1e-30
VMEM_LIMIT = 48 * 1024 * 1024


def rms_norm(values):
    return values * lax.rsqrt(jnp.mean(values * values, axis=-1, keepdims=True) + EPSILON)


def split(values):
    high = values.astype(jnp.bfloat16)
    return high, (values - high.astype(jnp.float32)).astype(jnp.bfloat16)


def dot(a, b):
    return jnp.dot(a, b, preferred_element_type=jnp.float32)


def dot_lanes(a, b):
    return lax.dot_general(a, b, (((1,), (1,)), ((), ())), preferred_element_type=jnp.float32)


def sums_kernel(block_ref, ids_ref, points_ref, prev_ref, prev_scale_ref, high_ref, low_ref, code_ref, stat_ref, acc, count):
    rows, w = acc.shape
    blocks = ids_ref.shape[0]
    acc[...] = jnp.zeros_like(acc)
    count[...] = jnp.zeros_like(count)
    centroid = lax.broadcasted_iota(jnp.int32, (BLOCK, BLOCK), 0)
    ones = jnp.ones((BLOCK, BLOCK), jnp.bfloat16)

    def add(i, carry):
        member = jnp.where(centroid == ids_ref[pl.ds(i, 1), :], 1.0, 0.0).astype(jnp.bfloat16)
        at = pl.ds(pl.multiple_of(block_ref[i] * BLOCK, BLOCK), BLOCK)
        part = dot(member, points_ref[pl.ds(pl.multiple_of(i * BLOCK, BLOCK), BLOCK), :])
        acc[at, :] += part
        count[at, :] += dot(member, ones)
        return carry

    lax.fori_loop(0, blocks, add, 0, unroll=4)
    step = 2 * BLOCK
    unit = jnp.ones((8, w), jnp.bfloat16)
    first = jnp.where(lax.broadcasted_iota(jnp.int32, (8, w), 1) == 0, 1.0, 0.0).astype(jnp.bfloat16)

    def finish(i, carry):
        at = pl.ds(pl.multiple_of(i * step, step), step)
        prev = prev_ref[at, :].astype(jnp.float32) * prev_scale_ref[at, :]
        x = acc[at, :] / jnp.maximum(count[at, :][:, :w], 1.0) + prev
        high, low = split(x)
        high_ref[at, :] = high
        low_ref[at, :] = low
        square_high, square_low = split(x * x)
        stat_ref[0:1, at] = (dot_lanes(unit, square_high) + dot_lanes(unit, square_low))[0:1]
        top = jnp.max(jnp.abs(x), axis=1, keepdims=True) * 1.01
        scale = jnp.maximum(top, FLOOR).astype(jnp.bfloat16)
        stat_ref[1:2, at] = dot_lanes(first, jnp.broadcast_to(scale, (step, w)))[0:1]
        code_ref[at, :] = jnp.round(x * (CODE / scale.astype(jnp.float32))).astype(jnp.int16)
        return carry

    lax.fori_loop(0, rows // step, finish, 0)


def upper_kernel(width, stat_ref, parent_ref, high_ref, low_ref, out_ref):
    squares = jnp.sum(stat_ref[:, 0, :], axis=0, keepdims=True)
    factor = lax.rsqrt(squares / width + EPSILON)
    parent = parent_ref[...]
    step = BLOCK
    at_row = lax.broadcasted_iota(jnp.int32, (step, parent.shape[1]), 0)

    def one(i, carry):
        weight = jnp.where(at_row + i * step == parent, factor, 0.0)
        weight_high, weight_low = split(weight)
        part = dot(weight_high, high_ref[...]) + dot(weight_high, low_ref[...])
        out_ref[pl.ds(pl.multiple_of(i * step, step), step), :] = part + dot(weight_low, high_ref[...])
        return carry

    lax.fori_loop(0, out_ref.shape[0] // step, one, 0)


def join_kernel(parts_ref, out_ref):
    parts, rows, w = parts_ref.shape
    squares = jnp.zeros((rows, 1), jnp.float32)
    for s in range(parts):
        values = parts_ref[s]
        squares += jnp.sum(values * values, axis=1, keepdims=True)
    factor = lax.rsqrt(squares / (parts * w) + EPSILON)
    for s in range(parts):
        out_ref[:, s * w : (s + 1) * w] = parts_ref[s] * factor


def decode_kernel(code_ref, scale_ref, out_ref):
    parts, rows, w = code_ref.shape
    squares = jnp.zeros((rows, 1), jnp.float32)
    for s in range(parts):
        values = code_ref[s].astype(jnp.float32) * scale_ref[:, s : s + 1]
        squares += jnp.sum(values * values, axis=1, keepdims=True)
        out_ref[:, s * w : (s + 1) * w] = values
    out_ref[...] *= lax.rsqrt(squares / (parts * w) + EPSILON)


def call(kernel, out_shape, **kw):
    params = pltpu.CompilerParams(vmem_limit_bytes=VMEM_LIMIT)
    return pl.pallas_call(kernel, out_shape=out_shape, compiler_params=params, **kw)


def columns(values, n):
    rows, width = values.shape
    return values.reshape(rows, n, width // n).transpose(1, 0, 2)


def exchange(values):
    return lax.all_to_all(values, "cent", split_axis=0, concat_axis=0, tiled=True)


def shards(points, point_cluster, cand_blocks, cent1_prev, parent, cent2_prev):
    point_rows, width = points.shape
    block_count = point_rows // BLOCK
    owned = cent1_prev.shape[0]
    upper_rows = cent2_prev.shape[0]
    n = lax.axis_size("cent")
    dp, me = lax.axis_index("dp"), lax.axis_index("cent")
    w = width // n
    rows = n * owned
    f32, bf16, i16, i32 = jnp.float32, jnp.bfloat16, jnp.int16, jnp.int32
    shape = jax.ShapeDtypeStruct

    prev_scale = jnp.maximum(jnp.max(jnp.abs(cent1_prev), axis=1), FLOOR)
    small = jnp.concatenate(
        [(point_cluster - dp * rows).astype(f32), (parent - dp * upper_rows).astype(f32), prev_scale]
    )
    small = lax.all_gather(small, "cent", axis=0, tiled=False)
    ids = small[:, :point_rows].astype(i32).reshape(n * block_count, BLOCK)
    parents = small[:, point_rows : point_rows + owned].astype(i32).reshape(1, rows)
    scales = (small[:, point_rows + owned :] / CODE).reshape(rows, 1)

    arrived = exchange(columns(points, n)).reshape(n * point_rows, w)
    prev_code = jnp.round(cent1_prev * (CODE / prev_scale)[:, None]).astype(i16)
    prev = exchange(columns(prev_code, n)).reshape(rows, w)

    table_rows = lax.all_gather(cent2_prev, "dp", axis=0, tiled=True)

    vmem = pl.BlockSpec(memory_space=pltpu.VMEM)
    high, low, code, stat = call(
        sums_kernel,
        (shape((rows, w), bf16), shape((rows, w), bf16), shape((rows, w), i16), shape((2, rows), f32)),
        in_specs=[pl.BlockSpec(memory_space=pltpu.SMEM)] + [vmem] * 4,
        out_specs=(vmem,) * 4,
        scratch_shapes=[pltpu.VMEM((rows, w), f32), pltpu.VMEM((rows, BLOCK), f32)],
        name="sums",
    )(ids[:, 0] // BLOCK, ids % BLOCK, arrived, prev, scales)
    stats = lax.all_gather(stat, "cent", axis=0, tiled=False)
    back = exchange(code.reshape(n, owned, w))

    upper = call(
        functools.partial(upper_kernel, width),
        shape((upper_rows, w), f32),
        in_specs=[vmem] * 4,
        out_specs=vmem,
        name="upper",
    )(stats, parents, high, low)
    uppers = lax.all_gather(upper, "cent", axis=0, tiled=False)

    mine = lax.dynamic_slice_in_dim(stats[:, 1, :], me * owned, owned, axis=1) / CODE
    cent1_new = call(
        decode_kernel, shape((owned, width), f32), in_specs=[vmem] * 2, out_specs=vmem, name="decode"
    )(back, mine.T)

    unit_points = rms_norm(points.astype(f32)).astype(bf16)
    table_units = rms_norm(table_rows.astype(f32)).astype(bf16)
    products = lax.dot_general(
        unit_points, table_units, (((1,), (1,)), ((), ())), preferred_element_type=f32
    )
    column_block = jnp.arange(table_rows.shape[0]) // BLOCK
    listed = jnp.any(cand_blocks[:, :, None] == column_block[None, None, :], axis=1)
    weights = jnp.exp(products * (SHARPNESS / width)).reshape(block_count, BLOCK, -1)
    running = jnp.sum(weights * listed[:, None, :].astype(f32), axis=2).reshape(point_rows)
    point_score = jnp.log(running)

    tile = min(upper_rows, BLOCK)
    cent2_new = call(
        join_kernel,
        shape((upper_rows, width), f32),
        grid=(upper_rows // tile,),
        in_specs=[pl.BlockSpec((n, tile, w), lambda i: (0, i, 0))],
        out_specs=pl.BlockSpec((tile, width), lambda i: (i, 0)),
        name="join",
    )(uppers)
    return (cent1_new, cent2_new, point_score)


def solution(mesh):
    placed = (
        P(("dp", "cent"), None),
        P(("dp", "cent")),
        P(("dp", "cent"), None),
        P(("dp", "cent"), None),
        P(("dp", "cent")),
        P("dp", None),
    )
    return jax.shard_map(
        shards,
        mesh=mesh,
        in_specs=placed,
        out_specs=(P(("dp", "cent"), None), P("dp", None), P(("dp", "cent"))),
        check_vma=False,
    )
```

```python
import functools

import jax
import jax.numpy as jnp
from jax import lax
from jax.experimental import pallas as pl
from jax.experimental.pallas import tpu as pltpu
from jax.sharding import PartitionSpec as P

BLOCK = 128
EPSILON = 1e-06
SHARPNESS = 20.0
CODE = 32000.0
FLOOR = 1e-30
VMEM_LIMIT = 48 * 1024 * 1024
f32, bf16, i16, i32 = jnp.float32, jnp.bfloat16, jnp.int16, jnp.int32
shape = jax.ShapeDtypeStruct
VMEM = pl.BlockSpec(memory_space=pltpu.VMEM)
SMEM = pl.BlockSpec(memory_space=pltpu.SMEM)


def rms_norm(values):
    return values * lax.rsqrt(jnp.mean(values * values, axis=-1, keepdims=True) + EPSILON)


def split(values):
    high = values.astype(bf16)
    return high, (values - high.astype(f32)).astype(bf16)


def dot(a, b):
    return jnp.dot(a, b, preferred_element_type=f32)


def dot_lanes(a, b):
    return lax.dot_general(a, b, (((1,), (1,)), ((), ())), preferred_element_type=f32)


def to_lanes(column):
    rows = column.shape[0]
    pick = jnp.where(lax.broadcasted_iota(i32, (8, BLOCK), 1) == 0, 1.0, 0.0).astype(bf16)
    return dot_lanes(pick, jnp.broadcast_to(column, (rows, BLOCK)).astype(bf16))[0:1]


def to_column(lanes):
    k = lanes.shape[1]
    eye = lax.broadcasted_iota(i32, (k, k), 0) == lax.broadcasted_iota(i32, (k, k), 1)
    return jnp.sum(jnp.where(eye, lanes, 0.0), axis=1, keepdims=True)


def exponent_of(top):
    return jnp.clip(jnp.ceil(jnp.log2(jnp.maximum(top * 1.001, FLOOR))), -100.0, 100.0)


def head_rows(count, w):
    return -(-count // (16 * w)) * 16


def part(ref, s, w):
    return ref.at[s] if len(ref.shape) == 3 else ref.at[:, pl.ds(pl.multiple_of(s * w, w), w)]


def pack_kernel(me_ref, *refs):
    n = len(refs) // 2
    for m in range(n):
        refs[n + m][...] = refs[m][...].reshape(refs[n + m].shape)


def prev_kernel(w, me_ref, prev_ref, small_ref, *refs):
    outs, head = refs[:-1], refs[-1]
    n = len(outs)
    owned = outs[0].shape[0] - head.shape[0]
    me = me_ref[0]
    top = jnp.zeros((owned, 1), f32)
    for s in range(n):
        top = jnp.maximum(top, jnp.max(jnp.abs(part(prev_ref, s, w)[...]), axis=1, keepdims=True))
    exponent = exponent_of(top)
    factor = CODE * jnp.exp2(-exponent)
    head[...] = jnp.zeros_like(head)
    known = small_ref.shape[0]
    head[0:known, :] = small_ref[...]
    for j in range(owned // w):
        lanes = to_lanes(exponent[j * w : (j + 1) * w])
        head[known + j : known + j + 1, :] = lanes.astype(i32)
    for m in range(n):
        outs[m][0:owned, :] = jnp.round(part(prev_ref, me ^ m, w)[...] * factor).astype(i16)
        outs[m][owned:, :] = head[...].astype(i16)


def sums_kernel(n, me_ref, block_ref, ids_ref, scale_ref, *refs):
    points, prevs, (high_ref, low_ref, stat_ref), codes = refs[:n], refs[n : 2 * n], refs[2 * n : 2 * n + 3], refs[2 * n + 3 : 3 * n + 3]
    acc, count = refs[3 * n + 3 :]
    rows, w = acc.shape
    owned = codes[0].shape[0]
    blocks = ids_ref.shape[0] // n
    me = me_ref[0]
    acc[...] = jnp.zeros_like(acc)
    count[...] = jnp.zeros_like(count)
    centroid = lax.broadcasted_iota(i32, (BLOCK, BLOCK), 0)
    ones = jnp.ones((BLOCK, BLOCK), bf16)
    for m in range(n):

        def add(i, carry, m=m):
            at_block = m * blocks + i
            member = jnp.where(centroid == ids_ref[pl.ds(at_block, 1), :], 1.0, 0.0).astype(bf16)
            at = pl.ds(pl.multiple_of(block_ref[at_block] * BLOCK, BLOCK), BLOCK)
            acc[at, :] += dot(member, points[m][pl.ds(pl.multiple_of(i * BLOCK, BLOCK), BLOCK), :])
            count[at, :] += dot(member, ones)
            return carry

        lax.fori_loop(0, blocks, add, 0, unroll=4)
    unit = jnp.ones((8, w), bf16)
    for m in range(n):
        at = pl.ds(pl.multiple_of((me ^ m) * owned, owned), owned)
        prev = prevs[m][0:owned, :].astype(f32) * scale_ref[m * owned : (m + 1) * owned, :]
        x = acc[at, :] / jnp.maximum(count[at, :][:, :w], 1.0) + prev
        high, low = split(x)
        high_ref[at, :] = high
        low_ref[at, :] = low
        square_high, square_low = split(x * x)
        stat_ref[0:1, at] = (dot_lanes(unit, square_high) + dot_lanes(unit, square_low))[0:1]
        top = jnp.max(jnp.abs(x), axis=1, keepdims=True) * 1.01
        scale = jnp.maximum(top, FLOOR).astype(bf16).astype(f32)
        stat_ref[1:2, at] = to_lanes(scale)
        codes[m][...] = jnp.round(x * (CODE / scale)).astype(i16)


def upper_kernel(n, width, parent_ref, high_ref, low_ref, *refs):
    stats, code_ref, sums, head = refs[:n], refs[n], refs[n + 1], refs[n + 2]
    rows, w = sums.shape
    squares = stats[0][0:1, :]
    for m in range(1, n):
        squares += stats[m][0:1, :]
    factor = lax.rsqrt(squares / width + EPSILON)
    parent = parent_ref[...]
    at_row = lax.broadcasted_iota(i32, (BLOCK, parent.shape[1]), 0)

    def one(i, carry):
        weight_high, weight_low = split(jnp.where(at_row + i * BLOCK == parent, factor, 0.0))
        total = dot(weight_high, high_ref[...]) + dot(weight_high, low_ref[...])
        sums[pl.ds(pl.multiple_of(i * BLOCK, BLOCK), BLOCK), :] = total + dot(weight_low, high_ref[...])
        return carry

    lax.fori_loop(0, rows // BLOCK, one, 0)
    head[...] = jnp.zeros_like(head)
    for j in range(rows // w):
        at = slice(j * w, (j + 1) * w)
        total = sums[at, :]
        exponent = exponent_of(jnp.max(jnp.abs(total), axis=1, keepdims=True))
        code_ref[at, :] = jnp.round(total * (CODE * jnp.exp2(-exponent))).astype(i16)
        head[j : j + 1, :] = to_lanes(exponent).astype(i32)
    code_ref[rows:, :] = head[...].astype(i16)


def join_kernel(w, me_ref, *refs):
    parts, out_ref, values = refs[:-2], refs[-2], refs[-1]
    n = len(parts)
    rows = values.shape[1]
    me = me_ref[0]

    for j in range(rows // w):
        at = slice(j * w, (j + 1) * w)
        squares = jnp.zeros((w, 1), f32)
        for m in range(n):
            head = parts[m][rows : rows + 16, :].astype(i32).astype(f32)
            scale = jnp.exp2(to_column(head[j : j + 1, :])) / CODE
            value = parts[m][at, :].astype(f32) * scale
            values[m, at, :] = value
            squares += jnp.sum(value * value, axis=1, keepdims=True)
        factor = lax.rsqrt(squares / (n * w) + EPSILON)
        for m in range(n):
            part(out_ref, me ^ m, w)[at, :] = values[m, at, :] * factor


def decode_kernel(w, n, me_ref, *refs):
    codes, stats, out_ref, values = refs[:n], refs[n : 2 * n], refs[2 * n], refs[2 * n + 1]
    rows = codes[0].shape[0]
    me = me_ref[0]
    for j in range(rows // BLOCK):
        at = slice(j * BLOCK, (j + 1) * BLOCK)
        squares = jnp.zeros((BLOCK, 1), f32)
        for m in range(n):
            lanes = stats[m][1:2, pl.ds(pl.multiple_of(me * rows + j * BLOCK, BLOCK), BLOCK)]
            value = codes[m][at, :].astype(f32) * (to_column(lanes) / CODE)
            values[m, at, :] = value
            squares += jnp.sum(value * value, axis=1, keepdims=True)
        factor = lax.rsqrt(squares / (n * w) + EPSILON)
        for m in range(n):
            part(out_ref, me ^ m, w)[at, :] = values[m, at, :] * factor


def call(kernel, out_shape, **kw):
    params = pltpu.CompilerParams(vmem_limit_bytes=VMEM_LIMIT)
    return pl.pallas_call(kernel, out_shape=out_shape, compiler_params=params, **kw)


def columns(values, n):
    rows, width = values.shape
    return values.reshape(rows, n, width // n).transpose(1, 0, 2)


def shards(points, point_cluster, cand_blocks, cent1_prev, parent, cent2_prev):
    point_rows, width = points.shape
    block_count = point_rows // BLOCK
    owned = cent1_prev.shape[0]
    upper_rows = cent2_prev.shape[0]
    n = lax.axis_size("cent")
    dp = lax.axis_index("dp")
    me = lax.axis_index("cent").astype(i32).reshape(1)
    w = width // n
    rows = n * owned
    wide = w % BLOCK == 0
    far_first = range(n - 1, 0, -1)

    def swap(value, mask):
        return lax.ppermute(value, "cent", [(i, i ^ mask) for i in range(n)])

    def swap_all(values):
        arrived = {m: swap(values[m], m) for m in far_first}
        return [values[0]] + [arrived[m] for m in range(1, n)]

    tile = 2 * BLOCK
    if wide:
        source = points
        specs = [pl.BlockSpec((tile, w), lambda i, at, m=m: (i, at[0] ^ m)) for m in range(n)]
    else:
        source = columns(points, n)
        specs = [pl.BlockSpec((1, tile, w), lambda i, at, m=m: (at[0] ^ m, i, 0)) for m in range(n)]
    packed = call(
        pack_kernel,
        [shape((point_rows, w), bf16)] * n,
        grid_spec=pltpu.PrefetchScalarGridSpec(
            num_scalar_prefetch=1,
            grid=(point_rows // tile,),
            in_specs=specs,
            out_specs=[pl.BlockSpec((tile, w), lambda i, at: (i, 0))] * n,
        ),
        name="pack",
    )(me, *([source] * n))
    arrived = swap_all(packed)

    small = jnp.concatenate([point_cluster - dp * rows, parent - dp * upper_rows]).reshape(-1, w)
    head = head_rows(point_rows + 2 * owned, w)
    prev_codes = call(
        functools.partial(prev_kernel, w),
        [shape((owned + head, w), i16)] * n,
        in_specs=[SMEM, VMEM, VMEM],
        out_specs=[VMEM] * n,
        scratch_shapes=[pltpu.VMEM((head, w), i32)],
        name="prev",
    )(me, cent1_prev if wide else columns(cent1_prev, n), small)
    prevs = swap_all(prev_codes)
    heads = jnp.stack([p[owned:].astype(i32) for p in prevs]).reshape(n, head * w)
    ids = heads[:, :point_rows].reshape(n * block_count, BLOCK)
    origin = me ^ jnp.arange(n)
    parents = heads[origin, point_rows : point_rows + owned].reshape(1, rows)
    scales = jnp.exp2(heads[:, point_rows + owned : point_rows + 2 * owned].astype(f32)) / CODE

    table_rows = lax.all_gather(cent2_prev, "dp", axis=0, tiled=True)

    out = call(
        functools.partial(sums_kernel, n),
        [shape((rows, w), bf16)] * 2 + [shape((2, rows), f32)] + [shape((owned, w), i16)] * n,
        in_specs=[SMEM, SMEM] + [VMEM] * (2 * n + 2),
        out_specs=[VMEM] * (n + 3),
        scratch_shapes=[pltpu.VMEM((rows, w), f32), pltpu.VMEM((rows, BLOCK), f32)],
        name="sums",
    )(me, ids[:, 0] // BLOCK, ids % BLOCK, scales.reshape(rows, 1), *arrived, *prevs)
    high, low, stat = out[:3]
    stats = swap_all([stat] * n)
    back = swap_all(out[3:])

    upper_head = head_rows(upper_rows, w)
    code = call(
        functools.partial(upper_kernel, n, width),
        shape((upper_rows + upper_head, w), i16),
        in_specs=[VMEM] * (n + 3),
        out_specs=VMEM,
        scratch_shapes=[pltpu.VMEM((upper_rows, w), f32), pltpu.VMEM((upper_head, w), i32)],
        name="upper",
    )(parents, high, low, *stats)
    half = n // 2
    parts = {0: code, half: swap(code, half)}
    for m in range(half - 1, 0, -1):
        parts[m] = swap(code, m)
    for m in range(half - 1, 0, -1):
        parts[half + m] = swap(parts[half], m)

    def joined(kernel, values, out_rows, name, scratch_rows):
        result = call(
            kernel,
            shape((out_rows, width) if wide else (n, out_rows, w), f32),
            in_specs=[SMEM] + [VMEM] * len(values),
            out_specs=VMEM,
            scratch_shapes=[pltpu.VMEM((n, scratch_rows, w), f32)],
            name=name,
        )(me, *values)
        return result if wide else result.transpose(1, 0, 2).reshape(out_rows, width)

    cent1_new = joined(functools.partial(decode_kernel, w, n), back + stats, owned, "decode", owned)

    unit_points = rms_norm(points.astype(f32)).astype(bf16)
    table_units = rms_norm(table_rows.astype(f32)).astype(bf16)
    products = lax.dot_general(
        unit_points, table_units, (((1,), (1,)), ((), ())), preferred_element_type=f32
    )
    column_block = jnp.arange(table_rows.shape[0]) // BLOCK
    listed = jnp.any(cand_blocks[:, :, None] == column_block[None, None, :], axis=1)
    weights = jnp.exp(products * (SHARPNESS / width)).reshape(block_count, BLOCK, -1)
    running = jnp.sum(weights * listed[:, None, :].astype(f32), axis=2).reshape(point_rows)
    point_score = jnp.log(running)

    cent2_new = joined(functools.partial(join_kernel, w), [parts[m] for m in range(n)], upper_rows, "join", upper_rows)
    return (cent1_new, cent2_new, point_score)


def solution(mesh):
    placed = (
        P(("dp", "cent"), None),
        P(("dp", "cent")),
        P(("dp", "cent"), None),
        P(("dp", "cent"), None),
        P(("dp", "cent")),
        P("dp", None),
    )
    return jax.shard_map(
        shards,
        mesh=mesh,
        in_specs=placed,
        out_specs=(P(("dp", "cent"), None), P("dp", None), P(("dp", "cent"))),
        check_vma=False,
    )
```

```python
import functools

import jax
import jax.numpy as jnp
from jax import lax
from jax.experimental import pallas as pl
from jax.experimental.pallas import tpu as pltpu
from jax.sharding import PartitionSpec as P

BLOCK = 128
EPSILON = 1e-06
SHARPNESS = 20.0
CODE = 32000.0
FLOOR = 1e-30
VMEM_LIMIT = 48 * 1024 * 1024
f32, bf16, i16, i32 = jnp.float32, jnp.bfloat16, jnp.int16, jnp.int32
shape = jax.ShapeDtypeStruct
VMEM = pl.BlockSpec(memory_space=pltpu.VMEM)
SMEM = pl.BlockSpec(memory_space=pltpu.SMEM)


def rms_norm(values):
    return values * lax.rsqrt(jnp.mean(values * values, axis=-1, keepdims=True) + EPSILON)


def split(values):
    high = values.astype(bf16)
    return high, (values - high.astype(f32)).astype(bf16)


def dot(a, b):
    return jnp.dot(a, b, preferred_element_type=f32)


def dot_lanes(a, b):
    return lax.dot_general(a, b, (((1,), (1,)), ((), ())), preferred_element_type=f32)


def to_lanes(column):
    rows = column.shape[0]
    pick = jnp.where(lax.broadcasted_iota(i32, (8, BLOCK), 1) == 0, 1.0, 0.0).astype(bf16)
    return dot_lanes(pick, jnp.broadcast_to(column, (rows, BLOCK)).astype(bf16))[0:1]


def to_column(lanes):
    k = lanes.shape[1]
    eye = lax.broadcasted_iota(i32, (k, k), 0) == lax.broadcasted_iota(i32, (k, k), 1)
    return jnp.sum(jnp.where(eye, lanes, 0.0), axis=1, keepdims=True)


def exponent_of(top):
    return jnp.clip(jnp.ceil(jnp.log2(jnp.maximum(top * 1.001, FLOOR))), -100.0, 100.0)


def head_rows(count, w):
    return -(-count // (16 * w)) * 16


def part(ref, s, w):
    return ref.at[s] if len(ref.shape) == 3 else ref.at[:, pl.ds(pl.multiple_of(s * w, w), w)]


def chunk(index, size):
    return pl.ds(pl.multiple_of(index * size, size), size)


def pack_kernel(points_ref, out_ref):
    n, _, w = out_ref.shape
    for s in range(n):
        out_ref[s] = points_ref[:, s * w : (s + 1) * w]


def prev_kernel(w, me_ref, prev_ref, small_ref, *refs):
    outs, head = refs[:-1], refs[-1]
    n = len(outs)
    owned = outs[0].shape[0] - head.shape[0]
    me = me_ref[0]
    top = jnp.zeros((owned, 1), f32)
    for s in range(n):
        top = jnp.maximum(top, jnp.max(jnp.abs(part(prev_ref, s, w)[...]), axis=1, keepdims=True))
    exponent = exponent_of(top)
    factor = CODE * jnp.exp2(-exponent)
    head[...] = jnp.zeros_like(head)
    known = small_ref.shape[0]
    head[0:known, :] = small_ref[...]
    for j in range(owned // w):
        lanes = to_lanes(exponent[j * w : (j + 1) * w])
        head[known + j : known + j + 1, :] = lanes.astype(i32)
    for m in range(n):
        outs[m][0:owned, :] = jnp.round(part(prev_ref, me ^ m, w)[...] * factor).astype(i16)
        outs[m][owned:, :] = head[...].astype(i16)


def prepare_kernel(blocks, me_ref, *refs):
    arrived, (member_ref, block_ref, inverse_ref, prev_ref, upper_ref, count) = refs[:-6], refs[-6:]
    n = len(arrived)
    rows, w = prev_ref.shape
    owned = rows // n
    upper_rows = upper_ref.shape[-2]
    me = me_ref[0]
    lines = blocks * BLOCK // w
    count[...] = jnp.zeros_like(count)
    centroid = lax.broadcasted_iota(i32, (BLOCK, BLOCK), 0)
    ones = jnp.ones((BLOCK, BLOCK), bf16)
    parent_at = lax.broadcasted_iota(i32, (upper_rows, w), 0)
    for m in range(n):
        s = me ^ m
        head = arrived[m][owned:, :].astype(i32)
        for i in range(blocks):
            row = [head[(i * BLOCK + k) // w : (i * BLOCK + k) // w + 1, :] for k in range(0, BLOCK, w)]
            ids = jnp.concatenate(row, axis=1) if len(row) > 1 else row[0]
            number = jnp.max(ids.astype(f32)).astype(i32) // BLOCK
            block_ref[s * blocks + i] = number
            member = jnp.where(centroid == ids - number * BLOCK, 1.0, 0.0).astype(bf16)
            member_ref[chunk(s * blocks + i, BLOCK), :] = member
            count[chunk(number, BLOCK), :] += dot(member, ones)
        for j in range(owned // w):
            parents = head[lines + j : lines + j + 1, :]
            one_hot = jnp.where(parent_at == parents, 1.0, 0.0).astype(bf16)
            if len(upper_ref.shape) == 2:
                upper_ref[:, chunk(s * (owned // w) + j, w)] = one_hot
            else:
                upper_ref[s * (owned // w) + j] = one_hot
            scale = head[lines + owned // w + j : lines + owned // w + j + 1, :].astype(f32)
            values = arrived[m][j * w : (j + 1) * w, :].astype(f32)
            prev_ref[chunk(s * (owned // w) + j, w), :] = values * (jnp.exp2(to_column(scale)) / CODE)
    inverse_ref[...] = 1.0 / jnp.maximum(count[...][:, :w], 1.0)


def sums_kernel(block_ref, points_ref, member_ref, inverse_ref, prev_ref, x_ref, stat_ref, code_ref, acc):
    s = pl.program_id(0)
    rows, w = acc.shape
    n, owned, _ = code_ref.shape
    blocks = points_ref.shape[1] // BLOCK

    @pl.when(s == 0)
    def _():
        acc[...] = jnp.zeros_like(acc)

    for i in range(blocks):
        at = slice(i * BLOCK, (i + 1) * BLOCK)
        acc[chunk(block_ref[s * blocks + i], BLOCK), :] += dot(member_ref[at, :], points_ref[0, at, :])

    @pl.when(s == pl.num_programs(0) - 1)
    def _():
        unit = jnp.ones((8, w), bf16)
        for o in range(n):
            at = slice(o * owned, (o + 1) * owned)
            x = acc[at, :] * inverse_ref[at, :] + prev_ref[at, :]
            x_ref[at, :] = x
            square_high, square_low = split(x * x)
            squares = (dot_lanes(unit, square_high) + dot_lanes(unit, square_low))[0:1]
            top = jnp.max(jnp.abs(x), axis=1, keepdims=True) * 1.01
            scale = jnp.maximum(top, FLOOR).astype(bf16).astype(f32)
            scales = to_lanes(scale)
            for d in range(n):
                stat_ref[d, 0:1, at] = squares
                stat_ref[d, 1:2, at] = scales
            code_ref[o] = jnp.round(x * (CODE / scale)).astype(i16)


def upper_kernel(width, stat_ref, member_ref, x_ref, code_ref, high, low, sums, head):
    n = stat_ref.shape[0]
    rows, w = sums.shape
    squares = stat_ref[0, 0:1, :]
    for s in range(1, n):
        squares += stat_ref[s, 0:1, :]
    factor = lax.rsqrt(squares / width + EPSILON)
    for j in range(x_ref.shape[0] // BLOCK):
        at = slice(j * BLOCK, (j + 1) * BLOCK)
        high[at, :], low[at, :] = split(x_ref[at, :] * to_column(factor[:, at]))
    member = member_ref[...]
    sums[...] = dot(member, high[...]) + dot(member, low[...])
    head[...] = jnp.zeros_like(head)
    for j in range(rows // w):
        at = slice(j * w, (j + 1) * w)
        total = sums[at, :]
        exponent = exponent_of(jnp.max(jnp.abs(total), axis=1, keepdims=True))
        code_ref[at, :] = jnp.round(total * (CODE * jnp.exp2(-exponent))).astype(i16)
        head[j : j + 1, :] = to_lanes(exponent).astype(i32)
    code_ref[rows:, :] = head[...].astype(i16)


def join_kernel(w, me_ref, *refs):
    parts, out_ref, values = refs[:-2], refs[-2], refs[-1]
    n = len(parts)
    rows = values.shape[1]
    me = me_ref[0]
    for j in range(rows // w):
        at = slice(j * w, (j + 1) * w)
        squares = jnp.zeros((w, 1), f32)
        for m in range(n):
            head = parts[m][rows : rows + 16, :].astype(i32).astype(f32)
            scale = jnp.exp2(to_column(head[j : j + 1, :])) / CODE
            value = parts[m][at, :].astype(f32) * scale
            values[m, at, :] = value
            squares += jnp.sum(value * value, axis=1, keepdims=True)
        factor = lax.rsqrt(squares / (n * w) + EPSILON)
        for m in range(n):
            part(out_ref, me ^ m, w)[at, :] = values[m, at, :] * factor


def decode_kernel(me_ref, code_ref, stat_ref, out_ref):
    n, rows, w = code_ref.shape
    me = me_ref[0]
    for j in range(rows // BLOCK):
        at = slice(j * BLOCK, (j + 1) * BLOCK)
        squares = jnp.zeros((BLOCK, 1), f32)
        for s in range(n):
            lanes = stat_ref[s, 1:2, chunk(me * (rows // BLOCK) + j, BLOCK)]
            value = code_ref[s, at, :].astype(f32) * (to_column(lanes) / CODE)
            out_ref[at, s * w : (s + 1) * w] = value
            squares += jnp.sum(value * value, axis=1, keepdims=True)
        out_ref[at, :] *= lax.rsqrt(squares / (n * w) + EPSILON)


def call(kernel, out_shape, **kw):
    params = pltpu.CompilerParams(vmem_limit_bytes=VMEM_LIMIT)
    return pl.pallas_call(kernel, out_shape=out_shape, compiler_params=params, **kw)


def columns(values, n):
    rows, width = values.shape
    return values.reshape(rows, n, width // n).transpose(1, 0, 2)


def shards(points, point_cluster, cand_blocks, cent1_prev, parent, cent2_prev):
    point_rows, width = points.shape
    block_count = point_rows // BLOCK
    owned = cent1_prev.shape[0]
    upper_rows = cent2_prev.shape[0]
    n = lax.axis_size("cent")
    dp = lax.axis_index("dp")
    me = lax.axis_index("cent").astype(i32).reshape(1)
    w = width // n
    rows = n * owned
    wide = w % BLOCK == 0

    def swap(value, mask):
        return lax.ppermute(value, "cent", [(i, i ^ mask) for i in range(n)])

    def exchange(values):
        return lax.all_to_all(values, "cent", split_axis=0, concat_axis=0, tiled=True)

    table_rows = lax.all_gather(cent2_prev, "dp", axis=0, tiled=True)
    tile = 2 * BLOCK
    if wide:
        packed = call(
            pack_kernel,
            shape((n, point_rows, w), bf16),
            grid=(point_rows // tile,),
            in_specs=[pl.BlockSpec((tile, width), lambda i: (i, 0))],
            out_specs=pl.BlockSpec((n, tile, w), lambda i: (0, i, 0)),
            name="pack",
        )(points)
    else:
        packed = columns(points, n)
    packed, point_cluster, parent = lax.optimization_barrier((packed, point_cluster, parent))
    arrived = exchange(packed)

    small = jnp.concatenate([point_cluster - dp * rows, parent - dp * upper_rows]).reshape(-1, w)
    head = head_rows(point_rows + 2 * owned, w)
    prev_codes = call(
        functools.partial(prev_kernel, w),
        [shape((owned + head, w), i16)] * n,
        in_specs=[SMEM, VMEM, VMEM],
        out_specs=[VMEM] * n,
        scratch_shapes=[pltpu.VMEM((head, w), i32)],
        name="prev",
    )(me, cent1_prev if wide else columns(cent1_prev, n), small)
    prevs = {m: swap(prev_codes[m], m) for m in range(n - 1, 0, -1)}
    prevs = [prev_codes[0]] + [prevs[m] for m in range(1, n)]
    upper_shape = (upper_rows, rows) if wide else (rows // w, upper_rows, w)
    member, numbers, inverse, prev, upper_member = call(
        functools.partial(prepare_kernel, block_count),
        [
            shape((n * point_rows, BLOCK), bf16),
            shape((n * block_count,), i32),
            shape((rows, w), f32),
            shape((rows, w), f32),
            shape(upper_shape, bf16),
        ],
        in_specs=[SMEM] + [VMEM] * n,
        out_specs=[VMEM, SMEM, VMEM, VMEM, VMEM],
        scratch_shapes=[pltpu.VMEM((rows, BLOCK), f32)],
        name="prepare",
    )(me, *prevs)

    points, table_rows = lax.optimization_barrier((points, table_rows))
    unit_points = rms_norm(points.astype(f32)).astype(bf16)
    table_units = rms_norm(table_rows.astype(f32)).astype(bf16)
    products = lax.dot_general(
        unit_points, table_units, (((1,), (1,)), ((), ())), preferred_element_type=f32
    )
    column_block = jnp.arange(table_rows.shape[0]) // BLOCK
    listed = jnp.any(cand_blocks[:, :, None] == column_block[None, None, :], axis=1)
    weights = jnp.exp(products * (SHARPNESS / width)).reshape(block_count, BLOCK, -1)
    running = jnp.sum(weights * listed[:, None, :].astype(f32), axis=2).reshape(point_rows)
    point_score, numbers = lax.optimization_barrier((jnp.log(running), numbers))

    whole = lambda *dims: pl.BlockSpec(dims, lambda s, *_: (0,) * len(dims))
    x, stat, code = call(
        sums_kernel,
        [shape((rows, w), f32), shape((n, 2, rows), f32), shape((n, owned, w), i16)],
        grid_spec=pltpu.PrefetchScalarGridSpec(
            num_scalar_prefetch=1,
            grid=(n,),
            in_specs=[
                pl.BlockSpec((1, point_rows, w), lambda s, _: (s, 0, 0)),
                pl.BlockSpec((point_rows, BLOCK), lambda s, _: (s, 0)),
                whole(rows, w),
                whole(rows, w),
            ],
            out_specs=[whole(rows, w), whole(n, 2, rows), whole(n, owned, w)],
            scratch_shapes=[pltpu.VMEM((rows, w), f32)],
        ),
        name="sums",
    )(numbers, arrived, member, inverse, prev)
    stats = exchange(stat)
    back = exchange(code)

    upper_head = head_rows(upper_rows, w)
    code = call(
        functools.partial(upper_kernel, width),
        shape((upper_rows + upper_head, w), i16),
        in_specs=[VMEM] * 3,
        out_specs=VMEM,
        scratch_shapes=[
            pltpu.VMEM((rows, w), bf16),
            pltpu.VMEM((rows, w), bf16),
            pltpu.VMEM((upper_rows, w), f32),
            pltpu.VMEM((upper_head, w), i32),
        ],
        name="upper",
    )(stats, upper_member if wide else upper_member.transpose(1, 0, 2).reshape(upper_rows, rows), x)
    half = n // 2
    parts = {0: code, half: swap(code, half)}
    for m in range(half - 1, 0, -1):
        parts[m] = swap(code, m)
    for m in range(half - 1, 0, -1):
        parts[half + m] = swap(parts[half], m)

    cent1_new = call(
        decode_kernel,
        shape((owned, width), f32),
        in_specs=[SMEM, VMEM, VMEM],
        out_specs=VMEM,
        name="decode",
    )(me, back, stats)

    cent2_new = call(
        functools.partial(join_kernel, w),
        shape((upper_rows, width) if wide else (n, upper_rows, w), f32),
        in_specs=[SMEM] + [VMEM] * n,
        out_specs=VMEM,
        scratch_shapes=[pltpu.VMEM((n, upper_rows, w), f32)],
        name="join",
    )(me, *[parts[m] for m in range(n)])
    if not wide:
        cent2_new = cent2_new.transpose(1, 0, 2).reshape(upper_rows, width)
    return (cent1_new, cent2_new, point_score)


def solution(mesh):
    placed = (
        P(("dp", "cent"), None),
        P(("dp", "cent")),
        P(("dp", "cent"), None),
        P(("dp", "cent"), None),
        P(("dp", "cent")),
        P("dp", None),
    )
    return jax.shard_map(
        shards,
        mesh=mesh,
        in_specs=placed,
        out_specs=(P(("dp", "cent"), None), P("dp", None), P(("dp", "cent"))),
        check_vma=False,
    )
```

```python
import functools

import jax
import jax.numpy as jnp
from jax import lax
from jax.experimental import pallas as pl
from jax.experimental.pallas import tpu as pltpu
from jax.sharding import PartitionSpec as P

BLOCK = 128
EPSILON = 1e-06
SHARPNESS = 20.0
CODE = 32000.0
FLOOR = 1e-30
VMEM_LIMIT = 48 * 1024 * 1024
f32, bf16, i16, i32 = jnp.float32, jnp.bfloat16, jnp.int16, jnp.int32
shape = jax.ShapeDtypeStruct
VMEM = pl.BlockSpec(memory_space=pltpu.VMEM)
SMEM = pl.BlockSpec(memory_space=pltpu.SMEM)
HBM = pl.BlockSpec(memory_space=pltpu.HBM)


def rms_norm(values):
    return values * lax.rsqrt(jnp.mean(values * values, axis=-1, keepdims=True) + EPSILON)


def split(values):
    high = values.astype(bf16)
    return high, (values - high.astype(f32)).astype(bf16)


def dot(a, b):
    return jnp.dot(a, b, preferred_element_type=f32)


def dot_lanes(a, b):
    return lax.dot_general(a, b, (((1,), (1,)), ((), ())), preferred_element_type=f32)


def to_lanes(column):
    rows = column.shape[0]
    pick = jnp.where(lax.broadcasted_iota(i32, (8, BLOCK), 1) == 0, 1.0, 0.0).astype(bf16)
    return dot_lanes(pick, jnp.broadcast_to(column, (rows, BLOCK)).astype(bf16))[0:1]


def to_column(lanes):
    k = lanes.shape[1]
    eye = lax.broadcasted_iota(i32, (k, k), 0) == lax.broadcasted_iota(i32, (k, k), 1)
    return jnp.sum(jnp.where(eye, lanes, 0.0), axis=1, keepdims=True)


def exponent_of(top):
    return jnp.clip(jnp.ceil(jnp.log2(jnp.maximum(top * 1.001, FLOOR))), -100.0, 100.0)


def encode(values, exponent):
    return jnp.round(values * (CODE * jnp.exp2(-exponent))).astype(i16)


def decode(codes, exponent):
    return codes.astype(f32) * (jnp.exp2(exponent) * (1.0 / CODE))


def head_rows(count, w):
    return -(-count // (16 * w)) * 16


def chunk(index, size):
    return pl.ds(pl.multiple_of(index * size, size), size)


def start(source, target, sem):
    copy = pltpu.make_async_copy(source, target, sem)
    copy.start()
    return copy


def start_all(sources, targets, sems):
    return [start(a, b, sems.at[k]) for k, (a, b) in enumerate(zip(sources, targets))]


def wait_all(copies):
    for copy in copies:
        copy.wait()


def pack_kernel(chunks, q_ref, points_ref, *refs):
    outs, sems = refs[:-1], refs[-1]
    sources = [
        points_ref.at[:, chunk((q_ref[0] ^ (k // chunks)) * chunks + k % chunks, BLOCK)] for k in range(len(outs))
    ]
    wait_all(start_all(sources, outs, sems))


def prev_kernel(q_ref, prev_ref, small_ref, *refs):
    h = (len(refs) - 4) // 2
    outs, (prev, head, sem, sems), held = refs[:h], refs[h : h + 4], refs[h + 4 :]
    owned, width = prev.shape
    w = width // h
    copy = start(prev_ref, prev, sem)
    known = small_ref.shape[0]
    head[...] = jnp.zeros_like(head)
    head[0:known, :] = small_ref[...]
    copy.wait()
    exponent = exponent_of(jnp.max(jnp.abs(prev[...]), axis=1, keepdims=True))
    for j in range(owned // w):
        lanes = to_lanes(exponent[j * w : (j + 1) * w])
        head[known + j : known + j + 1, :] = lanes.astype(i32)
    copies = []
    for m in range(h):
        held[m][0:owned, :] = encode(prev[:, chunk(q_ref[0] ^ m, w)], exponent)
        held[m][owned:, :] = head[...].astype(i16)
        copies.append(start(held[m], outs[m], sems.at[m]))
    wait_all(copies)


def prepare_kernel(blocks, n, me_ref, *refs):
    arrived, (member_ref, place_ref, near_ref, far_ref, prev_ref, upper_ref, count) = refs[:-7], refs[-7:]
    h = len(arrived)
    rows, w = prev_ref.shape
    owned = rows // h
    upper_rows = upper_ref.shape[0]
    me = me_ref[0]
    lines, each = blocks * BLOCK // w, owned // w
    count[...] = jnp.zeros_like(count)
    centroid = lax.broadcasted_iota(i32, (BLOCK, BLOCK), 0)
    ones = jnp.ones((BLOCK, BLOCK), bf16)
    parent_at = lax.broadcasted_iota(i32, (upper_rows, w), 0)
    for m in range(h):
        head = arrived[m][owned:, :].astype(i32)
        for i in range(blocks):
            row, lane = i * BLOCK // w, i * BLOCK % w
            ids = head[row : row + 1, lane : lane + BLOCK]
            number = jnp.max(ids.astype(f32)).astype(i32) // BLOCK
            place = number ^ (me * (owned // BLOCK))
            place_ref[m * blocks + i] = place
            member = jnp.where(centroid == ids - number * BLOCK, 1.0, 0.0).astype(bf16)
            at = (m * blocks + i) * BLOCK
            member_ref[at : at + BLOCK, :] = member
            count[chunk(place, BLOCK), :] += dot(member, ones)
        for j in range(each):
            at = slice(m * owned + j * w, m * owned + (j + 1) * w)
            parents = head[lines + j : lines + j + 1, :]
            upper_ref[:, at] = jnp.where(parent_at == parents, 1.0, 0.0).astype(bf16)
            exponent = to_column(head[lines + each + j : lines + each + j + 1, :].astype(f32))
            prev_ref[at, :] = decode(arrived[m][j * w : (j + 1) * w, :], exponent)
    near_ref[...] = count[0:rows, :]
    for j in range(rows // BLOCK):
        far = count[rows + j * BLOCK : rows + (j + 1) * BLOCK, 0:1]
        high = jnp.floor(far / 64.0)
        far_ref[j : j + 1, :] = (to_lanes(high) * 64.0 + to_lanes(far - high * 64.0)).astype(i32)


def sums_kernel(place_ref, member_ref, far_count_ref, *refs):
    h = (len(refs) - 5) // 2
    points, (acc_ref, code_ref), (code, head, sem), held = (
        refs[:h],
        refs[h : h + 2],
        refs[h + 2 : h + 5],
        refs[h + 5 :],
    )
    rows = acc_ref.shape[0] // 2
    blocks = held[0].shape[0] // BLOCK
    copies = start_all(points, held, sem)
    acc_ref[...] = jnp.zeros_like(acc_ref)
    for m in range(h):
        copies[m].wait()
        for i in range(blocks):
            at, here = (m * blocks + i) * BLOCK, slice(i * BLOCK, (i + 1) * BLOCK)
            acc_ref[chunk(place_ref[m * blocks + i], BLOCK), :] += dot(member_ref[at : at + BLOCK, :], held[m][here, :])
    copies = []
    lines = rows // BLOCK
    step = 2 * BLOCK
    for j in range(rows // step):
        at = slice(j * step, (j + 1) * step)
        value = acc_ref[rows + j * step : rows + (j + 1) * step, :]
        exponent = exponent_of(jnp.max(jnp.abs(value), axis=1, keepdims=True))
        code[at, :] = encode(value, exponent)
        lanes = to_lanes(exponent).astype(i32)
        for k in range(step // BLOCK):
            row = j * (step // BLOCK) + k
            head[row : row + 1, :] = lanes[:, k * BLOCK : (k + 1) * BLOCK]
    head[lines:, :] = far_count_ref[...]
    code[rows:, :] = head[...].astype(i16)
    start(code, code_ref, sem.at[h]).wait()


def refresh_kernel(chunks, h, near_ref, prev_ref, *refs):
    accs, crossed, (x_ref, stat_ref), outs = (
        refs[:chunks],
        refs[chunks : 2 * chunks],
        refs[2 * chunks : 2 * chunks + 2],
        refs[2 * chunks + 2 : 2 * chunks + 2 + h],
    )
    codes, stat, sem, held = refs[2 * chunks + 2 + h :][:h], *refs[2 * chunks + 2 + 2 * h :][:2], refs[2 * chunks + 4 + 2 * h :]
    rows, w = x_ref.shape
    owned = rows // h
    lines = rows // BLOCK
    wait_all(start_all(crossed, held, sem))
    heads = [held[c][rows:, :].astype(i32).astype(f32) for c in range(chunks)]
    unit = jnp.ones((8, BLOCK), bf16)
    copies = []
    for j in range(lines):
        at = slice(j * BLOCK, (j + 1) * BLOCK)
        count = near_ref[at, :] + to_column(heads[0][lines + j : lines + j + 1, :])
        inverse = 1.0 / jnp.maximum(count, 1.0)
        square, top = None, None
        for c in range(chunks):
            lanes = slice(c * BLOCK, (c + 1) * BLOCK)
            far = decode(held[c][at, :], to_column(heads[c][j : j + 1, :]))
            x = (accs[c][at, :] + far) * inverse + prev_ref[at, lanes]
            x_ref[at, lanes] = x
            square = x * x if c == 0 else square + x * x
            top = jnp.abs(x) if c == 0 else jnp.maximum(top, jnp.abs(x))
        square_high, square_low = split(square)
        stat[0:1, at] = (dot_lanes(unit, square_high) + dot_lanes(unit, square_low))[0:1]
        exponent = exponent_of(jnp.max(top, axis=1, keepdims=True))
        stat[1:2, at] = to_lanes(exponent)
        m, here = j * BLOCK // owned, slice(j * BLOCK % owned, j * BLOCK % owned + BLOCK)
        codes[m][here, :] = encode(x_ref[at, :], exponent)
        if (j + 1) * BLOCK % owned == 0:
            copies.append(start(codes[m], outs[m], sem.at[chunks + m]))
    copies.append(start(stat, stat_ref, sem.at[chunks + h]))
    wait_all(copies)


def put_codes(values, code, head):
    rows, w = values.shape
    head[...] = jnp.zeros_like(head)
    for j in range(rows // w):
        at = slice(j * w, (j + 1) * w)
        exponent = exponent_of(jnp.max(jnp.abs(values[at, :]), axis=1, keepdims=True))
        code[at, :] = encode(values[at, :], exponent)
        head[j : j + 1, :] = to_lanes(exponent).astype(i32)
    code[rows:, :] = head[...].astype(i16)


def get_codes(code, j, rows, size):
    w = code.shape[1]
    row, lane = j * size // w, j * size % w
    lanes = code[rows : rows + 16, :].astype(i32).astype(f32)[row : row + 1, lane : lane + size]
    return decode(code[j * size : (j + 1) * size, :], to_column(lanes))


def upper_kernel(width, member_ref, x_ref, *refs):
    stats, code_ref, (high, low, sums, code, head, sem) = refs[:-7], refs[-7], refs[-6:]
    h = len(stats)
    owned = x_ref.shape[0] // h
    for p in range(h):
        squares = stats[0][0:1, p * owned : (p + 1) * owned]
        for m in range(1, h):
            squares += stats[m][0:1, (p ^ m) * owned : ((p ^ m) + 1) * owned]
        factor = lax.rsqrt(squares / width + EPSILON)
        for j in range(0, owned, BLOCK):
            at = slice(p * owned + j, p * owned + j + BLOCK)
            high[at, :], low[at, :] = split(x_ref[at, :] * to_column(factor[:, j : j + BLOCK]))
    sums[...] = dot(member_ref[...], high[...]) + dot(member_ref[...], low[...])
    put_codes(sums, code, head)
    start(code, code_ref, sem).wait()


def both_kernel(own_ref, far_ref, code_ref, own, far, sums, code, head, sems):
    wait_all(start_all([own_ref, far_ref], [own, far], sems))
    rows = sums.shape[0]
    for j in range(rows // BLOCK):
        sums[j * BLOCK : (j + 1) * BLOCK, :] = get_codes(own, j, rows, BLOCK) + get_codes(far, j, rows, BLOCK)
    put_codes(sums, code, head)
    start(code, code_ref, sems.at[0]).wait()


def join_kernel(q_ref, *refs):
    h = (len(refs) - 4) // 2
    parts, (out_ref, out, sems, out_sems), held = refs[:h], refs[h : h + 4], refs[h + 4 :]
    rows, width = out.shape
    w = width // h
    wait_all(start_all(parts, held, sems))
    copies = []
    for j in range(rows // BLOCK):
        at = slice(j * BLOCK, (j + 1) * BLOCK)
        values = [get_codes(held[m], j, rows, BLOCK) for m in range(h)]
        square = sum(v * v for v in values)
        factor = lax.rsqrt(jnp.sum(square, axis=1, keepdims=True) / width + EPSILON)
        for m in range(h):
            out[at, chunk(q_ref[0] ^ m, w)] = values[m] * factor
        copies.append(start(out.at[at, :], out_ref.at[at, :], out_sems.at[j]))
    wait_all(copies)


def decode_kernel(q_ref, *refs):
    h = (len(refs) - 1) // 2
    codes, stats, out_ref = refs[:h], refs[h : 2 * h], refs[2 * h]
    rows, w = codes[0].shape
    width = h * w
    for j in range(rows // BLOCK):
        at = slice(j * BLOCK, (j + 1) * BLOCK)
        values = []
        for m in range(h):
            lanes = stats[m][1:2, m * rows + j * BLOCK : m * rows + (j + 1) * BLOCK]
            values.append(decode(codes[m][at, :], to_column(lanes)))
        square = sum(v * v for v in values)
        factor = lax.rsqrt(jnp.sum(square, axis=1, keepdims=True) / width + EPSILON)
        for m in range(h):
            out_ref[at, chunk(q_ref[0] ^ m, w)] = values[m] * factor


def call(kernel, out_shape, **kw):
    params = pltpu.CompilerParams(vmem_limit_bytes=VMEM_LIMIT)
    return pl.pallas_call(kernel, out_shape=out_shape, compiler_params=params, **kw)


def dma(*dims):
    return pltpu.SemaphoreType.DMA(dims) if dims else pltpu.SemaphoreType.DMA


def shards(points, point_cluster, cand_blocks, cent1_prev, parent, cent2_prev):
    point_rows, width = points.shape
    blocks = point_rows // BLOCK
    owned = cent1_prev.shape[0]
    upper_rows = cent2_prev.shape[0]
    n = lax.axis_size("cent")
    h = n // 2
    dp = lax.axis_index("dp")
    me = lax.axis_index("cent").astype(i32).reshape(1)
    q = me % h
    w = width // h
    chunks = w // BLOCK
    rows = h * owned

    def swap(value, mask):
        return lax.ppermute(value, "cent", [(i, i ^ mask) for i in range(n)])

    def swap_half(values):
        arrived = {m: swap(values[m], m) for m in range(h - 1, 0, -1)}
        return [values[0]] + [arrived[m] for m in range(1, h)]

    table = rms_norm(cent2_prev.astype(f32)).astype(bf16)
    table_units = lax.all_gather(table, "dp", axis=0, tiled=True)

    small = jnp.concatenate([point_cluster - dp * (n * owned), parent - dp * upper_rows]).reshape(-1, w)
    head = head_rows(point_rows + 2 * owned, w)
    prevs = call(
        prev_kernel,
        [shape((owned + head, w), i16)] * h,
        in_specs=[SMEM, HBM, VMEM],
        out_specs=[HBM] * h,
        scratch_shapes=[pltpu.VMEM((owned, width), f32), pltpu.VMEM((head, w), i32), dma(), dma(h)]
        + [pltpu.VMEM((owned + head, w), i16)] * h,
        name="prev",
    )(q, cent1_prev, small)
    prevs = swap_half(prevs)
    packed = call(
        functools.partial(pack_kernel, chunks),
        [shape((point_rows, BLOCK), bf16)] * (h * chunks),
        in_specs=[SMEM, HBM],
        out_specs=[HBM] * (h * chunks),
        scratch_shapes=[dma(h * chunks)],
        name="pack",
    )(q, points)
    arrived = [swap_half(packed[c::chunks]) for c in range(chunks)]

    member, place, near, far_count, prev, upper_member = call(
        functools.partial(prepare_kernel, blocks, n),
        [
            shape((h * point_rows, BLOCK), bf16),
            shape((h * blocks,), i32),
            shape((rows, BLOCK), f32),
            shape((rows // BLOCK, BLOCK), i32),
            shape((rows, w), f32),
            shape((upper_rows, rows), bf16),
        ],
        in_specs=[SMEM] + [VMEM] * h,
        out_specs=[VMEM, SMEM] + [VMEM] * 4,
        scratch_shapes=[pltpu.VMEM((2 * rows, BLOCK), f32)],
        name="prepare",
    )(me, *prevs)

    lines = rows + 2 * rows // BLOCK
    accs, crossed = [], []
    for c in range(chunks):
        acc, code = call(
            sums_kernel,
            [shape((2 * rows, BLOCK), f32), shape((lines, BLOCK), i16)],
            in_specs=[SMEM, VMEM, VMEM] + [HBM] * h,
            out_specs=[VMEM, HBM],
            scratch_shapes=[
                pltpu.VMEM((lines, BLOCK), i16),
                pltpu.VMEM((2 * rows // BLOCK, BLOCK), i32),
                dma(h + 1),
            ]
            + [pltpu.VMEM((point_rows, BLOCK), bf16)] * h,
            name=f"sums{c}",
        )(place, member, far_count, *arrived[c])
        accs.append(acc)
        crossed.append(swap(code, h))

    points, table_units = lax.optimization_barrier((points, table_units))
    unit_points = rms_norm(points.astype(f32)).astype(bf16)
    products = lax.dot_general(
        unit_points, table_units, (((1,), (1,)), ((), ())), preferred_element_type=f32
    )
    column_block = jnp.arange(table_units.shape[0]) // BLOCK
    listed = jnp.any(cand_blocks[:, :, None] == column_block[None, None, :], axis=1)
    weights = jnp.exp(products * (SHARPNESS / width)).reshape(blocks, BLOCK, -1)
    running = jnp.sum(weights * listed[:, None, :].astype(f32), axis=2).reshape(point_rows)
    point_score, near = lax.optimization_barrier((jnp.log(running), near))

    out = call(
        functools.partial(refresh_kernel, chunks, h),
        [shape((rows, w), f32), shape((2, rows), f32)] + [shape((owned, w), i16)] * h,
        in_specs=[VMEM] * (2 + chunks) + [HBM] * chunks,
        out_specs=[VMEM] + [HBM] * (h + 1),
        scratch_shapes=[pltpu.VMEM((owned, w), i16)] * h
        + [pltpu.VMEM((2, rows), f32), dma(chunks + h + 1)]
        + [pltpu.VMEM((lines, BLOCK), i16)] * chunks,
        name="refresh",
    )(near, prev, *accs, *crossed)
    x, stat = out[:2]
    stats = swap_half([stat] * h)
    back = swap_half(out[2:])

    upper_shape = shape((upper_rows + head_rows(upper_rows, w), w), i16)
    held_code = pltpu.VMEM(upper_shape.shape, i16)
    put = [pltpu.VMEM((upper_rows, w), f32), held_code, pltpu.VMEM((upper_shape.shape[0] - upper_rows, w), i32)]
    code = call(
        functools.partial(upper_kernel, width),
        upper_shape,
        in_specs=[VMEM] * (h + 2),
        out_specs=HBM,
        scratch_shapes=[pltpu.VMEM((rows, w), bf16), pltpu.VMEM((rows, w), bf16)] + put + [dma()],
        name="upper",
    )(upper_member, x, *stats)
    code = call(
        both_kernel,
        upper_shape,
        in_specs=[HBM, HBM],
        out_specs=HBM,
        scratch_shapes=[held_code, held_code] + put + [dma(2)],
        name="both",
    )(code, swap(code, h))
    parts = swap_half([code] * h)

    cent1_new = call(
        decode_kernel,
        shape((owned, width), f32),
        in_specs=[SMEM] + [VMEM] * (2 * h),
        out_specs=VMEM,
        name="decode",
    )(q, *back, *stats)
    q, cent1_new = lax.optimization_barrier((q, cent1_new))
    cent2_new = call(
        join_kernel,
        shape((upper_rows, width), f32),
        in_specs=[SMEM] + [HBM] * h,
        out_specs=HBM,
        scratch_shapes=[pltpu.VMEM((upper_rows, width), f32), dma(h), dma(upper_rows // BLOCK)] + [held_code] * h,
        name="join",
    )(q, *parts)
    return (cent1_new, cent2_new, point_score)


def solution(mesh):
    placed = (
        P(("dp", "cent"), None),
        P(("dp", "cent")),
        P(("dp", "cent"), None),
        P(("dp", "cent"), None),
        P(("dp", "cent")),
        P("dp", None),
    )
    return jax.shard_map(
        shards,
        mesh=mesh,
        in_specs=placed,
        out_specs=(P(("dp", "cent"), None), P("dp", None), P(("dp", "cent"))),
        check_vma=False,
    )
```

```python
import functools

import jax
import jax.numpy as jnp
from jax import lax
from jax.experimental import pallas as pl
from jax.experimental.pallas import tpu as pltpu
from jax.sharding import PartitionSpec as P

BLOCK = 128
EPSILON = 1e-06
SHARPNESS = 20.0
CODE = 32000.0
FLOOR = 1e-30
VMEM_LIMIT = 16 * 1024 * 1024
f32, bf16, i16, i32 = jnp.float32, jnp.bfloat16, jnp.int16, jnp.int32
shape = jax.ShapeDtypeStruct
VMEM = pl.BlockSpec(memory_space=pltpu.VMEM)
SMEM = pl.BlockSpec(memory_space=pltpu.SMEM)
HBM = pl.BlockSpec(memory_space=pltpu.HBM)


def rms_norm(values):
    return values * lax.rsqrt(jnp.mean(values * values, axis=-1, keepdims=True) + EPSILON)


def split(values):
    high = values.astype(bf16)
    return high, (values - high.astype(f32)).astype(bf16)


def dot(a, b):
    return jnp.dot(a, b, preferred_element_type=f32)


def dot_lanes(a, b):
    return lax.dot_general(a, b, (((1,), (1,)), ((), ())), preferred_element_type=f32)


def to_lanes(column):
    rows = column.shape[0]
    pick = jnp.where(lax.broadcasted_iota(i32, (8, BLOCK), 1) == 0, 1.0, 0.0).astype(bf16)
    return dot_lanes(pick, jnp.broadcast_to(column, (rows, BLOCK)).astype(bf16))[0:1]


def to_column(lanes):
    k = lanes.shape[1]
    eye = lax.broadcasted_iota(i32, (k, k), 0) == lax.broadcasted_iota(i32, (k, k), 1)
    return jnp.sum(jnp.where(eye, lanes, 0.0), axis=1, keepdims=True)


def exponent_of(top):
    return jnp.clip(jnp.ceil(jnp.log2(jnp.maximum(top * 1.001, FLOOR))), -100.0, 100.0)


def encode(values, exponent):
    return jnp.round(values * (CODE * jnp.exp2(-exponent))).astype(i16)


def decode(codes, exponent):
    return codes.astype(f32) * (jnp.exp2(exponent) * (1.0 / CODE))


def head_rows(count, w):
    return -(-count // (16 * w)) * 16


def chunk(index, size):
    return pl.ds(pl.multiple_of(index * size, size), size)


def start(source, target, sem):
    copy = pltpu.make_async_copy(source, target, sem)
    copy.start()
    return copy


def start_all(sources, targets, sems):
    return [start(a, b, sems.at[k]) for k, (a, b) in enumerate(zip(sources, targets))]


def wait_all(copies):
    for copy in copies:
        copy.wait()


def pack_kernel(chunks, q_ref, points_ref, *refs):
    outs, sems = refs[:-1], refs[-1]
    sources = [
        points_ref.at[:, chunk((q_ref[0] ^ (k // chunks)) * chunks + k % chunks, BLOCK)] for k in range(len(outs))
    ]
    wait_all(start_all(sources, outs, sems))


def prev_kernel(q_ref, prev_ref, small_ref, *refs):
    h = (len(refs) - 5) // 2
    outs, (next_ref, prev, head, sem, sems), held = refs[:h], refs[h : h + 5], refs[h + 5 :]
    next_ref[0] = q_ref[0]
    owned, width = prev.shape
    w = width // h
    copy = start(prev_ref, prev, sem)
    known = small_ref.shape[0]
    head[...] = jnp.zeros_like(head)
    head[0:known, :] = small_ref[...]
    copy.wait()
    exponent = exponent_of(jnp.max(jnp.abs(prev[...]), axis=1, keepdims=True))
    for j in range(owned // w):
        lanes = to_lanes(exponent[j * w : (j + 1) * w])
        head[known + j : known + j + 1, :] = lanes.astype(i32)
    copies = []
    for m in range(h):
        held[m][0:owned, :] = encode(prev[:, chunk(q_ref[0] ^ m, w)], exponent)
        held[m][owned:, :] = head[...].astype(i16)
        copies.append(start(held[m], outs[m], sems.at[m]))
    wait_all(copies)


def prepare_kernel(blocks, n, me_ref, *refs):
    arrived, (member_ref, place_ref, near_ref, far_ref, prev_ref, upper_ref, count) = refs[:-7], refs[-7:]
    h = len(arrived)
    rows, w = prev_ref.shape
    owned = rows // h
    upper_rows = upper_ref.shape[0]
    me = me_ref[0]
    lines, each = blocks * BLOCK // w, owned // w
    count[...] = jnp.zeros_like(count)
    centroid = lax.broadcasted_iota(i32, (BLOCK, BLOCK), 0)
    ones = jnp.ones((BLOCK, BLOCK), bf16)
    parent_at = lax.broadcasted_iota(i32, (upper_rows, w), 0)
    for m in range(h):
        head = arrived[m][owned:, :].astype(i32)
        for i in range(blocks):
            row, lane = i * BLOCK // w, i * BLOCK % w
            ids = head[row : row + 1, lane : lane + BLOCK]
            number = jnp.max(ids.astype(f32)).astype(i32) // BLOCK
            place = number ^ (me * (owned // BLOCK))
            place_ref[m * blocks + i] = place
            member = jnp.where(centroid == ids - number * BLOCK, 1.0, 0.0).astype(bf16)
            at = (m * blocks + i) * BLOCK
            member_ref[at : at + BLOCK, :] = member
            count[chunk(place, BLOCK), :] += dot(member, ones)
        for j in range(each):
            at = slice(m * owned + j * w, m * owned + (j + 1) * w)
            parents = head[lines + j : lines + j + 1, :]
            upper_ref[:, at] = jnp.where(parent_at == parents, 1.0, 0.0).astype(bf16)
            exponent = to_column(head[lines + each + j : lines + each + j + 1, :].astype(f32))
            prev_ref[at, :] = decode(arrived[m][j * w : (j + 1) * w, :], exponent)
    near_ref[...] = count[0:rows, :]
    for j in range(rows // BLOCK):
        far = count[rows + j * BLOCK : rows + (j + 1) * BLOCK, 0:1]
        high = jnp.floor(far / 64.0)
        far_ref[j : j + 1, :] = (to_lanes(high) * 64.0 + to_lanes(far - high * 64.0)).astype(i32)


def sums_kernel(place_ref, member_ref, far_count_ref, *refs):
    h = (len(refs) - 5) // 2
    points, (acc_ref, code_ref), (code, head, sem), held = (
        refs[:h],
        refs[h : h + 2],
        refs[h + 2 : h + 5],
        refs[h + 5 :],
    )
    rows = acc_ref.shape[0] // 2
    blocks = held[0].shape[0] // BLOCK
    copies = start_all(points, held, sem)
    acc_ref[...] = jnp.zeros_like(acc_ref)
    for m in range(h):
        copies[m].wait()
        for i in range(blocks):
            at, here = (m * blocks + i) * BLOCK, slice(i * BLOCK, (i + 1) * BLOCK)
            acc_ref[chunk(place_ref[m * blocks + i], BLOCK), :] += dot(member_ref[at : at + BLOCK, :], held[m][here, :])
    copies = []
    lines = rows // BLOCK
    step = 2 * BLOCK
    for j in range(rows // step):
        at = slice(j * step, (j + 1) * step)
        value = acc_ref[rows + j * step : rows + (j + 1) * step, :]
        exponent = exponent_of(jnp.max(jnp.abs(value), axis=1, keepdims=True))
        code[at, :] = encode(value, exponent)
        lanes = to_lanes(exponent).astype(i32)
        for k in range(step // BLOCK):
            row = j * (step // BLOCK) + k
            head[row : row + 1, :] = lanes[:, k * BLOCK : (k + 1) * BLOCK]
    head[lines:, :] = far_count_ref[...]
    code[rows:, :] = head[...].astype(i16)
    start(code, code_ref, sem.at[h]).wait()


def refresh_kernel(chunks, h, near_ref, prev_ref, *refs):
    accs, crossed, (x_ref, stat_ref), outs = (
        refs[:chunks],
        refs[chunks : 2 * chunks],
        refs[2 * chunks : 2 * chunks + 2],
        refs[2 * chunks + 2 : 2 * chunks + 2 + h],
    )
    codes, stat, sem, held = refs[2 * chunks + 2 + h :][:h], *refs[2 * chunks + 2 + 2 * h :][:2], refs[2 * chunks + 4 + 2 * h :]
    rows, w = x_ref.shape
    owned = rows // h
    lines = rows // BLOCK
    wait_all(start_all(crossed, held, sem))
    heads = [held[c][rows:, :].astype(i32).astype(f32) for c in range(chunks)]
    unit = jnp.ones((8, BLOCK), bf16)
    copies = []
    for j in range(lines):
        at = slice(j * BLOCK, (j + 1) * BLOCK)
        count = near_ref[at, :] + to_column(heads[0][lines + j : lines + j + 1, :])
        inverse = 1.0 / jnp.maximum(count, 1.0)
        square, top = None, None
        for c in range(chunks):
            lanes = slice(c * BLOCK, (c + 1) * BLOCK)
            far = decode(held[c][at, :], to_column(heads[c][j : j + 1, :]))
            x = (accs[c][at, :] + far) * inverse + prev_ref[at, lanes]
            x_ref[at, lanes] = x
            square = x * x if c == 0 else square + x * x
            top = jnp.abs(x) if c == 0 else jnp.maximum(top, jnp.abs(x))
        square_high, square_low = split(square)
        stat[0:1, at] = (dot_lanes(unit, square_high) + dot_lanes(unit, square_low))[0:1]
        exponent = exponent_of(jnp.max(top, axis=1, keepdims=True))
        stat[1:2, at] = to_lanes(exponent)
        m, here = j * BLOCK // owned, slice(j * BLOCK % owned, j * BLOCK % owned + BLOCK)
        codes[m][here, :] = encode(x_ref[at, :], exponent)
        if (j + 1) * BLOCK % owned == 0:
            copies.append(start(codes[m], outs[m], sem.at[chunks + m]))
    copies.append(start(stat, stat_ref, sem.at[chunks + h]))
    wait_all(copies)


def put_codes(values, code, head):
    rows, w = values.shape
    head[...] = jnp.zeros_like(head)
    for j in range(rows // w):
        at = slice(j * w, (j + 1) * w)
        exponent = exponent_of(jnp.max(jnp.abs(values[at, :]), axis=1, keepdims=True))
        code[at, :] = encode(values[at, :], exponent)
        head[j : j + 1, :] = to_lanes(exponent).astype(i32)
    code[rows:, :] = head[...].astype(i16)


def get_codes(code, j, rows, size):
    w = code.shape[1]
    row, lane = j * size // w, j * size % w
    lanes = code[rows : rows + 16, :].astype(i32).astype(f32)[row : row + 1, lane : lane + size]
    return decode(code[j * size : (j + 1) * size, :], to_column(lanes))


def upper_kernel(width, member_ref, x_ref, *refs):
    stats, code_ref, (high, low, sums, code, head, sem) = refs[:-7], refs[-7], refs[-6:]
    h = len(stats)
    owned = x_ref.shape[0] // h
    for p in range(h):
        squares = stats[0][0:1, p * owned : (p + 1) * owned]
        for m in range(1, h):
            squares += stats[m][0:1, (p ^ m) * owned : ((p ^ m) + 1) * owned]
        factor = lax.rsqrt(squares / width + EPSILON)
        for j in range(0, owned, BLOCK):
            at = slice(p * owned + j, p * owned + j + BLOCK)
            high[at, :], low[at, :] = split(x_ref[at, :] * to_column(factor[:, j : j + BLOCK]))
    sums[...] = dot(member_ref[...], high[...]) + dot(member_ref[...], low[...])
    put_codes(sums, code, head)
    start(code, code_ref, sem).wait()


def both_kernel(own_ref, far_ref, code_ref, own, far, sums, code, head, sems):
    wait_all(start_all([own_ref, far_ref], [own, far], sems))
    rows = sums.shape[0]
    for j in range(rows // BLOCK):
        sums[j * BLOCK : (j + 1) * BLOCK, :] = get_codes(own, j, rows, BLOCK) + get_codes(far, j, rows, BLOCK)
    put_codes(sums, code, head)
    start(code, code_ref, sems.at[0]).wait()


def join_kernel(q_ref, *refs):
    h = (len(refs) - 4) // 2
    parts, (out_ref, out, sems, out_sems), held = refs[:h], refs[h : h + 4], refs[h + 4 :]
    rows, width = out.shape
    w = width // h
    wait_all(start_all(parts, held, sems))
    copies = []
    for j in range(rows // BLOCK):
        at = slice(j * BLOCK, (j + 1) * BLOCK)
        values = [get_codes(held[m], j, rows, BLOCK) for m in range(h)]
        square = sum(v * v for v in values)
        factor = lax.rsqrt(jnp.sum(square, axis=1, keepdims=True) / width + EPSILON)
        for m in range(h):
            out[at, chunk(q_ref[0] ^ m, w)] = values[m] * factor
        copies.append(start(out.at[at, :], out_ref.at[at, :], out_sems.at[j]))
    wait_all(copies)


def decode_kernel(q_ref, *refs):
    h = (len(refs) - 1) // 2
    codes, stats, out_ref = refs[:h], refs[h : 2 * h], refs[2 * h]
    rows, w = codes[0].shape
    width = h * w
    for j in range(rows // BLOCK):
        at = slice(j * BLOCK, (j + 1) * BLOCK)
        values = []
        for m in range(h):
            lanes = stats[m][1:2, m * rows + j * BLOCK : m * rows + (j + 1) * BLOCK]
            values.append(decode(codes[m][at, :], to_column(lanes)))
        square = sum(v * v for v in values)
        factor = lax.rsqrt(jnp.sum(square, axis=1, keepdims=True) / width + EPSILON)
        for m in range(h):
            out_ref[at, chunk(q_ref[0] ^ m, w)] = values[m] * factor


def call(kernel, out_shape, **kw):
    params = pltpu.CompilerParams(vmem_limit_bytes=VMEM_LIMIT)
    return pl.pallas_call(kernel, out_shape=out_shape, compiler_params=params, **kw)


def dma(*dims):
    return pltpu.SemaphoreType.DMA(dims) if dims else pltpu.SemaphoreType.DMA


def shards(points, point_cluster, cand_blocks, cent1_prev, parent, cent2_prev):
    point_rows, width = points.shape
    blocks = point_rows // BLOCK
    owned = cent1_prev.shape[0]
    upper_rows = cent2_prev.shape[0]
    n = lax.axis_size("cent")
    h = n // 2
    dp = lax.axis_index("dp")
    me = lax.axis_index("cent").astype(i32).reshape(1)
    q = me & (h - 1)
    w = width // h
    chunks = w // BLOCK
    rows = h * owned

    def swap(value, mask):
        return lax.ppermute(value, "cent", [(i, i ^ mask) for i in range(n)])

    def swap_half(values):
        arrived = {m: swap(values[m], m) for m in range(h - 1, 0, -1)}
        return [values[0]] + [arrived[m] for m in range(1, h)]

    table_rows = lax.all_gather(cent2_prev, "dp", axis=0, tiled=True)

    small = jnp.concatenate([point_cluster - dp * (n * owned), parent - dp * upper_rows]).reshape(-1, w)
    head = head_rows(point_rows + 2 * owned, w)
    prevs = call(
        prev_kernel,
        [shape((owned + head, w), i16)] * h + [shape((1,), i32)],
        in_specs=[SMEM, HBM, VMEM],
        out_specs=[HBM] * h + [SMEM],
        scratch_shapes=[pltpu.VMEM((owned, width), f32), pltpu.VMEM((head, w), i32), dma(), dma(h)]
        + [pltpu.VMEM((owned + head, w), i16)] * h,
        name="prev",
    )(q, cent1_prev, small)
    prevs, after_prev = swap_half(prevs[:h]), prevs[h]
    packed = call(
        functools.partial(pack_kernel, chunks),
        [shape((point_rows, BLOCK), bf16)] * (h * chunks),
        in_specs=[SMEM, HBM],
        out_specs=[HBM] * (h * chunks),
        scratch_shapes=[dma(h * chunks)],
        name="pack",
    )(after_prev, points)
    arrived = [swap_half(packed[c::chunks]) for c in range(chunks)]

    member, place, near, far_count, prev, upper_member = call(
        functools.partial(prepare_kernel, blocks, n),
        [
            shape((h * point_rows, BLOCK), bf16),
            shape((h * blocks,), i32),
            shape((rows, BLOCK), f32),
            shape((rows // BLOCK, BLOCK), i32),
            shape((rows, w), f32),
            shape((upper_rows, rows), bf16),
        ],
        in_specs=[SMEM] + [VMEM] * h,
        out_specs=[VMEM, SMEM] + [VMEM] * 4,
        scratch_shapes=[pltpu.VMEM((2 * rows, BLOCK), f32)],
        name="prepare",
    )(me, *prevs)

    lines = rows + 2 * rows // BLOCK
    accs, crossed = [], []
    for c in range(chunks):
        acc, code = call(
            sums_kernel,
            [shape((2 * rows, BLOCK), f32), shape((lines, BLOCK), i16)],
            in_specs=[SMEM, VMEM, VMEM] + [HBM] * h,
            out_specs=[VMEM, HBM],
            scratch_shapes=[
                pltpu.VMEM((lines, BLOCK), i16),
                pltpu.VMEM((2 * rows // BLOCK, BLOCK), i32),
                dma(h + 1),
            ]
            + [pltpu.VMEM((point_rows, BLOCK), bf16)] * h,
            name=f"sums{c}",
        )(place, member, far_count, *arrived[c])
        accs.append(acc)
        crossed.append(swap(code, h))

    points, table_rows = lax.optimization_barrier((points, table_rows))
    unit_points = rms_norm(points.astype(f32)).astype(bf16)
    table_units = rms_norm(table_rows.astype(f32)).astype(bf16)
    products = lax.dot_general(
        unit_points, table_units, (((1,), (1,)), ((), ())), preferred_element_type=f32
    )
    column_block = jnp.arange(table_rows.shape[0]) // BLOCK
    listed = jnp.any(cand_blocks[:, :, None] == column_block[None, None, :], axis=1)
    weights = jnp.exp(products * (SHARPNESS / width)).reshape(blocks, BLOCK, -1)
    running = jnp.sum(weights * listed[:, None, :].astype(f32), axis=2).reshape(point_rows)
    point_score, near = lax.optimization_barrier((jnp.log(running), near))

    out = call(
        functools.partial(refresh_kernel, chunks, h),
        [shape((rows, w), f32), shape((2, rows), f32)] + [shape((owned, w), i16)] * h,
        in_specs=[VMEM] * (2 + chunks) + [HBM] * chunks,
        out_specs=[VMEM] + [HBM] * (h + 1),
        scratch_shapes=[pltpu.VMEM((owned, w), i16)] * h
        + [pltpu.VMEM((2, rows), f32), dma(chunks + h + 1)]
        + [pltpu.VMEM((lines, BLOCK), i16)] * chunks,
        name="refresh",
    )(near, prev, *accs, *crossed)
    x, stat = out[:2]
    stats = swap_half([stat] * h)
    back = swap_half(out[2:])

    upper_shape = shape((upper_rows + head_rows(upper_rows, w), w), i16)
    held_code = pltpu.VMEM(upper_shape.shape, i16)
    put = [pltpu.VMEM((upper_rows, w), f32), held_code, pltpu.VMEM((upper_shape.shape[0] - upper_rows, w), i32)]
    code = call(
        functools.partial(upper_kernel, width),
        upper_shape,
        in_specs=[VMEM] * (h + 2),
        out_specs=HBM,
        scratch_shapes=[pltpu.VMEM((rows, w), bf16), pltpu.VMEM((rows, w), bf16)] + put + [dma()],
        name="upper",
    )(upper_member, x, *stats)
    far_code = swap(code, h)
    code, back = lax.optimization_barrier((code, back))
    code = call(
        both_kernel,
        upper_shape,
        in_specs=[HBM, HBM],
        out_specs=HBM,
        scratch_shapes=[held_code, held_code] + put + [dma(2)],
        name="both",
    )(code, far_code)
    parts = swap_half([code] * h)

    cent1_new = call(
        decode_kernel,
        shape((owned, width), f32),
        in_specs=[SMEM] + [VMEM] * (2 * h),
        out_specs=VMEM,
        name="decode",
    )(q, *back, *stats)
    q, cent1_new = lax.optimization_barrier((q, cent1_new))
    cent2_new = call(
        join_kernel,
        shape((upper_rows, width), f32),
        in_specs=[SMEM] + [HBM] * h,
        out_specs=HBM,
        scratch_shapes=[pltpu.VMEM((upper_rows, width), f32), dma(h), dma(upper_rows // BLOCK)] + [held_code] * h,
        name="join",
    )(q, *parts)
    return (cent1_new, cent2_new, point_score)


def solution(mesh):
    placed = (
        P(("dp", "cent"), None),
        P(("dp", "cent")),
        P(("dp", "cent"), None),
        P(("dp", "cent"), None),
        P(("dp", "cent")),
        P("dp", None),
    )
    return jax.shard_map(
        shards,
        mesh=mesh,
        in_specs=placed,
        out_specs=(P(("dp", "cent"), None), P("dp", None), P(("dp", "cent"))),
        check_vma=False,
    )
```

```python
import functools

import jax
import jax.numpy as jnp
from jax import lax
from jax.experimental import pallas as pl
from jax.experimental.pallas import tpu as pltpu
from jax.sharding import PartitionSpec as P

BLOCK = 128
EPSILON = 1e-06
SHARPNESS = 20.0
CODE = 32000.0
FLOOR = 1e-30
VMEM_LIMIT = 16 * 1024 * 1024
PACK_LIMIT = 56 * 1024 * 1024
f32, bf16, i16, i32 = jnp.float32, jnp.bfloat16, jnp.int16, jnp.int32
shape = jax.ShapeDtypeStruct
VMEM = pl.BlockSpec(memory_space=pltpu.VMEM)
SMEM = pl.BlockSpec(memory_space=pltpu.SMEM)
HBM = pl.BlockSpec(memory_space=pltpu.HBM)


def rms_norm(values):
    return values * lax.rsqrt(jnp.mean(values * values, axis=-1, keepdims=True) + EPSILON)


def split(values):
    high = values.astype(bf16)
    return high, (values - high.astype(f32)).astype(bf16)


def dot(a, b):
    return jnp.dot(a, b, preferred_element_type=f32)


def dot_lanes(a, b):
    return lax.dot_general(a, b, (((1,), (1,)), ((), ())), preferred_element_type=f32)


def to_lanes(column):
    rows = column.shape[0]
    pick = jnp.where(lax.broadcasted_iota(i32, (8, BLOCK), 1) == 0, 1.0, 0.0).astype(bf16)
    return dot_lanes(pick, jnp.broadcast_to(column, (rows, BLOCK)).astype(bf16))[0:1]


def to_column(lanes):
    k = lanes.shape[1]
    eye = lax.broadcasted_iota(i32, (k, k), 0) == lax.broadcasted_iota(i32, (k, k), 1)
    return jnp.sum(jnp.where(eye, lanes, 0.0), axis=1, keepdims=True)


def exponent_of(top):
    return jnp.clip(jnp.ceil(jnp.log2(jnp.maximum(top * 1.001, FLOOR))), -100.0, 100.0)


def encode(values, exponent):
    return jnp.round(values * (CODE * jnp.exp2(-exponent))).astype(i16)


def decode(codes, exponent):
    return codes.astype(f32) * (jnp.exp2(exponent) * (1.0 / CODE))


def head_rows(count, w):
    return -(-count // (16 * w)) * 16


def chunk(index, size):
    return pl.ds(pl.multiple_of(index * size, size), size)


def start(source, target, sem):
    copy = pltpu.make_async_copy(source, target, sem)
    copy.start()
    return copy


def start_all(sources, targets, sems):
    return [start(a, b, sems.at[k]) for k, (a, b) in enumerate(zip(sources, targets))]


def wait_all(copies):
    for copy in copies:
        copy.wait()


def pack_kernel(chunks, me_ref, points_ref, cluster_ref, *refs):
    outs, (head, sems, head_sems) = refs[:-3], refs[-3:]
    rows = points_ref.shape[0]
    h = len(outs) // chunks
    q = me_ref[0] & (h - 1)
    sources = [points_ref.at[:, chunk((q ^ (k // chunks)) * chunks + k % chunks, BLOCK)] for k in range(len(outs))]
    copies = start_all(sources, [out.at[0:rows, :] for out in outs], sems)
    cluster = cluster_ref[...]
    head[...] = jnp.concatenate([cluster & (BLOCK - 1), (cluster - me_ref[1]) // BLOCK]).astype(f32).astype(bf16)
    copies += start_all([head] * h, [out.at[rows:, :] for out in outs[::chunks]], head_sems)
    wait_all(copies)


def prev_kernel(me_ref, after_ref, prev_ref, parent_ref, *refs):
    h = (len(refs) - 4) // 2
    outs, (prev, head, sem, sems), held = refs[:h], refs[h : h + 4], refs[h + 4 :]
    q = me_ref[0] & (h - 1)
    owned, width = prev.shape
    w = width // h
    copy = start(prev_ref, prev, sem)
    known = parent_ref.shape[0]
    head[...] = jnp.zeros_like(head)
    head[0:known, :] = parent_ref[...] - me_ref[2]
    copy.wait()
    exponent = exponent_of(jnp.max(jnp.abs(prev[...]), axis=1, keepdims=True))
    for j in range(owned // w):
        lanes = to_lanes(exponent[j * w : (j + 1) * w])
        head[known + j : known + j + 1, :] = lanes.astype(i32)
    copies = []
    for m in range(h):
        held[m][0:owned, :] = encode(prev[:, chunk(q ^ m, w)], exponent)
        held[m][owned:, :] = head[...].astype(i16)
        copies.append(start(held[m], outs[m], sems.at[m]))
    wait_all(copies)


def prepare_kernel(per, me_ref, *refs):
    arrived, (member_ref, place_ref, near_ref, far_ref, count, heads, sems) = refs[:-7], refs[-7:]
    h = len(arrived)
    rows = near_ref.shape[0]
    blocks = place_ref.shape[0] // h
    copies = start_all([a.at[blocks * BLOCK :, :] for a in arrived], [heads.at[m] for m in range(h)], sems)
    count[...] = jnp.zeros_like(count)
    centroid = lax.broadcasted_iota(i32, (BLOCK, BLOCK), 0)
    ones = jnp.ones((BLOCK, BLOCK), bf16)
    for m in range(h):
        copies[m].wait()
        head = heads[m].astype(f32)
        for i in range(blocks):
            number = jnp.max(head[blocks + i : blocks + i + 1, :]).astype(i32)
            place = number ^ (me_ref[0] * per)
            place_ref[m * blocks + i] = place
            member = jnp.where(centroid == head[i : i + 1, :].astype(i32), 1.0, 0.0).astype(bf16)
            at = (m * blocks + i) * BLOCK
            member_ref[at : at + BLOCK, :] = member
            count[chunk(place, BLOCK), :] += dot(member, ones)
    near_ref[...] = count[0:rows, :]
    for j in range(rows // BLOCK):
        far = count[rows + j * BLOCK : rows + (j + 1) * BLOCK, 0:1]
        high = jnp.floor(far / 64.0)
        far_ref[j : j + 1, :] = (to_lanes(high) * 64.0 + to_lanes(far - high * 64.0)).astype(i32)


def previous_kernel(*refs):
    arrived, (prev_ref, upper_ref) = refs[:-2], refs[-2:]
    h = len(arrived)
    rows, w = prev_ref.shape
    owned = rows // h
    each = owned // w
    parent_at = lax.broadcasted_iota(i32, (upper_ref.shape[0], w), 0)
    for m in range(h):
        head = arrived[m][owned:, :].astype(i32)
        for j in range(each):
            at = slice(m * owned + j * w, m * owned + (j + 1) * w)
            upper_ref[:, at] = jnp.where(parent_at == head[j : j + 1, :], 1.0, 0.0).astype(bf16)
            exponent = to_column(head[each + j : each + j + 1, :].astype(f32))
            prev_ref[at, :] = decode(arrived[m][j * w : (j + 1) * w, :], exponent)


def sums_kernel(place_ref, member_ref, far_count_ref, *refs):
    h = (len(refs) - 6) // 2
    points, (acc_ref, code_ref, after_ref), (code, head, sem), held = (
        refs[:h],
        refs[h : h + 3],
        refs[h + 3 : h + 6],
        refs[h + 6 :],
    )
    after_ref[0] = place_ref[0]
    rows = acc_ref.shape[0] // 2
    blocks = held[0].shape[0] // BLOCK
    copies = start_all([p.at[0 : blocks * BLOCK, :] for p in points], held, sem)
    acc_ref[...] = jnp.zeros_like(acc_ref)
    for m in range(h):
        copies[m].wait()
        for i in range(blocks):
            at, here = (m * blocks + i) * BLOCK, slice(i * BLOCK, (i + 1) * BLOCK)
            acc_ref[chunk(place_ref[m * blocks + i], BLOCK), :] += dot(member_ref[at : at + BLOCK, :], held[m][here, :])
    copies = []
    lines = rows // BLOCK
    step = 2 * BLOCK
    for j in range(rows // step):
        at = slice(j * step, (j + 1) * step)
        value = acc_ref[rows + j * step : rows + (j + 1) * step, :]
        exponent = exponent_of(jnp.max(jnp.abs(value), axis=1, keepdims=True))
        code[at, :] = encode(value, exponent)
        lanes = to_lanes(exponent).astype(i32)
        for k in range(step // BLOCK):
            row = j * (step // BLOCK) + k
            head[row : row + 1, :] = lanes[:, k * BLOCK : (k + 1) * BLOCK]
    head[lines:, :] = far_count_ref[...]
    code[rows:, :] = head[...].astype(i16)
    start(code, code_ref, sem.at[h]).wait()


def refresh_kernel(chunks, h, near_ref, prev_ref, *refs):
    accs, crossed, (x_ref, stat_ref), outs = (
        refs[:chunks],
        refs[chunks : 2 * chunks],
        refs[2 * chunks : 2 * chunks + 2],
        refs[2 * chunks + 2 : 2 * chunks + 2 + h],
    )
    codes, stat, sem, held = refs[2 * chunks + 2 + h :][:h], *refs[2 * chunks + 2 + 2 * h :][:2], refs[2 * chunks + 4 + 2 * h :]
    rows, w = x_ref.shape
    owned = rows // h
    lines = rows // BLOCK
    wait_all(start_all(crossed, held, sem))
    heads = [held[c][rows:, :].astype(i32).astype(f32) for c in range(chunks)]
    unit = jnp.ones((8, BLOCK), bf16)
    copies = []
    for j in range(lines):
        at = slice(j * BLOCK, (j + 1) * BLOCK)
        count = near_ref[at, :] + to_column(heads[0][lines + j : lines + j + 1, :])
        inverse = 1.0 / jnp.maximum(count, 1.0)
        square, top = None, None
        for c in range(chunks):
            lanes = slice(c * BLOCK, (c + 1) * BLOCK)
            far = decode(held[c][at, :], to_column(heads[c][j : j + 1, :]))
            x = (accs[c][at, :] + far) * inverse + prev_ref[at, lanes]
            x_ref[at, lanes] = x
            square = x * x if c == 0 else square + x * x
            top = jnp.abs(x) if c == 0 else jnp.maximum(top, jnp.abs(x))
        square_high, square_low = split(square)
        stat[0:1, at] = (dot_lanes(unit, square_high) + dot_lanes(unit, square_low))[0:1]
        exponent = exponent_of(jnp.max(top, axis=1, keepdims=True))
        stat[1:2, at] = to_lanes(exponent)
        m, here = j * BLOCK // owned, slice(j * BLOCK % owned, j * BLOCK % owned + BLOCK)
        codes[m][here, :] = encode(x_ref[at, :], exponent)
        if (j + 1) * BLOCK % owned == 0:
            copies.append(start(codes[m], outs[m], sem.at[chunks + m]))
    copies.append(start(stat, stat_ref, sem.at[chunks + h]))
    wait_all(copies)


def put_codes(values, code, head):
    rows, w = values.shape
    size = min(rows, w)
    head[...] = jnp.zeros_like(head)
    for j in range(rows // size):
        at = slice(j * size, (j + 1) * size)
        exponent = exponent_of(jnp.max(jnp.abs(values[at, :]), axis=1, keepdims=True))
        code[at, :] = encode(values[at, :], exponent)
        head[j : j + 1, 0:size] = to_lanes(exponent).astype(i32)
    code[rows:, :] = head[...].astype(i16)


def get_codes(code, j, rows, size):
    w = code.shape[1]
    row, lane = j * size // min(rows, w), j * size % min(rows, w)
    lanes = code[rows : rows + 16, :].astype(i32).astype(f32)[row : row + 1, lane : lane + size]
    return decode(code[j * size : (j + 1) * size, :], to_column(lanes))


def upper_kernel(width, member_ref, x_ref, *refs):
    stats, outs, (high, low, sums, sems), held = refs[:-10], refs[-10:-8], refs[-8:-4], refs[-4:]
    h = len(stats)
    owned = x_ref.shape[0] // h
    for p in range(h):
        squares = stats[0][0:1, p * owned : (p + 1) * owned]
        for m in range(1, h):
            squares += stats[m][0:1, (p ^ m) * owned : ((p ^ m) + 1) * owned]
        factor = lax.rsqrt(squares / width + EPSILON)
        for j in range(0, owned, BLOCK):
            at = slice(p * owned + j, p * owned + j + BLOCK)
            high[at, :], low[at, :] = split(x_ref[at, :] * to_column(factor[:, j : j + BLOCK]))
    rows = sums.shape[0]
    copies = []
    for k in range(2):
        member = member_ref[k * rows : (k + 1) * rows, :]
        sums[...] = dot(member, high[...]) + dot(member, low[...])
        put_codes(sums, held[k], held[2 + k])
        copies.append(start(held[k], outs[k], sems.at[k]))
    wait_all(copies)


def both_kernel(own_ref, far_ref, code_ref, own, far, sums, code, head, sems):
    wait_all(start_all([own_ref, far_ref], [own, far], sems))
    rows = sums.shape[0]
    for j in range(rows // BLOCK):
        sums[j * BLOCK : (j + 1) * BLOCK, :] = get_codes(own, j, rows, BLOCK) + get_codes(far, j, rows, BLOCK)
    put_codes(sums, code, head)
    start(code, code_ref, sems.at[0]).wait()


def join_kernel(first, me_ref, *refs):
    h = (len(refs) - 4) // 2
    parts, (out_ref, out, sems, out_sems), held = refs[:h], refs[-4 - h : -h], refs[-h:]
    q = me_ref[0] & (h - 1)
    rows, width = out.shape
    w = width // h
    wait_all(start_all(parts, held, sems))
    copies = []
    for j in range(rows // BLOCK):
        at = slice(j * BLOCK, (j + 1) * BLOCK)
        values = [get_codes(held[m], j, rows, BLOCK) for m in range(h)]
        square = sum(v * v for v in values)
        factor = lax.rsqrt(jnp.sum(square, axis=1, keepdims=True) / width + EPSILON)
        for m in range(h):
            out[at, chunk(q ^ m, w)] = values[m] * factor
        there = out_ref.at[first + j * BLOCK : first + (j + 1) * BLOCK, :]
        copies.append(start(out.at[at, :], there, out_sems.at[j]))
    wait_all(copies)


def decode_kernel(me_ref, *refs):
    h = (len(refs) - 1) // 2
    q = me_ref[0] & (h - 1)
    codes, stats, out_ref = refs[:h], refs[h : 2 * h], refs[2 * h]
    rows, w = codes[0].shape
    width = h * w
    for j in range(rows // BLOCK):
        at = slice(j * BLOCK, (j + 1) * BLOCK)
        values = []
        for m in range(h):
            lanes = stats[m][1:2, m * rows + j * BLOCK : m * rows + (j + 1) * BLOCK]
            values.append(decode(codes[m][at, :], to_column(lanes)))
        square = sum(v * v for v in values)
        factor = lax.rsqrt(jnp.sum(square, axis=1, keepdims=True) / width + EPSILON)
        for m in range(h):
            out_ref[at, chunk(q ^ m, w)] = values[m] * factor


def call(kernel, out_shape, limit=VMEM_LIMIT, **kw):
    params = pltpu.CompilerParams(vmem_limit_bytes=limit)
    return pl.pallas_call(kernel, out_shape=out_shape, compiler_params=params, **kw)


def dma(*dims):
    return pltpu.SemaphoreType.DMA(dims) if dims else pltpu.SemaphoreType.DMA


def shards(points, point_cluster, cand_blocks, cent1_prev, parent, cent2_prev):
    point_rows, width = points.shape
    blocks = point_rows // BLOCK
    owned = cent1_prev.shape[0]
    upper_rows = cent2_prev.shape[0]
    n = lax.axis_size("cent")
    h = n // 2
    dp = lax.axis_index("dp")
    w = width // h
    chunks = w // BLOCK
    rows = h * owned
    me = jnp.stack([lax.axis_index("cent").astype(i32), dp * (n * owned), dp * upper_rows])

    def swap(value, mask):
        return lax.ppermute(value, "cent", [(i, i ^ mask) for i in range(n)])

    def swap_half(values):
        arrived = {m: swap(values[m], m) for m in range(h - 1, 0, -1)}
        return [values[0]] + [arrived[m] for m in range(1, h)]

    table_rows = lax.all_gather(cent2_prev, "dp", axis=0, tiled=True)

    first_shape = shape((point_rows + 2 * blocks, BLOCK), bf16)
    packed = call(
        functools.partial(pack_kernel, chunks),
        ([first_shape] + [shape((point_rows, BLOCK), bf16)] * (chunks - 1)) * h,
        limit=PACK_LIMIT,
        in_specs=[SMEM, HBM, VMEM],
        out_specs=[HBM] * (h * chunks),
        scratch_shapes=[pltpu.VMEM((2 * blocks, BLOCK), bf16), dma(h * chunks), dma(h)],
        name="pack",
    )(me, points, point_cluster.reshape(blocks, BLOCK))
    arrived = [swap_half(packed[c::chunks]) for c in range(chunks)]

    member, place, near, far_count = call(
        functools.partial(prepare_kernel, owned // BLOCK),
        [
            shape((h * point_rows, BLOCK), bf16),
            shape((h * blocks,), i32),
            shape((rows, BLOCK), f32),
            shape((rows // BLOCK, BLOCK), i32),
        ],
        in_specs=[SMEM] + [HBM] * h,
        out_specs=[VMEM, SMEM] + [VMEM] * 2,
        scratch_shapes=[pltpu.VMEM((2 * rows, BLOCK), f32), pltpu.VMEM((h, 2 * blocks, BLOCK), bf16), dma(h)],
        name="prepare",
    )(me, *arrived[0])

    lines = rows + 2 * rows // BLOCK
    accs, crossed, after = [], [], None
    for c in range(chunks):
        acc, code, ended = call(
            sums_kernel,
            [shape((2 * rows, BLOCK), f32), shape((lines, BLOCK), i16), shape((1,), i32)],
            in_specs=[SMEM, VMEM, VMEM] + [HBM] * h,
            out_specs=[VMEM, HBM, SMEM],
            scratch_shapes=[
                pltpu.VMEM((lines, BLOCK), i16),
                pltpu.VMEM((2 * rows // BLOCK, BLOCK), i32),
                dma(h + 1),
            ]
            + [pltpu.VMEM((point_rows, BLOCK), bf16)] * h,
            name=f"sums{c}",
        )(place, member, far_count, *arrived[c])
        accs.append(acc)
        crossed.append(swap(code, h))
        after = ended

    head = head_rows(2 * owned, w)
    prevs = call(
        prev_kernel,
        [shape((owned + head, w), i16)] * h,
        in_specs=[SMEM, SMEM, HBM, VMEM],
        out_specs=[HBM] * h,
        scratch_shapes=[pltpu.VMEM((owned, width), f32), pltpu.VMEM((head, w), i32), dma(), dma(h)]
        + [pltpu.VMEM((owned + head, w), i16)] * h,
        name="prev",
    )(me, after, cent1_prev, parent.reshape(owned // w, w))
    prev, upper_member = call(
        previous_kernel,
        [shape((rows, w), f32), shape((upper_rows, rows), bf16)],
        in_specs=[VMEM] * h,
        out_specs=[VMEM] * 2,
        name="previous",
    )(*swap_half(prevs))

    points, table_rows = lax.optimization_barrier((points, table_rows))
    unit_points = rms_norm(points.astype(f32)).astype(bf16)
    table_units = rms_norm(table_rows.astype(f32)).astype(bf16)
    products = lax.dot_general(
        unit_points, table_units, (((1,), (1,)), ((), ())), preferred_element_type=f32
    )
    column_block = jnp.arange(table_rows.shape[0]) // BLOCK
    listed = jnp.any(cand_blocks[:, :, None] == column_block[None, None, :], axis=1)
    weights = jnp.exp(products * (SHARPNESS / width)).reshape(blocks, BLOCK, -1)
    running = jnp.sum(weights * listed[:, None, :].astype(f32), axis=2).reshape(point_rows)
    point_score, near = lax.optimization_barrier((jnp.log(running), near))

    out = call(
        functools.partial(refresh_kernel, chunks, h),
        [shape((rows, w), f32), shape((2, rows), f32)] + [shape((owned, w), i16)] * h,
        in_specs=[VMEM] * (2 + chunks) + [HBM] * chunks,
        out_specs=[VMEM] + [HBM] * (h + 1),
        scratch_shapes=[pltpu.VMEM((owned, w), i16)] * h
        + [pltpu.VMEM((2, rows), f32), dma(chunks + h + 1)]
        + [pltpu.VMEM((lines, BLOCK), i16)] * chunks,
        name="refresh",
    )(near, prev, *accs, *crossed)
    x, stat = out[:2]
    stats = swap_half([stat] * h)
    back = swap_half(out[2:])

    part = upper_rows // 2
    tail = head_rows(part, w)
    code_shape = shape((part + tail, w), i16)
    held_code, held_head = pltpu.VMEM(code_shape.shape, i16), pltpu.VMEM((tail, w), i32)
    codes = call(
        functools.partial(upper_kernel, width),
        [code_shape] * 2,
        in_specs=[VMEM] * (h + 2),
        out_specs=[HBM] * 2,
        scratch_shapes=[pltpu.VMEM((rows, w), bf16), pltpu.VMEM((rows, w), bf16), pltpu.VMEM((part, w), f32), dma(2)]
        + [held_code] * 2
        + [held_head] * 2,
        name="upper",
    )(upper_member, x, *stats)
    far_codes = [swap(code, h) for code in codes]
    parts = []
    for k in range(2):
        code = codes[k]
        if k == 0:
            code, back = lax.optimization_barrier((code, back))
        code = call(
            both_kernel,
            code_shape,
            in_specs=[HBM, HBM],
            out_specs=HBM,
            scratch_shapes=[held_code, held_code, pltpu.VMEM((part, w), f32), held_code, held_head, dma(2)],
            name=f"both{k}",
        )(code, far_codes[k])
        parts.append(swap_half([code] * h))

    cent1_new = call(
        decode_kernel,
        shape((owned, width), f32),
        in_specs=[SMEM] + [VMEM] * (2 * h),
        out_specs=VMEM,
        name="decode",
    )(me, *back, *stats)
    cent2_new = []
    for k in range(2):
        last = me
        if k == 1:
            last, cent1_new = lax.optimization_barrier((me, cent1_new))
        cent2_new = [
            call(
                functools.partial(join_kernel, k * part),
                shape((upper_rows, width), f32),
                in_specs=[SMEM] + [HBM] * (h + k),
                out_specs=HBM,
                scratch_shapes=[pltpu.VMEM((part, width), f32), dma(h), dma(part // BLOCK)] + [held_code] * h,
                input_output_aliases={h + 1: 0} if k else {},
                name=f"join{k}",
            )(last, *parts[k], *cent2_new)
        ]
    return (cent1_new, cent2_new[0], point_score)


def solution(mesh):
    placed = (
        P(("dp", "cent"), None),
        P(("dp", "cent")),
        P(("dp", "cent"), None),
        P(("dp", "cent"), None),
        P(("dp", "cent")),
        P("dp", None),
    )
    return jax.shard_map(
        shards,
        mesh=mesh,
        in_specs=placed,
        out_specs=(P(("dp", "cent"), None), P("dp", None), P(("dp", "cent"))),
        check_vma=False,
    )
```

```python
import functools

import jax
import jax.numpy as jnp
from jax import lax
from jax.experimental import pallas as pl
from jax.experimental.pallas import tpu as pltpu
from jax.sharding import PartitionSpec as P

BLOCK = 128
EPSILON = 1e-06
SHARPNESS = 20.0
CODE = 32000.0
FLOOR = 1e-30
VMEM_LIMIT = 16 * 1024 * 1024
f32, bf16, i16, i32 = jnp.float32, jnp.bfloat16, jnp.int16, jnp.int32
shape = jax.ShapeDtypeStruct
VMEM = pl.BlockSpec(memory_space=pltpu.VMEM)
SMEM = pl.BlockSpec(memory_space=pltpu.SMEM)
HBM = pl.BlockSpec(memory_space=pltpu.HBM)


def rms_norm(values):
    return values * lax.rsqrt(jnp.mean(values * values, axis=-1, keepdims=True) + EPSILON)


def split(values):
    high = values.astype(bf16)
    return high, (values - high.astype(f32)).astype(bf16)


def dot(a, b):
    return jnp.dot(a, b, preferred_element_type=f32)


def dot_lanes(a, b):
    return lax.dot_general(a, b, (((1,), (1,)), ((), ())), preferred_element_type=f32)


def to_lanes(column):
    rows = column.shape[0]
    pick = jnp.where(lax.broadcasted_iota(i32, (8, BLOCK), 1) == 0, 1.0, 0.0).astype(bf16)
    return dot_lanes(pick, jnp.broadcast_to(column, (rows, BLOCK)).astype(bf16))[0:1]


def to_column(lanes):
    k = lanes.shape[1]
    eye = lax.broadcasted_iota(i32, (k, k), 0) == lax.broadcasted_iota(i32, (k, k), 1)
    return jnp.sum(jnp.where(eye, lanes, 0.0), axis=1, keepdims=True)


def exponent_of(top):
    return jnp.clip(jnp.ceil(jnp.log2(jnp.maximum(top * 1.001, FLOOR))), -100.0, 100.0)


def encode(values, exponent):
    return jnp.round(values * (CODE * jnp.exp2(-exponent))).astype(i16)


def decode(codes, exponent):
    return codes.astype(f32) * (jnp.exp2(exponent) * (1.0 / CODE))


def head_rows(count, w):
    return -(-count // (16 * w)) * 16


def chunk(index, size):
    return pl.ds(pl.multiple_of(index * size, size), size)


def start(source, target, sem):
    copy = pltpu.make_async_copy(source, target, sem)
    copy.start()
    return copy


def start_all(sources, targets, sems):
    return [start(a, b, sems.at[k]) for k, (a, b) in enumerate(zip(sources, targets))]


def wait_all(copies):
    for copy in copies:
        copy.wait()


def pack_kernel(chunks, me_ref, points_ref, cluster_ref, *refs):
    outs, (after_ref, head, sems, head_sems) = refs[:-4], refs[-4:]
    after_ref[0] = me_ref[0]
    rows = points_ref.shape[0]
    h = len(outs) // chunks
    q = me_ref[0] & (h - 1)
    sources = [points_ref.at[:, chunk((q ^ (k // chunks)) * chunks + k % chunks, BLOCK)] for k in range(len(outs))]
    copies = start_all(sources, [out.at[0:rows, :] for out in outs], sems)
    cluster = cluster_ref[...]
    head[...] = jnp.concatenate([cluster & (BLOCK - 1), (cluster - me_ref[1]) // BLOCK]).astype(f32).astype(bf16)
    copies += start_all([head] * h, [out.at[rows:, :] for out in outs[::chunks]], head_sems)
    wait_all(copies)


def prev_kernel(me_ref, after_ref, prev_ref, parent_ref, *refs):
    h = (len(refs) - 4) // 2
    outs, (prev, head, sem, sems), held = refs[:h], refs[h : h + 4], refs[h + 4 :]
    q = me_ref[0] & (h - 1)
    owned, width = prev.shape
    w = width // h
    copy = start(prev_ref, prev, sem)
    known = parent_ref.shape[0]
    head[...] = jnp.zeros_like(head)
    head[0:known, :] = parent_ref[...] - me_ref[2]
    copy.wait()
    exponent = exponent_of(jnp.max(jnp.abs(prev[...]), axis=1, keepdims=True))
    for j in range(owned // w):
        lanes = to_lanes(exponent[j * w : (j + 1) * w])
        head[known + j : known + j + 1, :] = lanes.astype(i32)
    copies = []
    for m in range(h):
        held[m][0:owned, :] = encode(prev[:, chunk(q ^ m, w)], exponent)
        held[m][owned:, :] = head[...].astype(i16)
        copies.append(start(held[m], outs[m], sems.at[m]))
    wait_all(copies)


def prepare_kernel(per, me_ref, *refs):
    arrived, (member_ref, place_ref, near_ref, far_ref, count, heads, sems) = refs[:-7], refs[-7:]
    h = len(arrived)
    rows = near_ref.shape[0]
    blocks = place_ref.shape[0] // h
    copies = start_all([a.at[blocks * BLOCK :, :] for a in arrived], [heads.at[m] for m in range(h)], sems)
    count[...] = jnp.zeros_like(count)
    centroid = lax.broadcasted_iota(i32, (BLOCK, BLOCK), 0)
    ones = jnp.ones((BLOCK, BLOCK), bf16)
    for m in range(h):
        copies[m].wait()
        head = heads[m].astype(f32)
        for i in range(blocks):
            number = jnp.max(head[blocks + i : blocks + i + 1, :]).astype(i32)
            place = number ^ (me_ref[0] * per)
            place_ref[m * blocks + i] = place
            member = jnp.where(centroid == head[i : i + 1, :].astype(i32), 1.0, 0.0).astype(bf16)
            at = (m * blocks + i) * BLOCK
            member_ref[at : at + BLOCK, :] = member
            count[chunk(place, BLOCK), :] += dot(member, ones)
    near_ref[...] = count[0:rows, :]
    for j in range(rows // BLOCK):
        far = count[rows + j * BLOCK : rows + (j + 1) * BLOCK, 0:1]
        high = jnp.floor(far / 64.0)
        far_ref[j : j + 1, :] = (to_lanes(high) * 64.0 + to_lanes(far - high * 64.0)).astype(i32)


def previous_kernel(*refs):
    arrived, (prev_ref, upper_ref) = refs[:-2], refs[-2:]
    h = len(arrived)
    rows, w = prev_ref.shape
    owned = rows // h
    each = owned // w
    parent_at = lax.broadcasted_iota(i32, (upper_ref.shape[0], w), 0)
    for m in range(h):
        head = arrived[m][owned:, :].astype(i32)
        for j in range(each):
            at = slice(m * owned + j * w, m * owned + (j + 1) * w)
            upper_ref[:, at] = jnp.where(parent_at == head[j : j + 1, :], 1.0, 0.0).astype(bf16)
            exponent = to_column(head[each + j : each + j + 1, :].astype(f32))
            prev_ref[at, :] = decode(arrived[m][j * w : (j + 1) * w, :], exponent)


def sums_kernel(place_ref, before_ref, member_ref, far_count_ref, *refs):
    h = (len(refs) - 5) // 2
    points, (acc_ref, code, after_ref, head, sem), held = refs[:h], refs[h : h + 5], refs[h + 5 :]
    after_ref[0] = before_ref[0]
    rows = acc_ref.shape[0] // 2
    blocks = held[0].shape[0] // BLOCK
    copies = start_all([p.at[0 : blocks * BLOCK, :] for p in points], held, sem)
    acc_ref[...] = jnp.zeros_like(acc_ref)
    for m in range(h):
        copies[m].wait()
        for i in range(blocks):
            at, here = (m * blocks + i) * BLOCK, slice(i * BLOCK, (i + 1) * BLOCK)
            acc_ref[chunk(place_ref[m * blocks + i], BLOCK), :] += dot(member_ref[at : at + BLOCK, :], held[m][here, :])
    lines = rows // BLOCK
    step = 2 * BLOCK
    for j in range(rows // step):
        at = slice(j * step, (j + 1) * step)
        value = acc_ref[rows + j * step : rows + (j + 1) * step, :]
        exponent = exponent_of(jnp.max(jnp.abs(value), axis=1, keepdims=True))
        code[at, :] = encode(value, exponent)
        lanes = to_lanes(exponent).astype(i32)
        for k in range(step // BLOCK):
            row = j * (step // BLOCK) + k
            head[row : row + 1, :] = lanes[:, k * BLOCK : (k + 1) * BLOCK]
    head[lines:, :] = far_count_ref[...]
    code[rows:, :] = head[...].astype(i16)


def spot(index, w):
    return slice(index * BLOCK // w, index * BLOCK // w + 1), slice(index * BLOCK % w, index * BLOCK % w + BLOCK)


def refresh_kernel(chunks, near_ref, prev_ref, *refs):
    accs, crossed, x_ref, outs, tail = refs[:chunks], refs[chunks : 2 * chunks], refs[2 * chunks], refs[2 * chunks + 1 : -1], refs[-1]
    h = len(outs)
    rows, w = x_ref.shape
    owned = rows // h
    lines = rows // BLOCK
    heads = [crossed[c][rows:, :].astype(i32).astype(f32) for c in range(chunks)]
    unit = jnp.ones((8, BLOCK), bf16)
    for j in range(lines):
        at = slice(j * BLOCK, (j + 1) * BLOCK)
        count = near_ref[at, :] + to_column(heads[0][lines + j : lines + j + 1, :])
        inverse = 1.0 / jnp.maximum(count, 1.0)
        square, top = None, None
        for c in range(chunks):
            lanes = slice(c * BLOCK, (c + 1) * BLOCK)
            far = decode(crossed[c][at, :], to_column(heads[c][j : j + 1, :]))
            x = (accs[c][at, :] + far) * inverse + prev_ref[at, lanes]
            x_ref[at, lanes] = x
            square = x * x if c == 0 else square + x * x
            top = jnp.abs(x) if c == 0 else jnp.maximum(top, jnp.abs(x))
        square_high, square_low = split(square)
        sums = (dot_lanes(unit, square_high) + dot_lanes(unit, square_low))[0:1]
        sums_exponent = exponent_of(sums)
        scaled = sums * (16384.0 * jnp.exp2(-sums_exponent))
        whole = jnp.floor(scaled)
        exponent = exponent_of(jnp.max(top, axis=1, keepdims=True))
        for k, value in enumerate((sums_exponent, whole, jnp.floor((scaled - whole) * 16384.0), to_lanes(exponent))):
            tail[spot(k * lines + j, w)] = value.astype(i32)
        here = slice(j * BLOCK % owned, j * BLOCK % owned + BLOCK)
        outs[j * BLOCK // owned][here, :] = encode(x_ref[at, :], exponent)
    for out in outs:
        out[owned:, :] = tail[...].astype(i16)


def put_codes(values, code, head):
    rows, w = values.shape
    size = min(rows, w)
    head[...] = jnp.zeros_like(head)
    for j in range(rows // size):
        at = slice(j * size, (j + 1) * size)
        exponent = exponent_of(jnp.max(jnp.abs(values[at, :]), axis=1, keepdims=True))
        code[at, :] = encode(values[at, :], exponent)
        head[j : j + 1, 0:size] = to_lanes(exponent).astype(i32)
    code[rows:, :] = head[...].astype(i16)


def get_codes(code, j, rows, size):
    w = code.shape[1]
    row, lane = j * size // min(rows, w), j * size % min(rows, w)
    lanes = code[rows : rows + 16, :].astype(i32).astype(f32)[row : row + 1, lane : lane + size]
    return decode(code[j * size : (j + 1) * size, :], to_column(lanes))


def upper_kernel(width, member_ref, x_ref, *refs):
    backs, outs, (high, low, sums), heads = refs[:-7], refs[-7:-5], refs[-5:-2], refs[-2:]
    h = len(backs)
    total, w = x_ref.shape
    owned = total // h
    lines, per = total // BLOCK, owned // BLOCK
    tails = [back[owned:, :].astype(i32).astype(f32) for back in backs]
    for p in range(h):
        for j in range(per):
            squares = None
            for m in range(h):
                index = (p ^ m) * per + j
                exponent, whole, rest = (tails[m][spot(k * lines + index, w)] for k in range(3))
                value = (whole + rest * (1.0 / 16384.0)) * (jnp.exp2(exponent) * (1.0 / 16384.0))
                squares = value if m == 0 else squares + value
            factor = lax.rsqrt(squares / width + EPSILON)
            at = slice(p * owned + j * BLOCK, p * owned + (j + 1) * BLOCK)
            high[at, :], low[at, :] = split(x_ref[at, :] * to_column(factor))
    rows = sums.shape[0]
    for k in range(2):
        member = member_ref[k * rows : (k + 1) * rows, :]
        sums[...] = dot(member, high[...]) + dot(member, low[...])
        put_codes(sums, outs[k], heads[k])


def both_kernel(own, far, code_ref, sums, head):
    rows = sums.shape[0]
    for j in range(rows // BLOCK):
        sums[j * BLOCK : (j + 1) * BLOCK, :] = get_codes(own, j, rows, BLOCK) + get_codes(far, j, rows, BLOCK)
    put_codes(sums, code_ref, head)


def join_kernel(me_ref, *refs):
    parts, (out_ref, out, out_sems) = refs[:-3], refs[-3:]
    h = len(parts) // 2
    q = me_ref[0] & (h - 1)
    total, width = out.shape
    rows = total // 2
    w = width // h
    copies = []
    for j in range(total // BLOCK):
        at, k = slice(j * BLOCK, (j + 1) * BLOCK), j * BLOCK // rows
        values = [get_codes(parts[k * h + m], j - k * (rows // BLOCK), rows, BLOCK) for m in range(h)]
        square = sum(v * v for v in values)
        factor = lax.rsqrt(jnp.sum(square, axis=1, keepdims=True) / width + EPSILON)
        for m in range(h):
            out[at, chunk(q ^ m, w)] = values[m] * factor
        copies.append(start(out.at[at, :], out_ref.at[at, :], out_sems.at[j]))
    wait_all(copies)


def decode_kernel(me_ref, *refs):
    codes, out_ref = refs[:-1], refs[-1]
    h = len(codes)
    q = me_ref[0] & (h - 1)
    rows, width = out_ref.shape
    w = width // h
    lines, per = h * rows // BLOCK, rows // BLOCK
    tails = [code[rows:, :].astype(i32).astype(f32) for code in codes]
    for j in range(per):
        at = slice(j * BLOCK, (j + 1) * BLOCK)
        values = []
        for m in range(h):
            exponent = tails[m][spot(3 * lines + m * per + j, w)]
            values.append(decode(codes[m][at, :], to_column(exponent)))
        square = sum(v * v for v in values)
        factor = lax.rsqrt(jnp.sum(square, axis=1, keepdims=True) / width + EPSILON)
        for m in range(h):
            out_ref[at, chunk(q ^ m, w)] = values[m] * factor


def call(kernel, out_shape, **kw):
    params = pltpu.CompilerParams(vmem_limit_bytes=VMEM_LIMIT)
    return pl.pallas_call(kernel, out_shape=out_shape, compiler_params=params, **kw)


def dma(*dims):
    return pltpu.SemaphoreType.DMA(dims) if dims else pltpu.SemaphoreType.DMA


def shards(points, point_cluster, cand_blocks, cent1_prev, parent, cent2_prev):
    point_rows, width = points.shape
    blocks = point_rows // BLOCK
    owned = cent1_prev.shape[0]
    upper_rows = cent2_prev.shape[0]
    n = lax.axis_size("cent")
    h = n // 2
    dp = lax.axis_index("dp")
    w = width // h
    chunks = w // BLOCK
    rows = h * owned
    me = jnp.stack([lax.axis_index("cent").astype(i32), dp * (n * owned), dp * upper_rows])

    def swap(value, mask):
        return lax.ppermute(value, "cent", [(i, i ^ mask) for i in range(n)])

    def swap_half(values):
        arrived = {m: swap(values[m], m) for m in range(h - 1, 0, -1)}
        return [values[0]] + [arrived[m] for m in range(1, h)]

    table_rows = lax.all_gather(cent2_prev, "dp", axis=0, tiled=True)

    first_shape = shape((point_rows + 2 * blocks, BLOCK), bf16)
    *packed, after_pack = call(
        functools.partial(pack_kernel, chunks),
        ([first_shape] + [shape((point_rows, BLOCK), bf16)] * (chunks - 1)) * h + [shape((1,), i32)],
        in_specs=[SMEM, HBM, VMEM],
        out_specs=[HBM] * (h * chunks) + [SMEM],
        scratch_shapes=[pltpu.VMEM((2 * blocks, BLOCK), bf16), dma(h * chunks), dma(h)],
        name="pack",
    )(me, points, point_cluster.reshape(blocks, BLOCK))
    arrived = [swap_half(packed[c::chunks]) for c in range(chunks)]

    member, place, near, far_count = call(
        functools.partial(prepare_kernel, owned // BLOCK),
        [
            shape((h * point_rows, BLOCK), bf16),
            shape((h * blocks,), i32),
            shape((rows, BLOCK), f32),
            shape((rows // BLOCK, BLOCK), i32),
        ],
        in_specs=[SMEM] + [HBM] * h,
        out_specs=[VMEM, SMEM] + [VMEM] * 2,
        scratch_shapes=[pltpu.VMEM((2 * rows, BLOCK), f32), pltpu.VMEM((h, 2 * blocks, BLOCK), bf16), dma(h)],
        name="prepare",
    )(me, *arrived[0])

    lines = rows + 2 * rows // BLOCK
    accs, crossed, after = [], [], place
    for c in range(chunks):
        acc, code, ended = call(
            sums_kernel,
            [shape((2 * rows, BLOCK), f32), shape((lines, BLOCK), i16), shape((1,), i32)],
            in_specs=[SMEM, SMEM, VMEM, VMEM] + [HBM] * h,
            out_specs=[VMEM, VMEM, SMEM],
            scratch_shapes=[pltpu.VMEM((2 * rows // BLOCK, BLOCK), i32), dma(h)]
            + [pltpu.VMEM((point_rows, BLOCK), bf16)] * h,
            name=f"sums{c}",
        )(place, after, member, far_count, *arrived[c])
        accs.append(acc)
        crossed.append(swap(code, h))
        after = ended

    head = head_rows(2 * owned, w)
    prevs = call(
        prev_kernel,
        [shape((owned + head, w), i16)] * h,
        in_specs=[SMEM, SMEM, HBM, VMEM],
        out_specs=[HBM] * h,
        scratch_shapes=[pltpu.VMEM((owned, width), f32), pltpu.VMEM((head, w), i32), dma(), dma(h)]
        + [pltpu.VMEM((owned + head, w), i16)] * h,
        name="prev",
    )(me, after_pack, cent1_prev, parent.reshape(owned // w, w))
    prev, upper_member = call(
        previous_kernel,
        [shape((rows, w), f32), shape((upper_rows, rows), bf16)],
        in_specs=[VMEM] * h,
        out_specs=[VMEM] * 2,
        name="previous",
    )(*swap_half(prevs))

    points, table_rows = lax.optimization_barrier((points, table_rows))
    unit_points = rms_norm(points.astype(f32)).astype(bf16)
    table_scale = lax.rsqrt(jnp.mean(jnp.square(table_rows.astype(f32)), axis=-1) + EPSILON)
    table_scale, near = lax.optimization_barrier((table_scale, near))
    table_units = (table_rows.astype(f32) * table_scale[:, None]).astype(bf16)
    products = lax.dot_general(
        unit_points, table_units, (((1,), (1,)), ((), ())), preferred_element_type=f32
    )
    column_block = jnp.arange(table_rows.shape[0]) // BLOCK
    listed = jnp.any(cand_blocks[:, :, None] == column_block[None, None, :], axis=1)
    weights = jnp.exp(products * (SHARPNESS / width)).reshape(blocks, BLOCK, -1)
    running = jnp.sum(weights * listed[:, None, :].astype(f32), axis=2).reshape(point_rows)
    point_score = jnp.log(running)

    tail = 4 * rows // w
    x, *backs = call(
        functools.partial(refresh_kernel, chunks),
        [shape((rows, w), f32)] + [shape((owned + tail, w), i16)] * h,
        in_specs=[VMEM] * (2 + 2 * chunks),
        out_specs=[VMEM] * (h + 1),
        scratch_shapes=[pltpu.VMEM((tail, w), i32)],
        name="refresh",
    )(near, prev, *accs, *crossed)
    backs = swap_half(backs)

    part = upper_rows // 2
    tail = head_rows(part, w)
    code_shape = shape((part + tail, w), i16)
    held_head = pltpu.VMEM((tail, w), i32)
    codes = call(
        functools.partial(upper_kernel, width),
        [code_shape] * 2,
        in_specs=[VMEM] * (h + 2),
        out_specs=[VMEM] * 2,
        scratch_shapes=[pltpu.VMEM((rows, w), bf16), pltpu.VMEM((rows, w), bf16), pltpu.VMEM((part, w), f32)]
        + [held_head] * 2,
        name="upper",
    )(upper_member, x, *backs)
    far_codes = [swap(code, h) for code in codes]
    parts = []
    for k in range(2):
        code = codes[k]
        if k == 0:
            code, point_score = lax.optimization_barrier((code, point_score))
        code = call(
            both_kernel,
            code_shape,
            in_specs=[VMEM, VMEM],
            out_specs=VMEM,
            scratch_shapes=[pltpu.VMEM((part, w), f32), held_head],
            name=f"both{k}",
        )(code, far_codes[k])
        parts += swap_half([code] * h)

    cent1_new = call(
        decode_kernel,
        shape((owned, width), f32),
        in_specs=[SMEM] + [VMEM] * h,
        out_specs=VMEM,
        name="decode",
    )(me, *backs)
    last, cent1_new = lax.optimization_barrier((me, cent1_new))
    cent2_new = call(
        join_kernel,
        shape((upper_rows, width), f32),
        in_specs=[SMEM] + [VMEM] * (2 * h),
        out_specs=HBM,
        scratch_shapes=[pltpu.VMEM((upper_rows, width), f32), dma(upper_rows // BLOCK)],
        name="join",
    )(last, *parts)
    return (cent1_new, cent2_new, point_score)


def solution(mesh):
    placed = (
        P(("dp", "cent"), None),
        P(("dp", "cent")),
        P(("dp", "cent"), None),
        P(("dp", "cent"), None),
        P(("dp", "cent")),
        P("dp", None),
    )
    return jax.shard_map(
        shards,
        mesh=mesh,
        in_specs=placed,
        out_specs=(P(("dp", "cent"), None), P("dp", None), P(("dp", "cent"))),
        check_vma=False,
    )
```

```python
import functools

import jax
import jax.numpy as jnp
from jax import lax
from jax.experimental import pallas as pl
from jax.experimental.pallas import tpu as pltpu
from jax.sharding import PartitionSpec as P

BLOCK = 128
EPSILON = 1e-06
SHARPNESS = 20.0
CODE = 32000.0
FLOOR = 1e-30
VMEM_LIMIT = 16 * 1024 * 1024
f32, bf16, i16, i32 = jnp.float32, jnp.bfloat16, jnp.int16, jnp.int32
shape = jax.ShapeDtypeStruct
VMEM = pl.BlockSpec(memory_space=pltpu.VMEM)
SMEM = pl.BlockSpec(memory_space=pltpu.SMEM)
HBM = pl.BlockSpec(memory_space=pltpu.HBM)


def rms_norm(values):
    return values * lax.rsqrt(jnp.mean(values * values, axis=-1, keepdims=True) + EPSILON)


def split(values):
    high = values.astype(bf16)
    return high, (values - high.astype(f32)).astype(bf16)


def dot(a, b):
    return jnp.dot(a, b, preferred_element_type=f32)


def dot_lanes(a, b):
    return lax.dot_general(a, b, (((1,), (1,)), ((), ())), preferred_element_type=f32)


def to_lanes(column):
    rows = column.shape[0]
    pick = jnp.where(lax.broadcasted_iota(i32, (8, BLOCK), 1) == 0, 1.0, 0.0).astype(bf16)
    return dot_lanes(pick, jnp.broadcast_to(column, (rows, BLOCK)).astype(bf16))[0:1]


def to_column(lanes):
    k = lanes.shape[1]
    eye = lax.broadcasted_iota(i32, (k, k), 0) == lax.broadcasted_iota(i32, (k, k), 1)
    return jnp.sum(jnp.where(eye, lanes, 0.0), axis=1, keepdims=True)


def exponent_of(top):
    return jnp.clip(jnp.ceil(jnp.log2(jnp.maximum(top * 1.001, FLOOR))), -100.0, 100.0)


def encode(values, exponent):
    return jnp.round(values * (CODE * jnp.exp2(-exponent))).astype(i16)


def decode(codes, exponent):
    return codes.astype(f32) * (jnp.exp2(exponent) * (1.0 / CODE))


def head_rows(count, w):
    return -(-count // (16 * w)) * 16


def chunk(index, size):
    return pl.ds(pl.multiple_of(index * size, size), size)


def start(source, target, sem):
    copy = pltpu.make_async_copy(source, target, sem)
    copy.start()
    return copy


def start_all(sources, targets, sems):
    return [start(a, b, sems.at[k]) for k, (a, b) in enumerate(zip(sources, targets))]


def wait_all(copies):
    for copy in copies:
        copy.wait()


def pack_kernel(chunks, me_ref, points_ref, cluster_ref, *refs):
    outs, (head, sems, head_sems) = refs[:-3], refs[-3:]
    rows = points_ref.shape[0]
    h = len(outs) // chunks
    q = me_ref[0] & (h - 1)
    sources = [points_ref.at[:, chunk((q ^ (k // chunks)) * chunks + k % chunks, BLOCK)] for k in range(len(outs))]
    copies = start_all(sources, [out.at[0:rows, :] for out in outs], sems)
    cluster = cluster_ref[...]
    head[...] = jnp.concatenate([cluster & (BLOCK - 1), (cluster - me_ref[1]) // BLOCK]).astype(f32).astype(bf16)
    copies += start_all([head] * h, [out.at[rows:, :] for out in outs[::chunks]], head_sems)
    wait_all(copies)


def prev_kernel(after_ref, me_ref, prev_ref, parent_ref, out_ref, prev, head, sem):
    h = out_ref.shape[0]
    owned, width = prev.shape
    w = width // h
    copy = start(prev_ref, prev, sem)
    known = parent_ref.shape[0]
    head[...] = jnp.zeros_like(head)
    head[0:known, :] = parent_ref[...] - me_ref[2]
    copy.wait()
    exponent = exponent_of(jnp.max(jnp.abs(prev[...]), axis=1, keepdims=True))
    for j in range(owned // w):
        lanes = to_lanes(exponent[j * w : (j + 1) * w])
        head[known + j : known + j + 1, :] = lanes.astype(i32)
    for d in range(h):
        out_ref[d, 0:owned, :] = encode(prev[:, d * w : (d + 1) * w], exponent)
        out_ref[d, owned:, :] = head[...].astype(i16)


def prepare_kernel(per, me_ref, *refs):
    arrived, (member_ref, place_ref, near_ref, far_ref, count, heads, sems) = refs[:-7], refs[-7:]
    h = len(arrived)
    rows = near_ref.shape[0]
    blocks = place_ref.shape[0] // h
    copies = start_all([a.at[blocks * BLOCK :, :] for a in arrived], [heads.at[m] for m in range(h)], sems)
    count[...] = jnp.zeros_like(count)
    centroid = lax.broadcasted_iota(i32, (BLOCK, BLOCK), 0)
    ones = jnp.ones((BLOCK, BLOCK), bf16)
    for m in range(h):
        copies[m].wait()
        head = heads[m].astype(f32)
        for i in range(blocks):
            number = jnp.max(head[blocks + i : blocks + i + 1, :]).astype(i32)
            place = number ^ (me_ref[0] * per)
            place_ref[m * blocks + i] = place
            member = jnp.where(centroid == head[i : i + 1, :].astype(i32), 1.0, 0.0).astype(bf16)
            at = (m * blocks + i) * BLOCK
            member_ref[at : at + BLOCK, :] = member
            count[chunk(place, BLOCK), :] += dot(member, ones)
    near_ref[...] = count[0:rows, :]
    for j in range(rows // BLOCK):
        far = count[rows + j * BLOCK : rows + (j + 1) * BLOCK, 0:1]
        high = jnp.floor(far / 64.0)
        far_ref[j : j + 1, :] = (to_lanes(high) * 64.0 + to_lanes(far - high * 64.0)).astype(i32)


def previous_kernel(me_ref, arrived_ref, prev_ref, upper_ref):
    h = arrived_ref.shape[0]
    q = me_ref[0] & (h - 1)
    rows, w = prev_ref.shape
    owned = rows // h
    each = owned // w
    parent_at = lax.broadcasted_iota(i32, (upper_ref.shape[0], w), 0)
    for m in range(h):
        arrived = arrived_ref.at[q ^ m]
        head = arrived[owned:, :].astype(i32)
        for j in range(each):
            at = slice(m * owned + j * w, m * owned + (j + 1) * w)
            upper_ref[:, at] = jnp.where(parent_at == head[j : j + 1, :], 1.0, 0.0).astype(bf16)
            exponent = to_column(head[each + j : each + j + 1, :].astype(f32))
            prev_ref[at, :] = decode(arrived[j * w : (j + 1) * w, :], exponent)


def sums_kernel(place_ref, before_ref, member_ref, far_count_ref, *refs):
    h = (len(refs) - 5) // 2
    points, (acc_ref, code, after_ref, head, sem), held = refs[:h], refs[h : h + 5], refs[h + 5 :]
    after_ref[0] = before_ref[0]
    rows = acc_ref.shape[0] // 2
    blocks = held[0].shape[0] // BLOCK
    copies = start_all([p.at[0 : blocks * BLOCK, :] for p in points], held, sem)
    acc_ref[...] = jnp.zeros_like(acc_ref)
    for m in range(h):
        copies[m].wait()
        for i in range(blocks):
            at, here = (m * blocks + i) * BLOCK, slice(i * BLOCK, (i + 1) * BLOCK)
            acc_ref[chunk(place_ref[m * blocks + i], BLOCK), :] += dot(member_ref[at : at + BLOCK, :], held[m][here, :])
    lines = rows // BLOCK
    step = 2 * BLOCK
    for j in range(rows // step):
        at = slice(j * step, (j + 1) * step)
        value = acc_ref[rows + j * step : rows + (j + 1) * step, :]
        exponent = exponent_of(jnp.max(jnp.abs(value), axis=1, keepdims=True))
        code[at, :] = encode(value, exponent)
        lanes = to_lanes(exponent).astype(i32)
        for k in range(step // BLOCK):
            row = j * (step // BLOCK) + k
            head[row : row + 1, :] = lanes[:, k * BLOCK : (k + 1) * BLOCK]
    head[lines:, :] = far_count_ref[...]
    code[rows:, :] = head[...].astype(i16)


def spot(index, w):
    return slice(index * BLOCK // w, index * BLOCK // w + 1), slice(index * BLOCK % w, index * BLOCK % w + BLOCK)


def refresh_kernel(chunks, near_ref, prev_ref, *refs):
    accs, crossed, x_ref, outs, tail = refs[:chunks], refs[chunks : 2 * chunks], refs[2 * chunks], refs[2 * chunks + 1 : -1], refs[-1]
    h = len(outs)
    rows, w = x_ref.shape
    owned = rows // h
    lines = rows // BLOCK
    heads = [crossed[c][rows:, :].astype(i32).astype(f32) for c in range(chunks)]
    unit = jnp.ones((8, BLOCK), bf16)
    for j in range(lines):
        at = slice(j * BLOCK, (j + 1) * BLOCK)
        count = near_ref[at, :] + to_column(heads[0][lines + j : lines + j + 1, :])
        inverse = 1.0 / jnp.maximum(count, 1.0)
        square, top = None, None
        for c in range(chunks):
            lanes = slice(c * BLOCK, (c + 1) * BLOCK)
            far = decode(crossed[c][at, :], to_column(heads[c][j : j + 1, :]))
            x = (accs[c][at, :] + far) * inverse + prev_ref[at, lanes]
            x_ref[at, lanes] = x
            square = x * x if c == 0 else square + x * x
            top = jnp.abs(x) if c == 0 else jnp.maximum(top, jnp.abs(x))
        square_high, square_low = split(square)
        sums = (dot_lanes(unit, square_high) + dot_lanes(unit, square_low))[0:1]
        sums_exponent = exponent_of(sums)
        scaled = sums * (16384.0 * jnp.exp2(-sums_exponent))
        whole = jnp.floor(scaled)
        exponent = exponent_of(jnp.max(top, axis=1, keepdims=True))
        for k, value in enumerate((sums_exponent, whole, jnp.floor((scaled - whole) * 16384.0), to_lanes(exponent))):
            tail[spot(k * lines + j, w)] = value.astype(i32)
        here = slice(j * BLOCK % owned, j * BLOCK % owned + BLOCK)
        outs[j * BLOCK // owned][here, :] = encode(x_ref[at, :], exponent)
    for out in outs:
        out[owned:, :] = tail[...].astype(i16)


def put_codes(values, code, head):
    rows, w = values.shape
    size = min(rows, w)
    head[...] = jnp.zeros_like(head)
    for j in range(rows // size):
        at = slice(j * size, (j + 1) * size)
        exponent = exponent_of(jnp.max(jnp.abs(values[at, :]), axis=1, keepdims=True))
        code[at, :] = encode(values[at, :], exponent)
        head[j : j + 1, 0:size] = to_lanes(exponent).astype(i32)
    code[rows:, :] = head[...].astype(i16)


def get_codes(code, j, rows, size):
    w = code.shape[1]
    row, lane = j * size // min(rows, w), j * size % min(rows, w)
    lanes = code[rows : rows + 16, :].astype(i32).astype(f32)[row : row + 1, lane : lane + size]
    return decode(code[j * size : (j + 1) * size, :], to_column(lanes))


def upper_kernel(width, member_ref, x_ref, *refs):
    backs, outs, (high, low, sums), heads = refs[:-7], refs[-7:-5], refs[-5:-2], refs[-2:]
    h = len(backs)
    total, w = x_ref.shape
    owned = total // h
    lines, per = total // BLOCK, owned // BLOCK
    tails = [back[owned:, :].astype(i32).astype(f32) for back in backs]
    for p in range(h):
        for j in range(per):
            squares = None
            for m in range(h):
                index = (p ^ m) * per + j
                exponent, whole, rest = (tails[m][spot(k * lines + index, w)] for k in range(3))
                value = (whole + rest * (1.0 / 16384.0)) * (jnp.exp2(exponent) * (1.0 / 16384.0))
                squares = value if m == 0 else squares + value
            factor = lax.rsqrt(squares / width + EPSILON)
            at = slice(p * owned + j * BLOCK, p * owned + (j + 1) * BLOCK)
            high[at, :], low[at, :] = split(x_ref[at, :] * to_column(factor))
    rows = sums.shape[0]
    for k in range(2):
        member = member_ref[k * rows : (k + 1) * rows, :]
        sums[...] = dot(member, high[...]) + dot(member, low[...])
        put_codes(sums, outs[k], heads[k])


def both_kernel(own, far, code_ref, sums, head):
    rows = sums.shape[0]
    for j in range(rows // BLOCK):
        sums[j * BLOCK : (j + 1) * BLOCK, :] = get_codes(own, j, rows, BLOCK) + get_codes(far, j, rows, BLOCK)
    put_codes(sums, code_ref, head)


def join_kernel(me_ref, *refs):
    parts, (out_ref, out, out_sems) = refs[:-3], refs[-3:]
    h = len(parts) // 2
    q = me_ref[0] & (h - 1)
    total, width = out.shape
    rows = total // 2
    w = width // h
    copies = []
    for j in range(total // BLOCK):
        at, k = slice(j * BLOCK, (j + 1) * BLOCK), j * BLOCK // rows
        values = [get_codes(parts[k * h + m], j - k * (rows // BLOCK), rows, BLOCK) for m in range(h)]
        square = sum(v * v for v in values)
        factor = lax.rsqrt(jnp.sum(square, axis=1, keepdims=True) / width + EPSILON)
        for m in range(h):
            out[at, chunk(q ^ m, w)] = values[m] * factor
        copies.append(start(out.at[at, :], out_ref.at[at, :], out_sems.at[j]))
    wait_all(copies)


def decode_kernel(me_ref, *refs):
    codes, out_ref = refs[:-1], refs[-1]
    h = len(codes)
    q = me_ref[0] & (h - 1)
    rows, width = out_ref.shape
    w = width // h
    lines, per = h * rows // BLOCK, rows // BLOCK
    tails = [code[rows:, :].astype(i32).astype(f32) for code in codes]
    for j in range(per):
        at = slice(j * BLOCK, (j + 1) * BLOCK)
        values = []
        for m in range(h):
            exponent = tails[m][spot(3 * lines + m * per + j, w)]
            values.append(decode(codes[m][at, :], to_column(exponent)))
        square = sum(v * v for v in values)
        factor = lax.rsqrt(jnp.sum(square, axis=1, keepdims=True) / width + EPSILON)
        for m in range(h):
            out_ref[at, chunk(q ^ m, w)] = values[m] * factor


def call(kernel, out_shape, **kw):
    params = pltpu.CompilerParams(vmem_limit_bytes=VMEM_LIMIT)
    return pl.pallas_call(kernel, out_shape=out_shape, compiler_params=params, **kw)


def dma(*dims):
    return pltpu.SemaphoreType.DMA(dims) if dims else pltpu.SemaphoreType.DMA


def shards(points, point_cluster, cand_blocks, cent1_prev, parent, cent2_prev):
    point_rows, width = points.shape
    blocks = point_rows // BLOCK
    owned = cent1_prev.shape[0]
    upper_rows = cent2_prev.shape[0]
    n = lax.axis_size("cent")
    h = n // 2
    dp = lax.axis_index("dp")
    w = width // h
    chunks = w // BLOCK
    rows = h * owned
    me = jnp.stack([lax.axis_index("cent").astype(i32), dp * (n * owned), dp * upper_rows])

    def swap(value, mask):
        return lax.ppermute(value, "cent", [(i, i ^ mask) for i in range(n)])

    def swap_half(values):
        arrived = {m: swap(values[m], m) for m in range(h - 1, 0, -1)}
        return [values[0]] + [arrived[m] for m in range(1, h)]

    table_rows = lax.all_gather(cent2_prev, "dp", axis=0, tiled=True)

    first_shape = shape((point_rows + 2 * blocks, BLOCK), bf16)
    packed = call(
        functools.partial(pack_kernel, chunks),
        ([first_shape] + [shape((point_rows, BLOCK), bf16)] * (chunks - 1)) * h,
        in_specs=[SMEM, HBM, VMEM],
        out_specs=[HBM] * (h * chunks),
        scratch_shapes=[pltpu.VMEM((2 * blocks, BLOCK), bf16), dma(h * chunks), dma(h)],
        name="pack",
    )(me, points, point_cluster.reshape(blocks, BLOCK))
    arrived = [swap_half(packed[c::chunks]) for c in range(chunks)]

    member, place, near, far_count = call(
        functools.partial(prepare_kernel, owned // BLOCK),
        [
            shape((h * point_rows, BLOCK), bf16),
            shape((h * blocks,), i32),
            shape((rows, BLOCK), f32),
            shape((rows // BLOCK, BLOCK), i32),
        ],
        in_specs=[SMEM] + [HBM] * h,
        out_specs=[VMEM, SMEM] + [VMEM] * 2,
        scratch_shapes=[pltpu.VMEM((2 * rows, BLOCK), f32), pltpu.VMEM((h, 2 * blocks, BLOCK), bf16), dma(h)],
        name="prepare",
    )(me, *arrived[0])

    lines = rows + 2 * rows // BLOCK
    accs, crossed, after, first = [], [], place, None
    for c in range(chunks):
        acc, code, ended = call(
            sums_kernel,
            [shape((2 * rows, BLOCK), f32), shape((lines, BLOCK), i16), shape((1,), i32)],
            in_specs=[SMEM, SMEM, VMEM, VMEM] + [HBM] * h,
            out_specs=[VMEM, VMEM, SMEM],
            scratch_shapes=[pltpu.VMEM((2 * rows // BLOCK, BLOCK), i32), dma(h)]
            + [pltpu.VMEM((point_rows, BLOCK), bf16)] * h,
            name=f"sums{c}",
        )(place, after, member, far_count, *arrived[c])
        accs.append(acc)
        crossed.append(swap(code, h))
        after = ended
        first = first if c else ended

    head = head_rows(2 * owned, w)
    prevs = call(
        prev_kernel,
        shape((h, owned + head, w), i16),
        in_specs=[SMEM, SMEM, HBM, VMEM],
        out_specs=VMEM,
        scratch_shapes=[pltpu.VMEM((owned, width), f32), pltpu.VMEM((head, w), i32), dma()],
        name="prev",
    )(first, me, cent1_prev, parent.reshape(owned // w, w))
    halves = [list(range(k * h, (k + 1) * h)) for k in range(2)]
    prevs = lax.all_to_all(prevs, "cent", split_axis=0, concat_axis=0, axis_index_groups=halves, tiled=True)
    prev, upper_member = call(
        previous_kernel,
        [shape((rows, w), f32), shape((upper_rows, rows), bf16)],
        in_specs=[SMEM, VMEM],
        out_specs=[VMEM] * 2,
        name="previous",
    )(me, prevs)

    points, table_rows = lax.optimization_barrier((points, table_rows))
    unit_points = rms_norm(points.astype(f32)).astype(bf16)
    table_scale = lax.rsqrt(jnp.mean(jnp.square(table_rows.astype(f32)), axis=-1) + EPSILON)
    table_units = (table_rows.astype(f32) * table_scale[:, None]).astype(bf16)
    products = lax.dot_general(
        unit_points, table_units, (((1,), (1,)), ((), ())), preferred_element_type=f32
    )
    column_block = jnp.arange(table_rows.shape[0]) // BLOCK
    listed = jnp.any(cand_blocks[:, :, None] == column_block[None, None, :], axis=1)
    weights = jnp.exp(products * (SHARPNESS / width)).reshape(blocks, BLOCK, -1)
    running = jnp.sum(weights * listed[:, None, :].astype(f32), axis=2).reshape(point_rows)
    point_score, near = lax.optimization_barrier((jnp.log(running), near))

    tail = 4 * rows // w
    x, *backs = call(
        functools.partial(refresh_kernel, chunks),
        [shape((rows, w), f32)] + [shape((owned + tail, w), i16)] * h,
        in_specs=[VMEM] * (2 + 2 * chunks),
        out_specs=[VMEM] * (h + 1),
        scratch_shapes=[pltpu.VMEM((tail, w), i32)],
        name="refresh",
    )(near, prev, *accs, *crossed)
    backs = swap_half(backs)

    part = upper_rows // 2
    tail = head_rows(part, w)
    code_shape = shape((part + tail, w), i16)
    held_head = pltpu.VMEM((tail, w), i32)
    codes = call(
        functools.partial(upper_kernel, width),
        [code_shape] * 2,
        in_specs=[VMEM] * (h + 2),
        out_specs=[VMEM] * 2,
        scratch_shapes=[pltpu.VMEM((rows, w), bf16), pltpu.VMEM((rows, w), bf16), pltpu.VMEM((part, w), f32)]
        + [held_head] * 2,
        name="upper",
    )(upper_member, x, *backs)
    far_codes = [swap(code, h) for code in codes]
    parts = []
    for k in range(2):
        code = codes[k]
        code = call(
            both_kernel,
            code_shape,
            in_specs=[VMEM, VMEM],
            out_specs=VMEM,
            scratch_shapes=[pltpu.VMEM((part, w), f32), held_head],
            name=f"both{k}",
        )(code, far_codes[k])
        parts += swap_half([code] * h)

    cent1_new = call(
        decode_kernel,
        shape((owned, width), f32),
        in_specs=[SMEM] + [VMEM] * h,
        out_specs=VMEM,
        name="decode",
    )(me, *backs)
    last, cent1_new = lax.optimization_barrier((me, cent1_new))
    cent2_new = call(
        join_kernel,
        shape((upper_rows, width), f32),
        in_specs=[SMEM] + [VMEM] * (2 * h),
        out_specs=HBM,
        scratch_shapes=[pltpu.VMEM((upper_rows, width), f32), dma(upper_rows // BLOCK)],
        name="join",
    )(last, *parts)
    return (cent1_new, cent2_new, point_score)


def solution(mesh):
    placed = (
        P(("dp", "cent"), None),
        P(("dp", "cent")),
        P(("dp", "cent"), None),
        P(("dp", "cent"), None),
        P(("dp", "cent")),
        P("dp", None),
    )
    return jax.shard_map(
        shards,
        mesh=mesh,
        in_specs=placed,
        out_specs=(P(("dp", "cent"), None), P("dp", None), P(("dp", "cent"))),
        check_vma=False,
    )
```

```python
import functools

import jax
import jax.numpy as jnp
from jax import lax
from jax.experimental import pallas as pl
from jax.experimental.pallas import tpu as pltpu
from jax.sharding import PartitionSpec as P

BLOCK = 128
EPSILON = 1e-06
SHARPNESS = 20.0
CODE = 32000.0
FLOOR = 1e-30
VMEM_LIMIT = 16 * 1024 * 1024
f32, bf16, i16, i32 = jnp.float32, jnp.bfloat16, jnp.int16, jnp.int32
shape = jax.ShapeDtypeStruct
VMEM = pl.BlockSpec(memory_space=pltpu.VMEM)
SMEM = pl.BlockSpec(memory_space=pltpu.SMEM)
HBM = pl.BlockSpec(memory_space=pltpu.HBM)


def rms_norm(values):
    return values * lax.rsqrt(jnp.mean(values * values, axis=-1, keepdims=True) + EPSILON)


def split(values):
    high = values.astype(bf16)
    return high, (values - high.astype(f32)).astype(bf16)


def dot(a, b):
    return jnp.dot(a, b, preferred_element_type=f32)


def dot_lanes(a, b):
    return lax.dot_general(a, b, (((1,), (1,)), ((), ())), preferred_element_type=f32)


def to_lanes(column):
    rows = column.shape[0]
    pick = jnp.where(lax.broadcasted_iota(i32, (8, BLOCK), 1) == 0, 1.0, 0.0).astype(bf16)
    return dot_lanes(pick, jnp.broadcast_to(column, (rows, BLOCK)).astype(bf16))[0:1]


def to_column(lanes):
    k = lanes.shape[1]
    eye = lax.broadcasted_iota(i32, (k, k), 0) == lax.broadcasted_iota(i32, (k, k), 1)
    return jnp.sum(jnp.where(eye, lanes, 0.0), axis=1, keepdims=True)


def exponent_of(top):
    return jnp.clip(jnp.ceil(jnp.log2(jnp.maximum(top * 1.001, FLOOR))), -100.0, 100.0)


def encode(values, exponent):
    return jnp.round(values * (CODE * jnp.exp2(-exponent))).astype(i16)


def decode(codes, exponent):
    return codes.astype(f32) * (jnp.exp2(exponent) * (1.0 / CODE))


def head_rows(count, w):
    return -(-count // (16 * w)) * 16


def chunk(index, size):
    return pl.ds(pl.multiple_of(index * size, size), size)


def start(source, target, sem):
    copy = pltpu.make_async_copy(source, target, sem)
    copy.start()
    return copy


def start_all(sources, targets, sems):
    return [start(a, b, sems.at[k]) for k, (a, b) in enumerate(zip(sources, targets))]


def wait_all(copies):
    for copy in copies:
        copy.wait()


def pack_kernel(chunks, me_ref, points_ref, cluster_ref, first_ref, *refs):
    outs, (after_ref, head, sems, head_sems) = refs[:-4], refs[-4:]
    after_ref[0] = me_ref[0]
    rows = points_ref.shape[0]
    h = first_ref.shape[0]
    q = me_ref[0] & (h - 1)
    copies = []
    for d in range(h):
        source = points_ref.at[:, d * chunks * BLOCK : (d * chunks + 1) * BLOCK]
        copies.append(start(source, first_ref.at[d, 0:rows, :], head_sems.at[d]))
    cluster = cluster_ref[...]
    head[...] = jnp.concatenate([cluster & (BLOCK - 1), (cluster - me_ref[1]) // BLOCK]).astype(f32).astype(bf16)
    copies += [start(head, first_ref.at[d, rows:, :], head_sems.at[h + d]) for d in range(h)]
    for k, out in enumerate(outs):
        m, c = k // (chunks - 1), k % (chunks - 1) + 1
        copies.append(start(points_ref.at[:, chunk((q ^ m) * chunks + c, BLOCK)], out, sems.at[k]))
    wait_all(copies)


def prev_kernel(me_ref, after_ref, prev_ref, parent_ref, *refs):
    h = (len(refs) - 4) // 2
    outs, (prev, head, sem, sems), held = refs[:h], refs[h : h + 4], refs[h + 4 :]
    q = me_ref[0] & (h - 1)
    owned, width = prev.shape
    w = width // h
    copy = start(prev_ref, prev, sem)
    known = parent_ref.shape[0]
    head[...] = jnp.zeros_like(head)
    head[0:known, :] = parent_ref[...] - me_ref[2]
    copy.wait()
    exponent = exponent_of(jnp.max(jnp.abs(prev[...]), axis=1, keepdims=True))
    for j in range(owned // w):
        lanes = to_lanes(exponent[j * w : (j + 1) * w])
        head[known + j : known + j + 1, :] = lanes.astype(i32)
    copies = []
    for m in range(h):
        held[m][0:owned, :] = encode(prev[:, chunk(q ^ m, w)], exponent)
        held[m][owned:, :] = head[...].astype(i16)
        copies.append(start(held[m], outs[m], sems.at[m]))
    wait_all(copies)


def prepare_kernel(per, me_ref, *refs):
    arrived, member_ref, place_ref, near_ref, far_ref, count, heads, sems = refs
    h = arrived.shape[0]
    q = me_ref[0] & (h - 1)
    rows = near_ref.shape[0]
    blocks = place_ref.shape[0] // h
    copies = start_all([arrived.at[q ^ m, blocks * BLOCK :, :] for m in range(h)], [heads.at[m] for m in range(h)], sems)
    count[...] = jnp.zeros_like(count)
    centroid = lax.broadcasted_iota(i32, (BLOCK, BLOCK), 0)
    ones = jnp.ones((BLOCK, BLOCK), bf16)
    for m in range(h):
        copies[m].wait()
        head = heads[m].astype(f32)
        for i in range(blocks):
            number = jnp.max(head[blocks + i : blocks + i + 1, :]).astype(i32)
            place = number ^ (me_ref[0] * per)
            place_ref[m * blocks + i] = place
            member = jnp.where(centroid == head[i : i + 1, :].astype(i32), 1.0, 0.0).astype(bf16)
            at = (m * blocks + i) * BLOCK
            member_ref[at : at + BLOCK, :] = member
            count[chunk(place, BLOCK), :] += dot(member, ones)
    near_ref[...] = count[0:rows, :]
    for j in range(rows // BLOCK):
        far = count[rows + j * BLOCK : rows + (j + 1) * BLOCK, 0:1]
        high = jnp.floor(far / 64.0)
        far_ref[j : j + 1, :] = (to_lanes(high) * 64.0 + to_lanes(far - high * 64.0)).astype(i32)


def previous_kernel(*refs):
    arrived, (prev_ref, upper_ref) = refs[:-2], refs[-2:]
    h = len(arrived)
    rows, w = prev_ref.shape
    owned = rows // h
    each = owned // w
    parent_at = lax.broadcasted_iota(i32, (upper_ref.shape[0], w), 0)
    for m in range(h):
        head = arrived[m][owned:, :].astype(i32)
        for j in range(each):
            at = slice(m * owned + j * w, m * owned + (j + 1) * w)
            upper_ref[:, at] = jnp.where(parent_at == head[j : j + 1, :], 1.0, 0.0).astype(bf16)
            exponent = to_column(head[each + j : each + j + 1, :].astype(f32))
            prev_ref[at, :] = decode(arrived[m][j * w : (j + 1) * w, :], exponent)


def sums_kernel(h, me_ref, place_ref, before_ref, member_ref, far_count_ref, *refs):
    points, (acc_ref, code, after_ref, head, sem), held = refs[: -h - 5], refs[-h - 5 : -h], refs[-h:]
    q = me_ref[0] & (h - 1)
    if len(points) == 1:
        points = [points[0].at[q ^ m] for m in range(h)]
    after_ref[0] = before_ref[0]
    rows = acc_ref.shape[0] // 2
    blocks = held[0].shape[0] // BLOCK
    copies = start_all([p.at[0 : blocks * BLOCK, :] for p in points], held, sem)
    acc_ref[...] = jnp.zeros_like(acc_ref)
    for m in range(h):
        copies[m].wait()
        for i in range(blocks):
            at, here = (m * blocks + i) * BLOCK, slice(i * BLOCK, (i + 1) * BLOCK)
            acc_ref[chunk(place_ref[m * blocks + i], BLOCK), :] += dot(member_ref[at : at + BLOCK, :], held[m][here, :])
    lines = rows // BLOCK
    step = 2 * BLOCK
    for j in range(rows // step):
        at = slice(j * step, (j + 1) * step)
        value = acc_ref[rows + j * step : rows + (j + 1) * step, :]
        exponent = exponent_of(jnp.max(jnp.abs(value), axis=1, keepdims=True))
        code[at, :] = encode(value, exponent)
        lanes = to_lanes(exponent).astype(i32)
        for k in range(step // BLOCK):
            row = j * (step // BLOCK) + k
            head[row : row + 1, :] = lanes[:, k * BLOCK : (k + 1) * BLOCK]
    head[lines:, :] = far_count_ref[...]
    code[rows:, :] = head[...].astype(i16)


def spot(index, w):
    return slice(index * BLOCK // w, index * BLOCK // w + 1), slice(index * BLOCK % w, index * BLOCK % w + BLOCK)


def refresh_kernel(chunks, near_ref, prev_ref, *refs):
    accs, crossed, x_ref, outs, tail = refs[:chunks], refs[chunks : 2 * chunks], refs[2 * chunks], refs[2 * chunks + 1 : -1], refs[-1]
    h = len(outs)
    rows, w = x_ref.shape
    owned = rows // h
    lines = rows // BLOCK
    heads = [crossed[c][rows:, :].astype(i32).astype(f32) for c in range(chunks)]
    unit = jnp.ones((8, BLOCK), bf16)
    for j in range(lines):
        at = slice(j * BLOCK, (j + 1) * BLOCK)
        count = near_ref[at, :] + to_column(heads[0][lines + j : lines + j + 1, :])
        inverse = 1.0 / jnp.maximum(count, 1.0)
        square, top = None, None
        for c in range(chunks):
            lanes = slice(c * BLOCK, (c + 1) * BLOCK)
            far = decode(crossed[c][at, :], to_column(heads[c][j : j + 1, :]))
            x = (accs[c][at, :] + far) * inverse + prev_ref[at, lanes]
            x_ref[at, lanes] = x
            square = x * x if c == 0 else square + x * x
            top = jnp.abs(x) if c == 0 else jnp.maximum(top, jnp.abs(x))
        square_high, square_low = split(square)
        sums = (dot_lanes(unit, square_high) + dot_lanes(unit, square_low))[0:1]
        sums_exponent = exponent_of(sums)
        scaled = sums * (16384.0 * jnp.exp2(-sums_exponent))
        whole = jnp.floor(scaled)
        exponent = exponent_of(jnp.max(top, axis=1, keepdims=True))
        for k, value in enumerate((sums_exponent, whole, jnp.floor((scaled - whole) * 16384.0), to_lanes(exponent))):
            tail[spot(k * lines + j, w)] = value.astype(i32)
        here = slice(j * BLOCK % owned, j * BLOCK % owned + BLOCK)
        outs[j * BLOCK // owned][here, :] = encode(x_ref[at, :], exponent)
    for out in outs:
        out[owned:, :] = tail[...].astype(i16)


def put_codes(values, code, head):
    rows, w = values.shape
    size = min(rows, w)
    head[...] = jnp.zeros_like(head)
    for j in range(rows // size):
        at = slice(j * size, (j + 1) * size)
        exponent = exponent_of(jnp.max(jnp.abs(values[at, :]), axis=1, keepdims=True))
        code[at, :] = encode(values[at, :], exponent)
        head[j : j + 1, 0:size] = to_lanes(exponent).astype(i32)
    code[rows:, :] = head[...].astype(i16)


def get_codes(code, j, rows, size):
    w = code.shape[1]
    row, lane = j * size // min(rows, w), j * size % min(rows, w)
    lanes = code[rows : rows + 16, :].astype(i32).astype(f32)[row : row + 1, lane : lane + size]
    return decode(code[j * size : (j + 1) * size, :], to_column(lanes))


def upper_kernel(width, member_ref, x_ref, *refs):
    backs, outs, (high, low, sums), heads = refs[:-7], refs[-7:-5], refs[-5:-2], refs[-2:]
    h = len(backs)
    total, w = x_ref.shape
    owned = total // h
    lines, per = total // BLOCK, owned // BLOCK
    tails = [back[owned:, :].astype(i32).astype(f32) for back in backs]
    for p in range(h):
        for j in range(per):
            squares = None
            for m in range(h):
                index = (p ^ m) * per + j
                exponent, whole, rest = (tails[m][spot(k * lines + index, w)] for k in range(3))
                value = (whole + rest * (1.0 / 16384.0)) * (jnp.exp2(exponent) * (1.0 / 16384.0))
                squares = value if m == 0 else squares + value
            factor = lax.rsqrt(squares / width + EPSILON)
            at = slice(p * owned + j * BLOCK, p * owned + (j + 1) * BLOCK)
            high[at, :], low[at, :] = split(x_ref[at, :] * to_column(factor))
    rows = sums.shape[0]
    for k in range(2):
        member = member_ref[k * rows : (k + 1) * rows, :]
        sums[...] = dot(member, high[...]) + dot(member, low[...])
        put_codes(sums, outs[k], heads[k])


def both_kernel(own, far, code_ref, sums, head):
    rows = sums.shape[0]
    for j in range(rows // BLOCK):
        sums[j * BLOCK : (j + 1) * BLOCK, :] = get_codes(own, j, rows, BLOCK) + get_codes(far, j, rows, BLOCK)
    put_codes(sums, code_ref, head)


def join_kernel(me_ref, *refs):
    parts, (out_ref, out, out_sems) = refs[:-3], refs[-3:]
    h = len(parts) // 2
    q = me_ref[0] & (h - 1)
    total, width = out.shape
    rows = total // 2
    w = width // h
    copies = []
    for j in range(total // BLOCK):
        at, k = slice(j * BLOCK, (j + 1) * BLOCK), j * BLOCK // rows
        values = [get_codes(parts[k * h + m], j - k * (rows // BLOCK), rows, BLOCK) for m in range(h)]
        square = sum(v * v for v in values)
        factor = lax.rsqrt(jnp.sum(square, axis=1, keepdims=True) / width + EPSILON)
        for m in range(h):
            out[at, chunk(q ^ m, w)] = values[m] * factor
        copies.append(start(out.at[at, :], out_ref.at[at, :], out_sems.at[j]))
    wait_all(copies)


def decode_kernel(me_ref, *refs):
    codes, out_ref = refs[:-1], refs[-1]
    h = len(codes)
    q = me_ref[0] & (h - 1)
    rows, width = out_ref.shape
    w = width // h
    lines, per = h * rows // BLOCK, rows // BLOCK
    tails = [code[rows:, :].astype(i32).astype(f32) for code in codes]
    for j in range(per):
        at = slice(j * BLOCK, (j + 1) * BLOCK)
        values = []
        for m in range(h):
            exponent = tails[m][spot(3 * lines + m * per + j, w)]
            values.append(decode(codes[m][at, :], to_column(exponent)))
        square = sum(v * v for v in values)
        factor = lax.rsqrt(jnp.sum(square, axis=1, keepdims=True) / width + EPSILON)
        for m in range(h):
            out_ref[at, chunk(q ^ m, w)] = values[m] * factor


def call(kernel, out_shape, **kw):
    params = pltpu.CompilerParams(vmem_limit_bytes=VMEM_LIMIT)
    return pl.pallas_call(kernel, out_shape=out_shape, compiler_params=params, **kw)


def dma(*dims):
    return pltpu.SemaphoreType.DMA(dims) if dims else pltpu.SemaphoreType.DMA


def shards(points, point_cluster, cand_blocks, cent1_prev, parent, cent2_prev):
    point_rows, width = points.shape
    blocks = point_rows // BLOCK
    owned = cent1_prev.shape[0]
    upper_rows = cent2_prev.shape[0]
    n = lax.axis_size("cent")
    h = n // 2
    dp = lax.axis_index("dp")
    w = width // h
    chunks = w // BLOCK
    rows = h * owned
    me = jnp.stack([lax.axis_index("cent").astype(i32), dp * (n * owned), dp * upper_rows])

    def swap(value, mask):
        return lax.ppermute(value, "cent", [(i, i ^ mask) for i in range(n)])

    def swap_half(values):
        arrived = {m: swap(values[m], m) for m in range(h - 1, 0, -1)}
        return [values[0]] + [arrived[m] for m in range(1, h)]

    table_rows = lax.all_gather(cent2_prev, "dp", axis=0, tiled=True)

    others = h * (chunks - 1)
    first, *packed, after_pack = call(
        functools.partial(pack_kernel, chunks),
        [shape((h, point_rows + 2 * blocks, BLOCK), bf16)]
        + [shape((point_rows, BLOCK), bf16)] * others
        + [shape((1,), i32)],
        in_specs=[SMEM, HBM, VMEM],
        out_specs=[HBM] * (others + 1) + [SMEM],
        scratch_shapes=[pltpu.VMEM((2 * blocks, BLOCK), bf16), dma(max(others, 1)), dma(2 * h)],
        name="pack",
    )(me, points, point_cluster.reshape(blocks, BLOCK))
    halves = [list(range(k * h, (k + 1) * h)) for k in range(2)]
    first = lax.all_to_all(first, "cent", split_axis=0, concat_axis=0, axis_index_groups=halves, tiled=True)
    arrived = [[first]] + [swap_half(packed[c :: chunks - 1]) for c in range(chunks - 1)]

    member, place, near, far_count = call(
        functools.partial(prepare_kernel, owned // BLOCK),
        [
            shape((h * point_rows, BLOCK), bf16),
            shape((h * blocks,), i32),
            shape((rows, BLOCK), f32),
            shape((rows // BLOCK, BLOCK), i32),
        ],
        in_specs=[SMEM, HBM],
        out_specs=[VMEM, SMEM] + [VMEM] * 2,
        scratch_shapes=[pltpu.VMEM((2 * rows, BLOCK), f32), pltpu.VMEM((h, 2 * blocks, BLOCK), bf16), dma(h)],
        name="prepare",
    )(me, first)

    lines = rows + 2 * rows // BLOCK
    accs, crossed, after = [], [], place
    for c in range(chunks):
        acc, code, ended = call(
            functools.partial(sums_kernel, h),
            [shape((2 * rows, BLOCK), f32), shape((lines, BLOCK), i16), shape((1,), i32)],
            in_specs=[SMEM] * 3 + [VMEM, VMEM] + [HBM] * len(arrived[c]),
            out_specs=[VMEM, VMEM, SMEM],
            scratch_shapes=[pltpu.VMEM((2 * rows // BLOCK, BLOCK), i32), dma(h)]
            + [pltpu.VMEM((point_rows, BLOCK), bf16)] * h,
            name=f"sums{c}",
        )(me, place, after, member, far_count, *arrived[c])
        accs.append(acc)
        crossed.append(swap(code, h))
        after = ended

    head = head_rows(2 * owned, w)
    prevs = call(
        prev_kernel,
        [shape((owned + head, w), i16)] * h,
        in_specs=[SMEM, SMEM, HBM, VMEM],
        out_specs=[HBM] * h,
        scratch_shapes=[pltpu.VMEM((owned, width), f32), pltpu.VMEM((head, w), i32), dma(), dma(h)]
        + [pltpu.VMEM((owned + head, w), i16)] * h,
        name="prev",
    )(me, after_pack, cent1_prev, parent.reshape(owned // w, w))
    prev, upper_member = call(
        previous_kernel,
        [shape((rows, w), f32), shape((upper_rows, rows), bf16)],
        in_specs=[VMEM] * h,
        out_specs=[VMEM] * 2,
        name="previous",
    )(*swap_half(prevs))

    points, table_rows = lax.optimization_barrier((points, table_rows))
    unit_points = rms_norm(points.astype(f32)).astype(bf16)
    table_scale = lax.rsqrt(jnp.mean(jnp.square(table_rows.astype(f32)), axis=-1) + EPSILON)
    table_scale, near = lax.optimization_barrier((table_scale, near))
    table_units = (table_rows.astype(f32) * table_scale[:, None]).astype(bf16)
    products = lax.dot_general(
        unit_points, table_units, (((1,), (1,)), ((), ())), preferred_element_type=f32
    )
    column_block = jnp.arange(table_rows.shape[0]) // BLOCK
    listed = jnp.any(cand_blocks[:, :, None] == column_block[None, None, :], axis=1)
    weights = jnp.exp(products * (SHARPNESS / width)).reshape(blocks, BLOCK, -1)
    running = jnp.sum(weights * listed[:, None, :].astype(f32), axis=2).reshape(point_rows)
    point_score = jnp.log(running)

    tail = 4 * rows // w
    x, *backs = call(
        functools.partial(refresh_kernel, chunks),
        [shape((rows, w), f32)] + [shape((owned + tail, w), i16)] * h,
        in_specs=[VMEM] * (2 + 2 * chunks),
        out_specs=[VMEM] * (h + 1),
        scratch_shapes=[pltpu.VMEM((tail, w), i32)],
        name="refresh",
    )(near, prev, *accs, *crossed)
    backs = swap_half(backs)

    part = upper_rows // 2
    tail = head_rows(part, w)
    code_shape = shape((part + tail, w), i16)
    held_head = pltpu.VMEM((tail, w), i32)
    codes = call(
        functools.partial(upper_kernel, width),
        [code_shape] * 2,
        in_specs=[VMEM] * (h + 2),
        out_specs=[VMEM] * 2,
        scratch_shapes=[pltpu.VMEM((rows, w), bf16), pltpu.VMEM((rows, w), bf16), pltpu.VMEM((part, w), f32)]
        + [held_head] * 2,
        name="upper",
    )(upper_member, x, *backs)
    far_codes = [swap(code, h) for code in codes]
    parts = []
    for k in range(2):
        code = codes[k]
        if k == 0:
            code, point_score = lax.optimization_barrier((code, point_score))
        code = call(
            both_kernel,
            code_shape,
            in_specs=[VMEM, VMEM],
            out_specs=VMEM,
            scratch_shapes=[pltpu.VMEM((part, w), f32), held_head],
            name=f"both{k}",
        )(code, far_codes[k])
        parts += swap_half([code] * h)

    cent1_new = call(
        decode_kernel,
        shape((owned, width), f32),
        in_specs=[SMEM] + [VMEM] * h,
        out_specs=VMEM,
        name="decode",
    )(me, *backs)
    last, cent1_new = lax.optimization_barrier((me, cent1_new))
    cent2_new = call(
        join_kernel,
        shape((upper_rows, width), f32),
        in_specs=[SMEM] + [VMEM] * (2 * h),
        out_specs=HBM,
        scratch_shapes=[pltpu.VMEM((upper_rows, width), f32), dma(upper_rows // BLOCK)],
        name="join",
    )(last, *parts)
    return (cent1_new, cent2_new, point_score)


def solution(mesh):
    placed = (
        P(("dp", "cent"), None),
        P(("dp", "cent")),
        P(("dp", "cent"), None),
        P(("dp", "cent"), None),
        P(("dp", "cent")),
        P("dp", None),
    )
    return jax.shard_map(
        shards,
        mesh=mesh,
        in_specs=placed,
        out_specs=(P(("dp", "cent"), None), P("dp", None), P(("dp", "cent"))),
        check_vma=False,
    )
```

```python
import functools

import jax
import jax.numpy as jnp
from jax import lax
from jax.experimental import pallas as pl
from jax.experimental.pallas import tpu as pltpu
from jax.sharding import PartitionSpec as P

BLOCK = 128
EPSILON = 1e-06
SHARPNESS = 20.0
CODE = 32000.0
FLOOR = 1e-30
VMEM_LIMIT = 16 * 1024 * 1024
f32, bf16, i16, i32 = jnp.float32, jnp.bfloat16, jnp.int16, jnp.int32
shape = jax.ShapeDtypeStruct
VMEM = pl.BlockSpec(memory_space=pltpu.VMEM)
SMEM = pl.BlockSpec(memory_space=pltpu.SMEM)
HBM = pl.BlockSpec(memory_space=pltpu.HBM)


def rms_norm(values):
    return values * lax.rsqrt(jnp.mean(values * values, axis=-1, keepdims=True) + EPSILON)


def split(values):
    high = values.astype(bf16)
    return high, (values - high.astype(f32)).astype(bf16)


def dot(a, b):
    return jnp.dot(a, b, preferred_element_type=f32)


def dot_lanes(a, b):
    return lax.dot_general(a, b, (((1,), (1,)), ((), ())), preferred_element_type=f32)


def to_lanes(column):
    rows = column.shape[0]
    pick = jnp.where(lax.broadcasted_iota(i32, (8, BLOCK), 1) == 0, 1.0, 0.0).astype(bf16)
    return dot_lanes(pick, jnp.broadcast_to(column, (rows, BLOCK)).astype(bf16))[0:1]


def to_column(lanes):
    k = lanes.shape[1]
    eye = lax.broadcasted_iota(i32, (k, k), 0) == lax.broadcasted_iota(i32, (k, k), 1)
    return jnp.sum(jnp.where(eye, lanes, 0.0), axis=1, keepdims=True)


def exponent_of(top):
    return jnp.clip(jnp.ceil(jnp.log2(jnp.maximum(top * 1.001, FLOOR))), -100.0, 100.0)


def encode(values, exponent):
    return jnp.round(values * (CODE * jnp.exp2(-exponent))).astype(i16)


def decode(codes, exponent):
    return codes.astype(f32) * (jnp.exp2(exponent) * (1.0 / CODE))


def head_rows(count, w):
    return -(-count // (16 * w)) * 16


def chunk(index, size):
    return pl.ds(pl.multiple_of(index * size, size), size)


def start(source, target, sem):
    copy = pltpu.make_async_copy(source, target, sem)
    copy.start()
    return copy


def start_all(sources, targets, sems):
    return [start(a, b, sems.at[k]) for k, (a, b) in enumerate(zip(sources, targets))]


def wait_all(copies):
    for copy in copies:
        copy.wait()


def pack_kernel(chunks, me_ref, points_ref, cluster_ref, *refs):
    outs, (after_ref, head, sems, head_sems) = refs[:-4], refs[-4:]
    after_ref[0] = me_ref[0]
    rows = points_ref.shape[0]
    h = len(outs) // chunks
    q = me_ref[0] & (h - 1)
    sources = [points_ref.at[:, chunk((q ^ (k // chunks)) * chunks + k % chunks, BLOCK)] for k in range(len(outs))]
    copies = start_all(sources, [out.at[0:rows, :] for out in outs], sems)
    cluster = cluster_ref[...]
    head[...] = jnp.concatenate([cluster & (BLOCK - 1), (cluster - me_ref[1]) // BLOCK]).astype(f32).astype(bf16)
    copies += start_all([head] * h, [out.at[rows:, :] for out in outs[::chunks]], head_sems)
    wait_all(copies)


def prev_kernel(me_ref, after_ref, prev_ref, parent_ref, *refs):
    h = (len(refs) - 4) // 2
    outs, (prev, head, sem, sems), held = refs[:h], refs[h : h + 4], refs[h + 4 :]
    q = me_ref[0] & (h - 1)
    owned, width = prev.shape
    w = width // h
    copy = start(prev_ref, prev, sem)
    known = parent_ref.shape[0]
    head[...] = jnp.zeros_like(head)
    head[0:known, :] = parent_ref[...] - me_ref[2]
    copy.wait()
    exponent = exponent_of(jnp.max(jnp.abs(prev[...]), axis=1, keepdims=True))
    for j in range(owned // w):
        lanes = to_lanes(exponent[j * w : (j + 1) * w])
        head[known + j : known + j + 1, :] = lanes.astype(i32)
    copies = []
    for m in range(h):
        held[m][0:owned, :] = encode(prev[:, chunk(q ^ m, w)], exponent)
        held[m][owned:, :] = head[...].astype(i16)
        copies.append(start(held[m], outs[m], sems.at[m]))
    wait_all(copies)


def prepare_kernel(per, me_ref, *refs):
    arrived, (member_ref, place_ref, near_ref, far_ref, count, heads, sems) = refs[:-7], refs[-7:]
    h = len(arrived)
    rows = near_ref.shape[0]
    blocks = place_ref.shape[0] // h
    copies = start_all([a.at[blocks * BLOCK :, :] for a in arrived], [heads.at[m] for m in range(h)], sems)
    count[...] = jnp.zeros_like(count)
    centroid = lax.broadcasted_iota(i32, (BLOCK, BLOCK), 0)
    ones = jnp.ones((BLOCK, BLOCK), bf16)
    for m in range(h):
        copies[m].wait()
        head = heads[m].astype(f32)
        for i in range(blocks):
            number = jnp.max(head[blocks + i : blocks + i + 1, :]).astype(i32)
            place = number ^ (me_ref[0] * per)
            place_ref[m * blocks + i] = place
            member = jnp.where(centroid == head[i : i + 1, :].astype(i32), 1.0, 0.0).astype(bf16)
            at = (m * blocks + i) * BLOCK
            member_ref[at : at + BLOCK, :] = member
            count[chunk(place, BLOCK), :] += dot(member, ones)
    near_ref[...] = count[0:rows, :]
    for j in range(rows // BLOCK):
        far = count[rows + j * BLOCK : rows + (j + 1) * BLOCK, 0:1]
        high = jnp.floor(far / 64.0)
        far_ref[j : j + 1, :] = (to_lanes(high) * 64.0 + to_lanes(far - high * 64.0)).astype(i32)


def sums_kernel(place_ref, before_ref, member_ref, far_count_ref, *refs):
    h = (len(refs) - 6) // 2
    points, (near_ref, code, after_ref, acc_ref, head, sem), held = refs[:h], refs[h : h + 6], refs[h + 6 :]
    after_ref[0] = before_ref[0]
    rows = acc_ref.shape[0] // 2
    blocks = held[0].shape[0] // BLOCK
    copies = start_all([p.at[0 : blocks * BLOCK, :] for p in points], held, sem)
    acc_ref[...] = jnp.zeros_like(acc_ref)
    for m in range(h):
        copies[m].wait()
        for i in range(blocks):
            at, here = (m * blocks + i) * BLOCK, slice(i * BLOCK, (i + 1) * BLOCK)
            acc_ref[chunk(place_ref[m * blocks + i], BLOCK), :] += dot(member_ref[at : at + BLOCK, :], held[m][here, :])
    lines = rows // BLOCK
    step = 2 * BLOCK
    for j in range(rows // step):
        at = slice(j * step, (j + 1) * step)
        value = acc_ref[rows + j * step : rows + (j + 1) * step, :]
        exponent = exponent_of(jnp.max(jnp.abs(value), axis=1, keepdims=True))
        code[at, :] = encode(value, exponent)
        lanes = to_lanes(exponent).astype(i32)
        for k in range(step // BLOCK):
            row = j * (step // BLOCK) + k
            head[row : row + 1, :] = lanes[:, k * BLOCK : (k + 1) * BLOCK]
    head[lines:, :] = far_count_ref[...]
    near_ref[...] = acc_ref[0:rows, :]
    code[rows:, :] = head[...].astype(i16)


def spot(index, w):
    return slice(index * BLOCK // w, index * BLOCK // w + 1), slice(index * BLOCK % w, index * BLOCK % w + BLOCK)


def refresh_kernel(chunks, h, near_ref, *refs):
    accs, crossed, prevs, x_ref, outs, tail = (
        refs[:chunks],
        refs[chunks : 2 * chunks],
        refs[2 * chunks : -h - 2],
        refs[-h - 2],
        refs[-h - 1 : -1],
        refs[-1],
    )
    rows, w = x_ref.shape
    owned = rows // h
    per = owned // BLOCK
    prev_heads = [prev[owned:, :].astype(i32).astype(f32) for prev in prevs]
    lines = rows // BLOCK
    heads = [crossed[c][rows:, :].astype(i32).astype(f32) for c in range(chunks)]
    unit = jnp.ones((8, BLOCK), bf16)
    for j in range(lines):
        at = slice(j * BLOCK, (j + 1) * BLOCK)
        count = near_ref[at, :] + to_column(heads[0][lines + j : lines + j + 1, :])
        inverse = 1.0 / jnp.maximum(count, 1.0)
        square, top = None, None
        owner, here = j // per, slice(j % per * BLOCK, (j % per + 1) * BLOCK)
        prev_exponent = to_column(prev_heads[owner][spot(per + j % per, w)])
        for c in range(chunks):
            lanes = slice(c * BLOCK, (c + 1) * BLOCK)
            far = decode(crossed[c][at, :], to_column(heads[c][j : j + 1, :]))
            x = (accs[c][at, :] + far) * inverse + decode(prevs[owner][here, lanes], prev_exponent)
            x_ref[at, lanes] = x
            square = x * x if c == 0 else square + x * x
            top = jnp.abs(x) if c == 0 else jnp.maximum(top, jnp.abs(x))
        square_high, square_low = split(square)
        sums = (dot_lanes(unit, square_high) + dot_lanes(unit, square_low))[0:1]
        sums_exponent = exponent_of(sums)
        scaled = sums * (16384.0 * jnp.exp2(-sums_exponent))
        whole = jnp.floor(scaled)
        exponent = exponent_of(jnp.max(top, axis=1, keepdims=True))
        for k, value in enumerate((sums_exponent, whole, jnp.floor((scaled - whole) * 16384.0), to_lanes(exponent))):
            tail[spot(k * lines + j, w)] = value.astype(i32)
        outs[owner][here, :] = encode(x_ref[at, :], exponent)
    for out in outs:
        out[owned:, :] = tail[...].astype(i16)


def put_codes(values, code, head):
    rows, w = values.shape
    size = min(rows, w)
    head[...] = jnp.zeros_like(head)
    for j in range(rows // size):
        at = slice(j * size, (j + 1) * size)
        exponent = exponent_of(jnp.max(jnp.abs(values[at, :]), axis=1, keepdims=True))
        code[at, :] = encode(values[at, :], exponent)
        head[j : j + 1, 0:size] = to_lanes(exponent).astype(i32)
    code[rows:, :] = head[...].astype(i16)


def get_codes(code, j, rows, size):
    w = code.shape[1]
    row, lane = j * size // min(rows, w), j * size % min(rows, w)
    lanes = code[rows : rows + 16, :].astype(i32).astype(f32)[row : row + 1, lane : lane + size]
    return decode(code[j * size : (j + 1) * size, :], to_column(lanes))


def upper_kernel(width, h, x_ref, *refs):
    backs, prevs, outs, (high, low, sums, member), heads = refs[:h], refs[h:-8], refs[-8:-6], refs[-6:-2], refs[-2:]
    total, w = x_ref.shape
    owned = total // h
    lines, per = total // BLOCK, owned // BLOCK
    tails = [back[owned:, :].astype(i32).astype(f32) for back in backs]
    for p in range(h):
        for j in range(per):
            squares = None
            for m in range(h):
                index = (p ^ m) * per + j
                exponent, whole, rest = (tails[m][spot(k * lines + index, w)] for k in range(3))
                value = (whole + rest * (1.0 / 16384.0)) * (jnp.exp2(exponent) * (1.0 / 16384.0))
                squares = value if m == 0 else squares + value
            factor = lax.rsqrt(squares / width + EPSILON)
            at = slice(p * owned + j * BLOCK, p * owned + (j + 1) * BLOCK)
            high[at, :], low[at, :] = split(x_ref[at, :] * to_column(factor))
    rows = sums.shape[0]
    parent_at = lax.broadcasted_iota(i32, (rows, BLOCK), 0)
    parents = [prev[owned:, :].astype(i32) for prev in prevs]
    for k in range(2):
        for j in range(lines):
            row = parents[j // per][spot(j % per, w)] - k * rows
            member[:, j * BLOCK : (j + 1) * BLOCK] = jnp.where(parent_at == row, 1.0, 0.0).astype(bf16)
        sums[...] = dot(member[...], high[...]) + dot(member[...], low[...])
        put_codes(sums, outs[k], heads[k])


def both_kernel(own, far, code_ref, sums, head):
    rows = sums.shape[0]
    for j in range(rows // BLOCK):
        sums[j * BLOCK : (j + 1) * BLOCK, :] = get_codes(own, j, rows, BLOCK) + get_codes(far, j, rows, BLOCK)
    put_codes(sums, code_ref, head)


def join_kernel(me_ref, *refs):
    parts, (out_ref, out, out_sems) = refs[:-3], refs[-3:]
    h = len(parts) // 2
    q = me_ref[0] & (h - 1)
    total, width = out.shape
    rows = total // 2
    w = width // h
    copies = []
    for j in range(total // BLOCK):
        at, k = slice(j * BLOCK, (j + 1) * BLOCK), j * BLOCK // rows
        values = [get_codes(parts[k * h + m], j - k * (rows // BLOCK), rows, BLOCK) for m in range(h)]
        square = sum(v * v for v in values)
        factor = lax.rsqrt(jnp.sum(square, axis=1, keepdims=True) / width + EPSILON)
        for m in range(h):
            out[at, chunk(q ^ m, w)] = values[m] * factor
        copies.append(start(out.at[at, :], out_ref.at[at, :], out_sems.at[j]))
    wait_all(copies)


def decode_kernel(me_ref, *refs):
    codes, out_ref = refs[:-1], refs[-1]
    h = len(codes)
    q = me_ref[0] & (h - 1)
    rows, width = out_ref.shape
    w = width // h
    lines, per = h * rows // BLOCK, rows // BLOCK
    tails = [code[rows:, :].astype(i32).astype(f32) for code in codes]
    for j in range(per):
        at = slice(j * BLOCK, (j + 1) * BLOCK)
        values = []
        for m in range(h):
            exponent = tails[m][spot(3 * lines + m * per + j, w)]
            values.append(decode(codes[m][at, :], to_column(exponent)))
        square = sum(v * v for v in values)
        factor = lax.rsqrt(jnp.sum(square, axis=1, keepdims=True) / width + EPSILON)
        for m in range(h):
            out_ref[at, chunk(q ^ m, w)] = values[m] * factor


def call(kernel, out_shape, **kw):
    params = pltpu.CompilerParams(vmem_limit_bytes=VMEM_LIMIT)
    return pl.pallas_call(kernel, out_shape=out_shape, compiler_params=params, **kw)


def dma(*dims):
    return pltpu.SemaphoreType.DMA(dims) if dims else pltpu.SemaphoreType.DMA


def shards(points, point_cluster, cand_blocks, cent1_prev, parent, cent2_prev):
    point_rows, width = points.shape
    blocks = point_rows // BLOCK
    owned = cent1_prev.shape[0]
    upper_rows = cent2_prev.shape[0]
    n = lax.axis_size("cent")
    h = n // 2
    dp = lax.axis_index("dp")
    w = width // h
    chunks = w // BLOCK
    rows = h * owned
    me = jnp.stack([lax.axis_index("cent").astype(i32), dp * (n * owned), dp * upper_rows])

    def swap(value, mask):
        return lax.ppermute(value, "cent", [(i, i ^ mask) for i in range(n)])

    def swap_half(values):
        arrived = {m: swap(values[m], m) for m in range(h - 1, 0, -1)}
        return [values[0]] + [arrived[m] for m in range(1, h)]

    table_rows = lax.all_gather(cent2_prev, "dp", axis=0, tiled=True)

    first_shape = shape((point_rows + 2 * blocks, BLOCK), bf16)
    *packed, after_pack = call(
        functools.partial(pack_kernel, chunks),
        ([first_shape] + [shape((point_rows, BLOCK), bf16)] * (chunks - 1)) * h + [shape((1,), i32)],
        in_specs=[SMEM, HBM, VMEM],
        out_specs=[HBM] * (h * chunks) + [SMEM],
        scratch_shapes=[pltpu.VMEM((2 * blocks, BLOCK), bf16), dma(h * chunks), dma(h)],
        name="pack",
    )(me, points, point_cluster.reshape(blocks, BLOCK))
    arrived = [swap_half(packed[c::chunks]) for c in range(chunks)]

    member, place, near, far_count = call(
        functools.partial(prepare_kernel, owned // BLOCK),
        [
            shape((h * point_rows, BLOCK), bf16),
            shape((h * blocks,), i32),
            shape((rows, BLOCK), f32),
            shape((rows // BLOCK, BLOCK), i32),
        ],
        in_specs=[SMEM] + [HBM] * h,
        out_specs=[VMEM, SMEM] + [VMEM] * 2,
        scratch_shapes=[pltpu.VMEM((2 * rows, BLOCK), f32), pltpu.VMEM((h, 2 * blocks, BLOCK), bf16), dma(h)],
        name="prepare",
    )(me, *arrived[0])

    lines = rows + 2 * rows // BLOCK
    accs, crossed, after = [], [], place
    for c in range(chunks):
        acc, code, ended = call(
            sums_kernel,
            [shape((rows, BLOCK), f32), shape((lines, BLOCK), i16), shape((1,), i32)],
            in_specs=[SMEM, SMEM, VMEM, VMEM] + [HBM] * h,
            out_specs=[VMEM, VMEM, SMEM],
            scratch_shapes=[pltpu.VMEM((2 * rows, BLOCK), f32), pltpu.VMEM((2 * rows // BLOCK, BLOCK), i32), dma(h)]
            + [pltpu.VMEM((point_rows, BLOCK), bf16)] * h,
            name=f"sums{c}",
        )(place, after, member, far_count, *arrived[c])
        accs.append(acc)
        crossed.append(swap(code, h))
        after = ended

    head = head_rows(2 * owned, w)
    prevs = call(
        prev_kernel,
        [shape((owned + head, w), i16)] * h,
        in_specs=[SMEM, SMEM, HBM, VMEM],
        out_specs=[HBM] * h,
        scratch_shapes=[pltpu.VMEM((owned, width), f32), pltpu.VMEM((head, w), i32), dma(), dma(h)]
        + [pltpu.VMEM((owned + head, w), i16)] * h,
        name="prev",
    )(me, after_pack, cent1_prev, parent.reshape(owned // w, w))
    prevs, crossed[0] = lax.optimization_barrier((prevs, crossed[0]))
    prevs = swap_half(prevs)

    points, table_rows = lax.optimization_barrier((points, table_rows))
    unit_points = rms_norm(points.astype(f32)).astype(bf16)
    table_scale = lax.rsqrt(jnp.mean(jnp.square(table_rows.astype(f32)), axis=-1) + EPSILON)
    table_scale, near = lax.optimization_barrier((table_scale, near))
    table_units = (table_rows.astype(f32) * table_scale[:, None]).astype(bf16)
    products = lax.dot_general(
        unit_points, table_units, (((1,), (1,)), ((), ())), preferred_element_type=f32
    )
    column_block = jnp.arange(table_rows.shape[0]) // BLOCK
    listed = jnp.any(cand_blocks[:, :, None] == column_block[None, None, :], axis=1)
    weights = jnp.exp(products * (SHARPNESS / width)).reshape(blocks, BLOCK, -1)
    running = jnp.sum(weights * listed[:, None, :].astype(f32), axis=2).reshape(point_rows)
    point_score = jnp.log(running)

    tail = 4 * rows // w
    x, *backs = call(
        functools.partial(refresh_kernel, chunks, h),
        [shape((rows, w), f32)] + [shape((owned + tail, w), i16)] * h,
        in_specs=[VMEM] * (1 + 2 * chunks + h),
        out_specs=[VMEM] * (h + 1),
        scratch_shapes=[pltpu.VMEM((tail, w), i32)],
        name="refresh",
    )(near, *accs, *crossed, *prevs)
    backs = swap_half(backs)

    part = upper_rows // 2
    tail = head_rows(part, w)
    code_shape = shape((part + tail, w), i16)
    held_head = pltpu.VMEM((tail, w), i32)
    codes = call(
        functools.partial(upper_kernel, width, h),
        [code_shape] * 2,
        in_specs=[VMEM] * (2 * h + 1),
        out_specs=[VMEM] * 2,
        scratch_shapes=[pltpu.VMEM((rows, w), bf16), pltpu.VMEM((rows, w), bf16), pltpu.VMEM((part, w), f32)]
        + [pltpu.VMEM((part, rows), bf16)]
        + [held_head] * 2,
        name="upper",
    )(x, *backs, *prevs)
    far_codes = [swap(code, h) for code in codes]
    parts = []
    for k in range(2):
        code = codes[k]
        if k == 0:
            code, point_score = lax.optimization_barrier((code, point_score))
        code = call(
            both_kernel,
            code_shape,
            in_specs=[VMEM, VMEM],
            out_specs=VMEM,
            scratch_shapes=[pltpu.VMEM((part, w), f32), held_head],
            name=f"both{k}",
        )(code, far_codes[k])
        parts += swap_half([code] * h)

    cent1_new = call(
        decode_kernel,
        shape((owned, width), f32),
        in_specs=[SMEM] + [VMEM] * h,
        out_specs=VMEM,
        name="decode",
    )(me, *backs)
    last, cent1_new = lax.optimization_barrier((me, cent1_new))
    cent2_new = call(
        join_kernel,
        shape((upper_rows, width), f32),
        in_specs=[SMEM] + [VMEM] * (2 * h),
        out_specs=HBM,
        scratch_shapes=[pltpu.VMEM((upper_rows, width), f32), dma(upper_rows // BLOCK)],
        name="join",
    )(last, *parts)
    return (cent1_new, cent2_new, point_score)


def solution(mesh):
    placed = (
        P(("dp", "cent"), None),
        P(("dp", "cent")),
        P(("dp", "cent"), None),
        P(("dp", "cent"), None),
        P(("dp", "cent")),
        P("dp", None),
    )
    return jax.shard_map(
        shards,
        mesh=mesh,
        in_specs=placed,
        out_specs=(P(("dp", "cent"), None), P("dp", None), P(("dp", "cent"))),
        check_vma=False,
    )
```

```python
import functools

import jax
import jax.numpy as jnp
from jax import lax
from jax.experimental import pallas as pl
from jax.experimental.pallas import tpu as pltpu
from jax.sharding import PartitionSpec as P

BLOCK = 128
EPSILON = 1e-06
SHARPNESS = 20.0
CODE = 32000.0
FLOOR = 1e-30
VMEM_LIMIT = 16 * 1024 * 1024
f32, bf16, i16, i32 = jnp.float32, jnp.bfloat16, jnp.int16, jnp.int32
shape = jax.ShapeDtypeStruct
VMEM = pl.BlockSpec(memory_space=pltpu.VMEM)
SMEM = pl.BlockSpec(memory_space=pltpu.SMEM)
HBM = pl.BlockSpec(memory_space=pltpu.HBM)


def rms_norm(values):
    return values * lax.rsqrt(jnp.mean(values * values, axis=-1, keepdims=True) + EPSILON)


def split(values):
    high = values.astype(bf16)
    return high, (values - high.astype(f32)).astype(bf16)


def dot(a, b):
    return jnp.dot(a, b, preferred_element_type=f32)


def dot_lanes(a, b):
    return lax.dot_general(a, b, (((1,), (1,)), ((), ())), preferred_element_type=f32)


def to_lanes(column):
    rows = column.shape[0]
    pick = jnp.where(lax.broadcasted_iota(i32, (8, BLOCK), 1) == 0, 1.0, 0.0).astype(bf16)
    return dot_lanes(pick, jnp.broadcast_to(column, (rows, BLOCK)).astype(bf16))[0:1]


def to_column(lanes):
    k = lanes.shape[1]
    eye = lax.broadcasted_iota(i32, (k, k), 0) == lax.broadcasted_iota(i32, (k, k), 1)
    return jnp.sum(jnp.where(eye, lanes, 0.0), axis=1, keepdims=True)


def exponent_of(top):
    return jnp.clip(jnp.ceil(jnp.log2(jnp.maximum(top * 1.001, FLOOR))), -100.0, 100.0)


def encode(values, exponent):
    return jnp.round(values * (CODE * jnp.exp2(-exponent))).astype(i16)


def decode(codes, exponent):
    return codes.astype(f32) * (jnp.exp2(exponent) * (1.0 / CODE))


def head_rows(count, w):
    return -(-count // (16 * w)) * 16


def chunk(index, size):
    return pl.ds(pl.multiple_of(index * size, size), size)


def start(source, target, sem):
    copy = pltpu.make_async_copy(source, target, sem)
    copy.start()
    return copy


def start_all(sources, targets, sems):
    return [start(a, b, sems.at[k]) for k, (a, b) in enumerate(zip(sources, targets))]


def wait_all(copies):
    for copy in copies:
        copy.wait()


def pack_kernel(chunks, me_ref, points_ref, cluster_ref, *refs):
    outs, (after_ref, head, sems, head_sems) = refs[:-4], refs[-4:]
    after_ref[0] = me_ref[0]
    rows = points_ref.shape[0]
    h = len(outs) // chunks
    q = me_ref[0] & (h - 1)
    sources = [points_ref.at[:, chunk((q ^ (k // chunks)) * chunks + k % chunks, BLOCK)] for k in range(len(outs))]
    copies = start_all(sources, [out.at[0:rows, :] for out in outs], sems)
    cluster = cluster_ref[...]
    head[...] = jnp.concatenate([cluster & (BLOCK - 1), (cluster - me_ref[1]) // BLOCK]).astype(f32).astype(bf16)
    copies += start_all([head] * h, [out.at[rows:, :] for out in outs[::chunks]], head_sems)
    wait_all(copies)


def prev_kernel(me_ref, after_ref, prev_ref, parent_ref, *refs):
    h = (len(refs) - 4) // 2
    outs, (prev, head, sem, sems), held = refs[:h], refs[h : h + 4], refs[h + 4 :]
    q = me_ref[0] & (h - 1)
    owned, width = prev.shape
    w = width // h
    copy = start(prev_ref, prev, sem)
    known = parent_ref.shape[0]
    head[...] = jnp.zeros_like(head)
    head[0:known, :] = parent_ref[...] - me_ref[2]
    copy.wait()
    exponent = exponent_of(jnp.max(jnp.abs(prev[...]), axis=1, keepdims=True))
    for j in range(owned // w):
        lanes = to_lanes(exponent[j * w : (j + 1) * w])
        head[known + j : known + j + 1, :] = lanes.astype(i32)
    copies = []
    for m in range(h):
        held[m][0:owned, :] = encode(prev[:, chunk(q ^ m, w)], exponent)
        held[m][owned:, :] = head[...].astype(i16)
        copies.append(start(held[m], outs[m], sems.at[m]))
    wait_all(copies)


def prepare_kernel(per, me_ref, *refs):
    arrived, (member_ref, place_ref, near_ref, far_ref, count, heads, sems) = refs[:-7], refs[-7:]
    h = len(arrived)
    rows = near_ref.shape[0]
    blocks = place_ref.shape[0] // h
    copies = start_all([a.at[blocks * BLOCK :, :] for a in arrived], [heads.at[m] for m in range(h)], sems)
    count[...] = jnp.zeros_like(count)
    centroid = lax.broadcasted_iota(i32, (BLOCK, BLOCK), 0)
    ones = jnp.ones((BLOCK, BLOCK), bf16)
    for m in range(h):
        copies[m].wait()
        head = heads[m].astype(f32)
        for i in range(blocks):
            number = jnp.max(head[blocks + i : blocks + i + 1, :]).astype(i32)
            place = number ^ (me_ref[0] * per)
            place_ref[m * blocks + i] = place
            member = jnp.where(centroid == head[i : i + 1, :].astype(i32), 1.0, 0.0).astype(bf16)
            at = (m * blocks + i) * BLOCK
            member_ref[at : at + BLOCK, :] = member
            count[chunk(place, BLOCK), :] += dot(member, ones)
    near_ref[...] = count[0:rows, :]
    for j in range(rows // BLOCK):
        far = count[rows + j * BLOCK : rows + (j + 1) * BLOCK, 0:1]
        high = jnp.floor(far / 64.0)
        far_ref[j : j + 1, :] = (to_lanes(high) * 64.0 + to_lanes(far - high * 64.0)).astype(i32)


def sums_kernel(place_ref, before_ref, member_ref, far_count_ref, *refs):
    h = (len(refs) - 6) // 2
    points, (near_ref, code, after_ref, acc_ref, head, sem), held = refs[:h], refs[h : h + 6], refs[h + 6 :]
    after_ref[0] = before_ref[0]
    rows = acc_ref.shape[0] // 2
    blocks = held[0].shape[0] // BLOCK
    copies = start_all([p.at[0 : blocks * BLOCK, :] for p in points], held, sem)
    acc_ref[...] = jnp.zeros_like(acc_ref)
    for m in range(h):
        copies[m].wait()
        for i in range(blocks):
            at, here = (m * blocks + i) * BLOCK, slice(i * BLOCK, (i + 1) * BLOCK)
            acc_ref[chunk(place_ref[m * blocks + i], BLOCK), :] += dot(member_ref[at : at + BLOCK, :], held[m][here, :])
    lines = rows // BLOCK
    step = 2 * BLOCK
    for j in range(rows // step):
        at = slice(j * step, (j + 1) * step)
        value = acc_ref[rows + j * step : rows + (j + 1) * step, :]
        exponent = exponent_of(jnp.max(jnp.abs(value), axis=1, keepdims=True))
        code[at, :] = encode(value, exponent)
        lanes = to_lanes(exponent).astype(i32)
        for k in range(step // BLOCK):
            row = j * (step // BLOCK) + k
            head[row : row + 1, :] = lanes[:, k * BLOCK : (k + 1) * BLOCK]
    head[lines:, :] = far_count_ref[...]
    near_ref[...] = acc_ref[0:rows, :]
    code[rows:, :] = head[...].astype(i16)


def spot(index, w):
    return slice(index * BLOCK // w, index * BLOCK // w + 1), slice(index * BLOCK % w, index * BLOCK % w + BLOCK)


def refresh_kernel(chunks, h, near_ref, *refs):
    accs, crossed, prevs, x_ref, outs, tail = (
        refs[:chunks],
        refs[chunks : 2 * chunks],
        refs[2 * chunks : -h - 2],
        refs[-h - 2],
        refs[-h - 1 : -1],
        refs[-1],
    )
    rows, w = x_ref.shape
    owned = rows // h
    per = owned // BLOCK
    prev_heads = [prev[owned:, :].astype(i32).astype(f32) for prev in prevs]
    lines = rows // BLOCK
    heads = [crossed[c][rows:, :].astype(i32).astype(f32) for c in range(chunks)]
    unit = jnp.ones((8, BLOCK), bf16)
    for j in range(lines):
        at = slice(j * BLOCK, (j + 1) * BLOCK)
        count = near_ref[at, :] + to_column(heads[0][lines + j : lines + j + 1, :])
        inverse = 1.0 / jnp.maximum(count, 1.0)
        square, top = None, None
        owner, here = j // per, slice(j % per * BLOCK, (j % per + 1) * BLOCK)
        prev_exponent = to_column(prev_heads[owner][spot(per + j % per, w)])
        for c in range(chunks):
            lanes = slice(c * BLOCK, (c + 1) * BLOCK)
            far = decode(crossed[c][at, :], to_column(heads[c][j : j + 1, :]))
            x = (accs[c][at, :] + far) * inverse + decode(prevs[owner][here, lanes], prev_exponent)
            x_ref[at, lanes] = x
            square = x * x if c == 0 else square + x * x
            top = jnp.abs(x) if c == 0 else jnp.maximum(top, jnp.abs(x))
        square_high, square_low = split(square)
        sums = (dot_lanes(unit, square_high) + dot_lanes(unit, square_low))[0:1]
        sums_exponent = exponent_of(sums)
        scaled = sums * (16384.0 * jnp.exp2(-sums_exponent))
        whole = jnp.floor(scaled)
        exponent = exponent_of(jnp.max(top, axis=1, keepdims=True))
        for k, value in enumerate((sums_exponent, whole, jnp.floor((scaled - whole) * 16384.0), to_lanes(exponent))):
            tail[spot(k * lines + j, w)] = value.astype(i32)
        outs[owner][here, :] = encode(x_ref[at, :], exponent)
    for out in outs:
        out[owned:, :] = tail[...].astype(i16)


def put_codes(values, code, head):
    rows, w = values.shape
    size = min(rows, w)
    head[...] = jnp.zeros_like(head)
    for j in range(rows // size):
        at = slice(j * size, (j + 1) * size)
        exponent = exponent_of(jnp.max(jnp.abs(values[at, :]), axis=1, keepdims=True))
        code[at, :] = encode(values[at, :], exponent)
        head[j : j + 1, 0:size] = to_lanes(exponent).astype(i32)
    code[rows:, :] = head[...].astype(i16)


def get_codes(code, j, rows, size):
    w = code.shape[1]
    row, lane = j * size // min(rows, w), j * size % min(rows, w)
    lanes = code[rows : rows + 16, :].astype(i32).astype(f32)[row : row + 1, lane : lane + size]
    return decode(code[j * size : (j + 1) * size, :], to_column(lanes))


def upper_kernel(width, h, x_ref, *refs):
    backs, prevs, outs, (high, low, sums, member), heads = refs[:h], refs[h:-8], refs[-8:-6], refs[-6:-2], refs[-2:]
    total, w = x_ref.shape
    owned = total // h
    lines, per = total // BLOCK, owned // BLOCK
    tails = [back[owned:, :].astype(i32).astype(f32) for back in backs]
    for p in range(h):
        for j in range(per):
            squares = None
            for m in range(h):
                index = (p ^ m) * per + j
                exponent, whole, rest = (tails[m][spot(k * lines + index, w)] for k in range(3))
                value = (whole + rest * (1.0 / 16384.0)) * (jnp.exp2(exponent) * (1.0 / 16384.0))
                squares = value if m == 0 else squares + value
            factor = lax.rsqrt(squares / width + EPSILON)
            at = slice(p * owned + j * BLOCK, p * owned + (j + 1) * BLOCK)
            high[at, :], low[at, :] = split(x_ref[at, :] * to_column(factor))
    rows = sums.shape[0]
    parent_at = lax.broadcasted_iota(i32, (rows, BLOCK), 0)
    parents = [prev[owned:, :].astype(i32) for prev in prevs]
    for k in range(2):
        for j in range(lines):
            row = parents[j // per][spot(j % per, w)] - k * rows
            member[:, j * BLOCK : (j + 1) * BLOCK] = jnp.where(parent_at == row, 1.0, 0.0).astype(bf16)
        sums[...] = dot(member[...], high[...]) + dot(member[...], low[...])
        put_codes(sums, outs[k], heads[k])


def both_kernel(own, far, code_ref, sums, head):
    rows = sums.shape[0]
    for j in range(rows // BLOCK):
        sums[j * BLOCK : (j + 1) * BLOCK, :] = get_codes(own, j, rows, BLOCK) + get_codes(far, j, rows, BLOCK)
    put_codes(sums, code_ref, head)


def join_kernel(me_ref, *refs):
    parts, (out_ref, out, out_sems) = refs[:-3], refs[-3:]
    h = len(parts) // 2
    q = me_ref[0] & (h - 1)
    total, width = out.shape
    rows = total // 2
    w = width // h
    copies = []
    for j in range(total // BLOCK):
        at, k = slice(j * BLOCK, (j + 1) * BLOCK), j * BLOCK // rows
        values = [get_codes(parts[k * h + m], j - k * (rows // BLOCK), rows, BLOCK) for m in range(h)]
        square = sum(v * v for v in values)
        factor = lax.rsqrt(jnp.sum(square, axis=1, keepdims=True) / width + EPSILON)
        for m in range(h):
            out[at, chunk(q ^ m, w)] = values[m] * factor
        copies.append(start(out.at[at, :], out_ref.at[at, :], out_sems.at[j]))
    wait_all(copies)


def decode_kernel(me_ref, *refs):
    codes, out_ref = refs[:-1], refs[-1]
    h = len(codes)
    q = me_ref[0] & (h - 1)
    rows, width = out_ref.shape
    w = width // h
    lines, per = h * rows // BLOCK, rows // BLOCK
    tails = [code[rows:, :].astype(i32).astype(f32) for code in codes]
    for j in range(per):
        at = slice(j * BLOCK, (j + 1) * BLOCK)
        values = []
        for m in range(h):
            exponent = tails[m][spot(3 * lines + m * per + j, w)]
            values.append(decode(codes[m][at, :], to_column(exponent)))
        square = sum(v * v for v in values)
        factor = lax.rsqrt(jnp.sum(square, axis=1, keepdims=True) / width + EPSILON)
        for m in range(h):
            out_ref[at, chunk(q ^ m, w)] = values[m] * factor


def call(kernel, out_shape, **kw):
    params = pltpu.CompilerParams(vmem_limit_bytes=VMEM_LIMIT)
    return pl.pallas_call(kernel, out_shape=out_shape, compiler_params=params, **kw)


def dma(*dims):
    return pltpu.SemaphoreType.DMA(dims) if dims else pltpu.SemaphoreType.DMA


def shards(points, point_cluster, cand_blocks, cent1_prev, parent, cent2_prev):
    point_rows, width = points.shape
    blocks = point_rows // BLOCK
    owned = cent1_prev.shape[0]
    upper_rows = cent2_prev.shape[0]
    n = lax.axis_size("cent")
    h = n // 2
    dp = lax.axis_index("dp")
    w = width // h
    chunks = w // BLOCK
    rows = h * owned
    me = jnp.stack([lax.axis_index("cent").astype(i32), dp * (n * owned), dp * upper_rows])

    def swap(value, mask):
        return lax.ppermute(value, "cent", [(i, i ^ mask) for i in range(n)])

    def swap_half(values):
        arrived = {m: swap(values[m], m) for m in range(h - 1, 0, -1)}
        return [values[0]] + [arrived[m] for m in range(1, h)]

    table_rows = lax.all_gather(cent2_prev, "dp", axis=0, tiled=True)

    first_shape = shape((point_rows + 2 * blocks, BLOCK), bf16)
    *packed, after_pack = call(
        functools.partial(pack_kernel, chunks),
        ([first_shape] + [shape((point_rows, BLOCK), bf16)] * (chunks - 1)) * h + [shape((1,), i32)],
        in_specs=[SMEM, HBM, VMEM],
        out_specs=[HBM] * (h * chunks) + [SMEM],
        scratch_shapes=[pltpu.VMEM((2 * blocks, BLOCK), bf16), dma(h * chunks), dma(h)],
        name="pack",
    )(me, points, point_cluster.reshape(blocks, BLOCK))
    arrived = [swap_half(packed[c::chunks]) for c in range(chunks)]

    member, place, near, far_count = call(
        functools.partial(prepare_kernel, owned // BLOCK),
        [
            shape((h * point_rows, BLOCK), bf16),
            shape((h * blocks,), i32),
            shape((rows, BLOCK), f32),
            shape((rows // BLOCK, BLOCK), i32),
        ],
        in_specs=[SMEM] + [HBM] * h,
        out_specs=[VMEM, SMEM] + [VMEM] * 2,
        scratch_shapes=[pltpu.VMEM((2 * rows, BLOCK), f32), pltpu.VMEM((h, 2 * blocks, BLOCK), bf16), dma(h)],
        name="prepare",
    )(me, *arrived[0])

    lines = rows + 2 * rows // BLOCK
    accs, crossed, after = [], [], place
    for c in range(chunks):
        acc, code, ended = call(
            sums_kernel,
            [shape((rows, BLOCK), f32), shape((lines, BLOCK), i16), shape((1,), i32)],
            in_specs=[SMEM, SMEM, VMEM, VMEM] + [HBM] * h,
            out_specs=[VMEM, VMEM, SMEM],
            scratch_shapes=[pltpu.VMEM((2 * rows, BLOCK), f32), pltpu.VMEM((2 * rows // BLOCK, BLOCK), i32), dma(h)]
            + [pltpu.VMEM((point_rows, BLOCK), bf16)] * h,
            name=f"sums{c}",
        )(place, after, member, far_count, *arrived[c])
        accs.append(acc)
        crossed.append(swap(code, h))
        after = ended

    head = head_rows(2 * owned, w)
    prevs = call(
        prev_kernel,
        [shape((owned + head, w), i16)] * h,
        in_specs=[SMEM, SMEM, HBM, VMEM],
        out_specs=[HBM] * h,
        scratch_shapes=[pltpu.VMEM((owned, width), f32), pltpu.VMEM((head, w), i32), dma(), dma(h)]
        + [pltpu.VMEM((owned + head, w), i16)] * h,
        name="prev",
    )(me, after_pack, cent1_prev, parent.reshape(owned // w, w))
    prevs, crossed[0] = lax.optimization_barrier((prevs, crossed[0]))
    prevs = swap_half(prevs)

    points, table_rows = lax.optimization_barrier((points, table_rows))
    unit_points = rms_norm(points.astype(f32)).astype(bf16)
    table_scale = lax.rsqrt(jnp.mean(jnp.square(table_rows.astype(f32)), axis=-1) + EPSILON)
    table_scale, near = lax.optimization_barrier((table_scale, near))
    table_units = (table_rows.astype(f32) * table_scale[:, None]).astype(bf16)
    products = lax.dot_general(
        unit_points, table_units, (((1,), (1,)), ((), ())), preferred_element_type=f32
    )
    column_block = jnp.arange(table_rows.shape[0]) // BLOCK
    listed = jnp.any(cand_blocks[:, :, None] == column_block[None, None, :], axis=1)
    weights = jnp.exp(products * (SHARPNESS / width)).reshape(blocks, BLOCK, -1)
    running = jnp.sum(weights * listed[:, None, :].astype(f32), axis=2).reshape(point_rows)
    point_score = jnp.log(running)

    tail = 4 * rows // w
    x, *backs = call(
        functools.partial(refresh_kernel, chunks, h),
        [shape((rows, w), f32)] + [shape((owned + tail, w), i16)] * h,
        in_specs=[VMEM] * (1 + 2 * chunks + h),
        out_specs=[VMEM] * (h + 1),
        scratch_shapes=[pltpu.VMEM((tail, w), i32)],
        name="refresh",
    )(near, *accs, *crossed, *prevs)
    backs = swap_half(backs)

    part = upper_rows // 2
    tail = head_rows(part, w)
    code_shape = shape((part + tail, w), i16)
    held_head = pltpu.VMEM((tail, w), i32)
    codes = call(
        functools.partial(upper_kernel, width, h),
        [code_shape] * 2,
        in_specs=[VMEM] * (2 * h + 1),
        out_specs=[VMEM] * 2,
        scratch_shapes=[pltpu.VMEM((rows, w), bf16), pltpu.VMEM((rows, w), bf16), pltpu.VMEM((part, w), f32)]
        + [pltpu.VMEM((part, rows), bf16)]
        + [held_head] * 2,
        name="upper",
    )(x, *backs, *prevs)
    far_codes = [swap(code, h) for code in codes]
    *codes, point_score = lax.optimization_barrier((*codes, point_score))
    parts = []
    for k in range(2):
        code = codes[k]
        code = call(
            both_kernel,
            code_shape,
            in_specs=[VMEM, VMEM],
            out_specs=VMEM,
            scratch_shapes=[pltpu.VMEM((part, w), f32), held_head],
            name=f"both{k}",
        )(code, far_codes[k])
        parts += swap_half([code] * h)

    cent1_new = call(
        decode_kernel,
        shape((owned, width), f32),
        in_specs=[SMEM] + [VMEM] * h,
        out_specs=VMEM,
        name="decode",
    )(me, *backs)
    last, cent1_new = lax.optimization_barrier((me, cent1_new))
    cent2_new = call(
        join_kernel,
        shape((upper_rows, width), f32),
        in_specs=[SMEM] + [VMEM] * (2 * h),
        out_specs=HBM,
        scratch_shapes=[pltpu.VMEM((upper_rows, width), f32), dma(upper_rows // BLOCK)],
        name="join",
    )(last, *parts)
    return (cent1_new, cent2_new, point_score)


def solution(mesh):
    placed = (
        P(("dp", "cent"), None),
        P(("dp", "cent")),
        P(("dp", "cent"), None),
        P(("dp", "cent"), None),
        P(("dp", "cent")),
        P("dp", None),
    )
    return jax.shard_map(
        shards,
        mesh=mesh,
        in_specs=placed,
        out_specs=(P(("dp", "cent"), None), P("dp", None), P(("dp", "cent"))),
        check_vma=False,
    )
```
